32 devices in a mesh: region: 2 (over core), patch: 16 (over z, y, x).
Axes of the slice: x: 2, y: 2, z: 4, core: 2. Of those that a mesh axis runs over, the one named last changes fastest.
Arguments:
- fine_input: bfloat16 [32, 64, 4096], P(('region', 'patch')), may hold values from -6 to 6
- fine_weight: bfloat16 [576, 64], replicated, may hold values from -0.25 to 0.25
- fine_bias: float32 [64], replicated, may hold values from -3 to 3
- cotangent: bfloat16 [32, 64, 4096], P(('region', 'patch')), may hold values from -6 to 6
- halo_index: int32 [32, 260], P('region'), may hold values from 0 to 8191, as said below
Outputs:
- input_grad: bfloat16 [32, 64, 4096], P(('region', 'patch'))
- weight_grad: float32 [576, 64], replicated
- bias_grad: float32 [64], replicated
The draws below stay inside these ranges and needn't reach their ends.
Inputs may be any that keep to these rules, and one draw needn't show every extreme that they name: `halo_index`: entries in the top and bottom halo rows outside their first and last cell name top- or bottom-row rim entries of patches in the same region. All other entries (the four corner cells and the left and right halo columns) name left- or right-column rim entries of the patch at the same owner index in the region just before or just after (regions form a closed loop).
All inputs are finite; a program needn't handle non-finite values.
Results may differ from the reference program's by a relative error of at most 0.0075.
Values may be sent and summed in bfloat16 or wider, within the bound.
No kernel may reach another device: no remote copies, remote signals or barrier semaphores. Data moves between devices by JAX's collectives and lax.ppermute only.
A program may use at most 64 MiB of HBM per device.

```python
import math
import jax
import jax.numpy as jnp
from jax import lax

CHANNELS = 64
SIDE = 64
REGIONS = 2
REGION_PATCHES = 16
PATCHES = 32
PIXELS = 131072


def draw_halo_index(key, part):
    order = jax.random.permutation(jax.random.fold_in(key, 11), REGION_PATCHES)
    place = jnp.argsort(order, stable=True)
    flips = jax.random.randint(jax.random.fold_in(key, 12), (REGIONS,), 0, 2)
    patch_ids = jnp.arange(PATCHES)
    region = patch_ids // REGION_PATCHES
    slot = patch_ids % REGION_PATCHES
    position = place[slot]
    last = REGION_PATCHES - 1
    north = jnp.where(position > 0, order[jnp.maximum(position - 1, 0)], slot)
    south = jnp.where(position < last, order[jnp.minimum(position + 1, last)], slot)
    north_row = jnp.where(position > 0, SIDE, 0)
    south_row = jnp.where(position < last, 0, SIDE)
    cells = jnp.arange(SIDE)
    rim_size = 4 * SIDE
    base = region * REGION_PATCHES
    top = ((base + north) * rim_size + north_row)[:, None] + cells[None, :]
    bottom = ((base + south) * rim_size + south_row)[:, None] + cells[None, :]
    west_region = (region - 1) % REGIONS
    east_region = (region + 1) % REGIONS
    west_rows = jnp.where(flips[west_region][:, None] == 1, SIDE - 1 - cells[None, :], cells[None, :])
    east_rows = jnp.where(flips[region][:, None] == 1, SIDE - 1 - cells[None, :], cells[None, :])
    west = ((west_region * REGION_PATCHES + slot) * rim_size + 3 * SIDE)[:, None] + west_rows
    east = ((east_region * REGION_PATCHES + slot) * rim_size + 2 * SIDE)[:, None] + east_rows
    result = jnp.concatenate([west[:, :1], top, east[:, :1], west[:, -1:], bottom, east[:, -1:], west, east], axis=1)
    return result.astype(jnp.int32)


def levels(rng, shape, shards, least, largest):
    def one(dim, shards_of):
        heights = jax.random.uniform(jax.random.fold_in(jax.random.fold_in(rng, 6), dim), (shards_of,), jnp.float32, least / len(shards), largest / len(shards))
        return jnp.repeat(jnp.exp(heights), shape[dim] // shards_of).reshape((-1,) + (1,) * (len(shape) - dim - 1))

    factor_of = one(*shards[0])
    for cut in shards[1:]:
        factor_of = factor_of * one(*cut)
    return factor_of


def noise(rng, dims, deviation, most, pieces=(), kind=jnp.bfloat16):
    values = deviation * jax.random.normal(rng, dims, jnp.float32)
    if pieces:
        values = values * levels(rng, dims, pieces, -0.22, 0.18)
    return jnp.clip(values, -most, most).astype(kind)


def setup_inputs(seed: int = 0) -> dict:
    arg_keys = jax.random.split(jax.random.key(seed), 6)
    fine_input = noise(arg_keys[0], (PATCHES, SIDE, SIDE * CHANNELS), 1.0, 6.0, ((0, 32),))
    fine_weight = noise(arg_keys[1], (9 * CHANNELS, CHANNELS), (9 * CHANNELS) ** -0.5, 0.25)
    fine_bias = noise(arg_keys[2], (CHANNELS,), 0.5, 3.0, (), jnp.float32)
    cotangent = noise(arg_keys[3], (PATCHES, SIDE, SIDE * CHANNELS), 1.0, 6.0, ((0, 32),))
    halo_index = draw_halo_index(jax.random.fold_in(arg_keys[5], 71), 0)
    return {"fine_input": fine_input, "fine_weight": fine_weight, "fine_bias": fine_bias, "cotangent": cotangent, "halo_index": halo_index}


def build_padded(field, halo_cells):
    top = halo_cells[0:SIDE + 2]
    bottom = halo_cells[SIDE + 2:2 * SIDE + 4]
    left = halo_cells[2 * SIDE + 4:3 * SIDE + 4]
    right = halo_cells[3 * SIDE + 4:4 * SIDE + 4]
    middle = jnp.concatenate([left[:, None, :], field, right[:, None, :]], axis=1)
    return jnp.concatenate([top[None], middle, bottom[None]], axis=0)

def signal_gradient(padded, upstream, weight, bias):
    signal = jnp.zeros((SIDE * SIDE, CHANNELS), jnp.float32) + bias[None, :]
    for row_step in range(3):
        for column_step in range(3):
            tap_index = 3 * row_step + column_step
            window = padded[row_step:row_step + SIDE, column_step:column_step + SIDE].reshape(SIDE * SIDE, CHANNELS)
            signal = signal + jnp.dot(window, weight[tap_index * CHANNELS:(tap_index + 1) * CHANNELS], preferred_element_type=jnp.float32)
    sigma = jax.nn.sigmoid(signal)
    slope = sigma * (1.0 + signal * (1.0 - sigma))
    return (upstream.reshape(SIDE * SIDE, CHANNELS).astype(jnp.float32) * slope).astype(jnp.bfloat16)

def padded_gradient(signal_grad, weight):
    running = jnp.zeros((SIDE + 2, SIDE + 2, CHANNELS), jnp.float32)
    for row_step in range(3):
        for column_step in range(3):
            tap_index = 3 * row_step + column_step
            term = lax.dot_general(signal_grad, weight[tap_index * CHANNELS:(tap_index + 1) * CHANNELS], (((1,), (1,)), ((), ())), preferred_element_type=jnp.float32)
            running = running.at[row_step:row_step + SIDE, column_step:column_step + SIDE].add(term.reshape(SIDE, SIDE, CHANNELS))
    return running

def weight_terms(padded, signal_grad):
    blocks = []
    for row_step in range(3):
        for column_step in range(3):
            window = padded[row_step:row_step + SIDE, column_step:column_step + SIDE].reshape(SIDE * SIDE, CHANNELS)
            blocks.append(lax.dot_general(window, signal_grad, (((0,), (0,)), ((), ())), preferred_element_type=jnp.float32))
    return (jnp.concatenate(blocks, axis=0), lax.optimization_barrier(jnp.sum(signal_grad.astype(jnp.float32), axis=0)))

def border_of(running):
    return jnp.concatenate([running[0], running[SIDE + 1], running[1:SIDE + 1, 0], running[1:SIDE + 1, SIDE + 1]], axis=0)

def add_rims(inner, rim_grads):
    inner = inner.at[0].add(rim_grads[0:SIDE])
    inner = inner.at[SIDE - 1].add(rim_grads[SIDE:2 * SIDE])
    inner = inner.at[:, 0].add(rim_grads[2 * SIDE:3 * SIDE])
    inner = inner.at[:, SIDE - 1].add(rim_grads[3 * SIDE:4 * SIDE])
    return inner

def reference(fine_input, fine_weight, fine_bias, cotangent, halo_index):
    fields = fine_input.reshape(PATCHES, SIDE, SIDE, CHANNELS)
    upstreams = cotangent.reshape(PATCHES, SIDE, SIDE, CHANNELS)
    rims = jnp.concatenate([fields[:, 0], fields[:, SIDE - 1], fields[:, :, 0], fields[:, :, SIDE - 1]], axis=1)
    rims = rims.reshape(PATCHES * 4 * SIDE, CHANNELS)
    halos = rims[halo_index]

    def first_pass(items):
        field, halo_cells, upstream = items
        padded = build_padded(field, halo_cells)
        signal_grad = signal_gradient(padded, upstream, fine_weight, fine_bias)
        running = padded_gradient(signal_grad, fine_weight)
        weight_part, bias_part = weight_terms(padded, signal_grad)
        return (border_of(running), weight_part, bias_part)
    borders, weight_parts, bias_parts = lax.map(first_pass, (fields, halos, upstreams))
    rim_grads = jax.ops.segment_sum(borders.reshape(-1, CHANNELS), halo_index.reshape(-1), num_segments=PATCHES * 4 * SIDE)
    rim_grads = rim_grads.reshape(PATCHES, 4 * SIDE, CHANNELS)

    def second_pass(items):
        field, halo_cells, upstream, rim_part = items
        padded = build_padded(field, halo_cells)
        signal_grad = signal_gradient(padded, upstream, fine_weight, fine_bias)
        running = padded_gradient(signal_grad, fine_weight)
        inner = add_rims(running[1:SIDE + 1, 1:SIDE + 1], rim_part)
        return inner.astype(jnp.bfloat16).reshape(SIDE, SIDE * CHANNELS)
    input_grad = lax.map(second_pass, (fields, halos, upstreams, rim_grads))
    scale = 1.0 / math.sqrt(PIXELS)
    weight_grad = lax.optimization_barrier(jnp.sum(weight_parts, axis=0)) * scale
    bias_grad = lax.optimization_barrier(jnp.sum(bias_parts, axis=0)) * scale
    return (input_grad, weight_grad, bias_grad)
```

```python
import math

import jax
import jax.numpy as jnp
from jax import lax
from jax.sharding import PartitionSpec as P

CHANNELS = 64
SIDE = 64


def swap(x, axis, k):
    n = lax.axis_size(axis)
    return lax.ppermute(x, axis, [(i, i ^ k) for i in range(n)])


def steps_of(n):
    ks = []
    k = n // 2
    while k:
        ks.append(k)
        k //= 2
    return ks


def slot_of(relative, ks):
    slot = jnp.zeros_like(relative)
    for bit, k in enumerate(ks):
        slot = slot + jnp.where((relative & k) != 0, 1 << bit, 0)
    return slot


def gathered(x, axis, ks):
    x = x[None]
    for k in ks:
        x = jnp.concatenate([x, swap(x, axis, k)], axis=0)
    return x


def from_neighbours(x, axis):
    count = lax.axis_size(axis)
    before = lax.ppermute(x, axis, [(i, (i + 1) % count) for i in range(count)])
    if count == 2:
        return before, before
    return before, lax.ppermute(x, axis, [((i + 1) % count, i) for i in range(count)])


def build_padded(field, halo_cells):
    top = halo_cells[0 : SIDE + 2]
    bottom = halo_cells[SIDE + 2 : 2 * SIDE + 4]
    left = halo_cells[2 * SIDE + 4 : 3 * SIDE + 4]
    right = halo_cells[3 * SIDE + 4 : 4 * SIDE + 4]
    middle = jnp.concatenate([left[:, None, :], field, right[:, None, :]], axis=1)
    return jnp.concatenate([top[None], middle, bottom[None]], axis=0)


def body(fine_input, fine_weight, fine_bias, cotangent, halo_index):
    owners = lax.axis_size("patch")
    regions = lax.axis_size("region")
    owner_id = lax.axis_index("patch")
    region_id = lax.axis_index("region")
    field = fine_input.reshape(SIDE, SIDE, CHANNELS)
    ks = steps_of(owners)
    row_rims = jnp.concatenate([field[0], field[SIDE - 1]], axis=0)
    column_rims = jnp.concatenate([field[:, 0], field[:, SIDE - 1]], axis=0)
    before, after = from_neighbours(column_rims, "region")
    rows = gathered(row_rims, "patch", ks).reshape(owners * 2 * SIDE, CHANNELS)
    table = jnp.concatenate([rows, before, after], axis=0)
    row_count = owners * 2 * SIDE
    source = halo_index // (4 * SIDE)
    within = halo_index % (4 * SIDE)
    own_source = lax.dynamic_index_in_dim(source, owner_id, 0, keepdims=False)
    own_within = lax.dynamic_index_in_dim(within, owner_id, 0, keepdims=False)
    relative = (own_source // owners - region_id) % regions
    column_slot = row_count + jnp.where(relative == 1, 2 * SIDE, 0) + own_within - 2 * SIDE
    row_slot = slot_of((own_source % owners) ^ owner_id, ks) * (2 * SIDE) + own_within
    local_ids = jnp.where(own_within < 2 * SIDE, row_slot, column_slot)
    padded = build_padded(field, table[local_ids])

    kernel = fine_weight.reshape(3, 3, CHANNELS, CHANNELS)
    dims = ("NHWC", "HWIO", "NHWC")
    signal = lax.conv_general_dilated(
        padded[None], kernel, (1, 1), "VALID", dimension_numbers=dims, preferred_element_type=jnp.float32
    )[0] + fine_bias
    sigma = jax.nn.sigmoid(signal)
    slope = sigma * (1.0 + signal * (1.0 - sigma))
    signal_grad = (cotangent.reshape(SIDE, SIDE, CHANNELS).astype(jnp.float32) * slope).astype(jnp.bfloat16)
    flipped = jnp.swapaxes(kernel[::-1, ::-1], 2, 3)
    running = lax.conv_general_dilated(
        signal_grad[None], flipped, (1, 1), [(2, 2), (2, 2)], dimension_numbers=dims,
        preferred_element_type=jnp.float32,
    )[0]
    blocks = []
    flat_grad = signal_grad.reshape(SIDE * SIDE, CHANNELS)
    for a in range(3):
        for b in range(3):
            window = padded[a : a + SIDE, b : b + SIDE].reshape(SIDE * SIDE, CHANNELS)
            blocks.append(
                lax.dot_general(window, flat_grad, (((0,), (0,)), ((), ())), preferred_element_type=jnp.float32)
            )
    bias_part = jnp.sum(flat_grad.astype(jnp.float32), axis=0)
    terms = jnp.concatenate(blocks + [bias_part[None]], axis=0)

    row_grads = jnp.concatenate([running[0, 1 : SIDE + 1], running[SIDE + 1, 1 : SIDE + 1]], axis=0)
    column_grads = jnp.concatenate(
        [
            running[0, :1], running[0, SIDE + 1 :], running[SIDE + 1, :1], running[SIDE + 1, SIDE + 1 :],
            running[1 : SIDE + 1, 0], running[1 : SIDE + 1, SIDE + 1],
        ],
        axis=0,
    )
    corners = jnp.array([0, SIDE + 1, SIDE + 2, 2 * SIDE + 3])
    own_column_ids = jnp.concatenate([own_within[corners], own_within[2 * SIDE + 4 :]])
    own_column_rel = jnp.concatenate([relative[corners], relative[2 * SIDE + 4 :]])
    side_slots = jnp.where(own_column_rel == 1, 2 * SIDE, 0) + own_column_ids - 2 * SIDE
    side_terms = jax.ops.segment_sum(column_grads, side_slots, num_segments=4 * SIDE).reshape(2, 2 * SIDE, CHANNELS)
    sent = side_terms.astype(jnp.bfloat16)
    if regions == 2:
        got = swap(sent, "region", 1)
        own_columns = got[0].astype(jnp.float32) + got[1].astype(jnp.float32)
    else:
        up = lax.ppermute(sent[1], "region", [(i, (i + 1) % regions) for i in range(regions)])
        down = lax.ppermute(sent[0], "region", [((i + 1) % regions, i) for i in range(regions)])
        own_columns = up.astype(jnp.float32) + down.astype(jnp.float32)

    all_grads = gathered(row_grads.astype(jnp.bfloat16), "patch", ks).reshape(owners * 2 * SIDE, CHANNELS)
    wanted = jnp.concatenate([halo_index[:, 1 : SIDE + 1], halo_index[:, SIDE + 3 : 2 * SIDE + 3]], axis=1)
    wanted_slot = jnp.take(wanted, owner_id ^ order_of(ks, owners), axis=0).reshape(-1)
    base = (region_id * owners + owner_id) * 4 * SIDE
    hit = (wanted_slot - base)[None, :] == jnp.arange(2 * SIDE)[:, None]
    own_rows = jnp.dot(hit.astype(jnp.bfloat16), all_grads, preferred_element_type=jnp.float32)

    inner = running[1 : SIDE + 1, 1 : SIDE + 1]
    zeros = jnp.zeros((SIDE - 2, SIDE, CHANNELS), jnp.float32)
    inner = inner + jnp.concatenate([own_rows[None, :SIDE], zeros, own_rows[None, SIDE:]], axis=0)
    gap = jnp.zeros((SIDE, SIDE - 2, CHANNELS), jnp.float32)
    inner = inner + jnp.concatenate([own_columns[:SIDE, None], gap, own_columns[SIDE:, None]], axis=1)
    input_grad = inner.astype(jnp.bfloat16).reshape(1, SIDE, SIDE * CHANNELS)

    for axis, many in (("region", regions), ("patch", owners)):
        for k in steps_of(many):
            sent = terms.astype(jnp.bfloat16)
            terms = sent.astype(jnp.float32) + swap(sent, axis, k).astype(jnp.float32)
    scale = 1.0 / math.sqrt(regions * owners * SIDE * SIDE)
    terms = terms * scale
    return (input_grad, terms[: 9 * CHANNELS], terms[9 * CHANNELS])


def order_of(ks, owners):
    slots = jnp.arange(owners)
    result = jnp.zeros_like(slots)
    for bit, k in enumerate(ks):
        result = result + jnp.where((slots >> bit) & 1 != 0, k, 0)
    return result


def solution(mesh):
    placed = (
        P(("region", "patch"), None, None),
        P(),
        P(),
        P(("region", "patch"), None, None),
        P("region", None),
    )
    return jax.shard_map(
        body,
        mesh=mesh,
        in_specs=placed,
        out_specs=(P(("region", "patch"), None, None), P(), P()),
        check_vma=False,
    )
```

```python
import functools
import math

import jax
import jax.numpy as jnp
from jax import lax
from jax.experimental import pallas as pl
from jax.experimental.pallas import tpu as pltpu
from jax.sharding import PartitionSpec as P

CHANNELS = 64
SIDE = 64
PAIRS = SIDE // 2
LANES = 2 * CHANNELS
ROWS = PAIRS * SIDE
WROWS = 5 * CHANNELS
F32 = jnp.float32
BF16 = jnp.bfloat16


def call(kernel, outs, *args, scratch=(), flops=0, moved=0):
    whole = pl.BlockSpec(memory_space=pltpu.VMEM)
    shapes = [jax.ShapeDtypeStruct(s, d) for s, d in outs]
    return pl.pallas_call(
        kernel,
        out_shape=shapes,
        in_specs=[whole] * len(args),
        out_specs=[whole] * len(outs),
        scratch_shapes=list(scratch),
        compiler_params=pltpu.CompilerParams(vmem_limit_bytes=48 * 2**20),
        cost_estimate=pl.CostEstimate(flops=flops, bytes_accessed=moved, transcendentals=0),
    )(*args)


def iota(shape, dim):
    return lax.broadcasted_iota(jnp.int32, shape, dim)


def low(shape):
    return iota(shape, len(shape) - 1) < CHANNELS


def turn(x):
    return pltpu.roll(x, CHANNELS, 1)


def tile(q):
    return pl.ds(pl.multiple_of(q * LANES, LANES), LANES)


def block(q):
    return pl.ds(pl.multiple_of(q * SIDE, SIDE), SIDE)


def dot(a, b, dims=((1,), (0,))):
    return lax.dot_general(a, b, (dims, ((), ())), preferred_element_type=F32)


NT = ((1,), (1,))
TN = ((0,), (0,))


def shifted_copies(load, p0, p1, p2):
    is_low = low((SIDE, LANES))
    row = iota((SIDE, LANES), 0)

    def put(q, before, now):
        v = jnp.where(is_low, before, now)
        p1[block(q), :] = v.astype(BF16)
        p0[block(q), :] = jnp.where(row == 0, 0.0, pltpu.roll(v, 1, 0)).astype(BF16)
        p2[block(q), :] = jnp.where(row == SIDE - 1, 0.0, pltpu.roll(v, SIDE - 1, 0)).astype(BF16)

    def step(q, before):
        now = turn(load(q))
        put(q, before, now)
        return now

    zero = jnp.zeros((SIDE, LANES), F32)
    last = lax.fori_loop(0, PAIRS, step, zero, unroll=2)
    put(PAIRS, last, zero)


def product(p0, p1, p2, w_ref, start, n, dims):
    total = None
    for a, p in enumerate((p0, p1, p2)):
        window = jnp.concatenate([p[pl.ds(start, n), :], p[pl.ds(start + SIDE, n), :]], axis=1)
        term = dot(window, w_ref[a], dims)
        total = term if total is None else total + term
    return total


def rim_kernel(x_ref, rows_ref, cols_ref, scr):
    for q in range(PAIRS):
        lanes = slice(q * LANES, (q + 1) * LANES)
        scr[q : q + 1, :] = x_ref[0:16, lanes].astype(F32)[0:1]
        scr[PAIRS + q : PAIRS + q + 1, :] = x_ref[SIDE - 16 : SIDE, lanes].astype(F32)[15:16]
    rows_ref[...] = scr[...].astype(BF16)
    first = x_ref[:, 0:LANES].astype(F32)
    last = x_ref[:, (PAIRS - 1) * LANES :].astype(F32)
    cols_ref[...] = jnp.where(low((SIDE, LANES)), first, last).astype(BF16)


def before_kernel(x_ref, w_ref, bias_ref, p0, p1, p2, s_ref):
    shifted_copies(lambda q: x_ref[:, tile(q)].astype(F32), p0, p1, p2)
    n = 4 * SIDE

    def step(c, carry):
        start = pl.multiple_of(c * n, n)
        s_ref[pl.ds(start, n), :] = product(p0, p1, p2, w_ref, start, n, NT) + bias_ref[0:1, :]
        return carry

    lax.fori_loop(0, ROWS // n, step, 0)


def slope_times(signal, upstream):
    sigma = 1.0 / (1.0 + jnp.exp(-signal))
    return upstream * (sigma * (1.0 + signal * (1.0 - sigma)))


def halves(even, odd):
    return jnp.where(low(even.shape), even, odd)


def middle_kernel(
    s_in, cot_ref, p0, p1, p2, rows_ref, cols_ref, hot_ref, half_ref, w_ref, wb_ref, wc_ref, scat_ref,
    g_ref, msg_ref, own_ref, sums_ref, s_ref, ht, hb, gt, gb, gc,
):
    many = rows_ref.shape[0]
    cells = dot(hot_ref[:, :many], rows_ref[...]) + dot(hot_ref[:, many:], cols_ref[...])
    other = turn(cells)
    upper = half_ref[...] > 0.5
    as_low = jnp.where(upper, other, cells)
    as_high = jnp.where(upper, cells, other)
    ht[...] = halves(as_low[0:40], as_high[40:80])
    hb[...] = halves(as_low[80:120], as_high[120:160])
    sides = halves(as_low[160:224], as_high[224:288])
    is_low = low((SIDE, LANES))
    row = iota((SIDE, LANES), 0)
    top = jnp.concatenate([ht[0:PAIRS, :], ht[1 : PAIRS + 1, :]], axis=1).astype(BF16)
    bottom = jnp.concatenate([hb[0:PAIRS, :], hb[1 : PAIRS + 1, :]], axis=1).astype(BF16)
    s_ref[...] = s_in[...]
    first = pl.ds(0, PAIRS, stride=SIDE)
    final = pl.ds(SIDE - 1, PAIRS, stride=SIDE)
    s_ref[first, :] += dot(top, w_ref[0], NT)
    s_ref[final, :] += dot(bottom, w_ref[2], NT)
    moved = (
        jnp.where(row == 0, 0.0, pltpu.roll(sides, 1, 0)),
        sides,
        jnp.where(row == SIDE - 1, 0.0, pltpu.roll(sides, SIDE - 1, 0)),
    )
    lefts = [jnp.where(is_low, m, 0.0).astype(BF16) for m in moved]
    rights = [jnp.where(is_low, 0.0, m).astype(BF16) for m in moved]
    for a in range(3):
        s_ref[0:SIDE, :] += dot(lefts[a], w_ref[a, :, 0:LANES], NT)
        s_ref[ROWS - SIDE : ROWS, :] += dot(rights[a], w_ref[a, :, LANES:], NT)

    def step(q, carry):
        bias, before = carry
        g = slope_times(s_ref[block(q), :], cot_ref[:, tile(q)].astype(F32)).astype(BF16)
        g_ref[block(q), :] = g
        wide = g.astype(F32)
        now = turn(wide)
        pair = jnp.where(is_low, before, now)
        gt[pl.ds(q, 1), :] = pair[0:1]
        gb[pl.ds(q, 1), :] = pair[SIDE - 1 :]
        s_ref[block(q), :] = wide
        return bias + jnp.sum(wide.reshape(8, 8, LANES), axis=0), now

    zero = jnp.zeros((SIDE, LANES), F32)
    bias, last = lax.fori_loop(0, PAIRS, step, (jnp.zeros((8, LANES), F32), zero), unroll=2)
    pair = jnp.where(is_low, last, 0.0)
    gt[PAIRS : PAIRS + 1, :] = pair[0:1]
    gb[PAIRS : PAIRS + 1, :] = pair[SIDE - 1 :]

    g = g_ref[...]
    g_first = s_ref[first, :].astype(BF16)
    g_final = s_ref[final, :].astype(BF16)
    terms = []
    for a, p in enumerate((p0, p1, p2)):
        for shift in (0, 1):
            t = dot(g, p[shift * SIDE : shift * SIDE + ROWS, :], TN)
            lanes = slice(shift * LANES, (shift + 1) * LANES)
            if a == 0:
                t += dot(g_first, top[:, lanes], TN)
            if a == 2:
                t += dot(g_final, bottom[:, lanes], TN)
            if shift == 0:
                t += dot(g[0:SIDE], lefts[a], TN)
            else:
                t += dot(g[ROWS - SIDE :], rights[a], TN)
            terms.append(t)

    def tap(m, high):
        a, b = m // 3, m % 3
        result = 0.0
        for e in (0, 1):
            w = e + b
            part = terms[2 * a + w // 2][e * CHANNELS : (e + 1) * CHANNELS]
            result = result + (part if (w % 2 == 1) == high else turn(part))
        return result

    total = jnp.sum(bias, axis=0, keepdims=True)
    total = total + turn(total)
    coarse = total.astype(BF16).astype(F32)
    fine = total - coarse
    for t in range(5):
        if t < 4:
            high = tap(2 * t + 1, True)
        else:
            high = jnp.where(row == 0, coarse, jnp.where(row == 1, fine, 0.0))
        msg_ref[t * SIDE : (t + 1) * SIDE, :] = halves(tap(2 * t, False), high).astype(BF16)

    for dest, src, tap_row in ((0, gt, 2), (1, gb, 0)):
        window = jnp.concatenate([src[0:PAIRS, :], src[1 : PAIRS + 1, :]], axis=1).astype(BF16)
        own_ref[dest * PAIRS : (dest + 1) * PAIRS, :] = dot(window, wb_ref[tap_row]).astype(BF16)

    gc[...] = jnp.zeros(gc.shape, F32)
    gc[8 : 8 + SIDE, :] = jnp.where(is_low, s_ref[0:SIDE, :], s_ref[ROWS - SIDE : ROWS, :])
    grads = dot(gc[8:88, :].astype(BF16), wc_ref[0])
    grads = grads + dot(gc[7:87, :].astype(BF16), wc_ref[1])
    grads = grads + dot(gc[6:86, :].astype(BF16), wc_ref[2])
    spread = dot(scat_ref[...], grads.astype(BF16))
    n = spread.shape[0] // 4
    l0, l1, r0, r1 = (spread[i * n : (i + 1) * n] for i in range(4))
    sums_ref[...] = halves(l0 + turn(r0), turn(l1) + r1).astype(BF16)


def inner_kernel(g_ref, wb_ref, out_ref, p0, p1, p2):
    shifted_copies(lambda q: g_ref[block(q), :].astype(F32), p0, p1, p2)
    n = 4 * SIDE

    def step(c, carry):
        start = pl.multiple_of(c * n, n)
        out_ref[pl.ds(start, n), :] = product(p0, p1, p2, wb_ref, start, n, ((1,), (0,)))
        return carry

    lax.fori_loop(0, ROWS // n, step, 0)


def added_weights(mine, other):
    total = mine[0:WROWS, :].astype(F32) + other[0:WROWS, :].astype(F32)
    tail = total[WROWS - SIDE :]
    whole = tail + pltpu.roll(tail, SIDE - 1, 0)
    return total[: WROWS - SIDE], tail, whole


def join_kernel(mine, other, *rest):
    extra, out = rest[:-1], rest[-1]
    total, tail, whole = added_weights(mine, other)
    out[0 : WROWS - SIDE, :] = total.astype(BF16)
    row = iota(tail.shape, 0)
    coarse = whole.astype(BF16).astype(F32)
    fine = pltpu.roll(whole - coarse, 1, 0)
    is_low = low(tail.shape)
    out[WROWS - SIDE : WROWS, :] = jnp.where(
        is_low, tail, jnp.where(row == 0, coarse, jnp.where(row == 1, fine, 0.0))
    ).astype(BF16)
    n = mine.shape[0] - WROWS
    if n:
        out[WROWS : WROWS + n, :] = mine[WROWS:, :]
        out[WROWS + n :, :] = other[WROWS:, :]
    if extra:
        out[WROWS:, :] = extra[0][...]


def last_kernel(scale, mine, other, inner, pick, side_a, side_b, grad_ref, wt_ref, bias_ref):
    total, tail, whole = added_weights(mine, other)
    for t in range(4):
        wt_ref[:, t * LANES : (t + 1) * LANES] = total[t * SIDE : (t + 1) * SIDE] * scale
    wt_ref[:, 4 * LANES :] = tail[:, :CHANNELS] * scale
    bias_ref[...] = turn(whole)[0:8] * scale
    n = mine.shape[0] - WROWS
    got = dot(pick[:, :n], mine[WROWS:, :]) + dot(pick[:, n:], other[WROWS:, :])
    a, b, c, d = (got[i * SIDE : (i + 1) * SIDE] for i in range(4))
    rims = halves(a + turn(b), turn(c) + d)
    sides = side_a[...].astype(F32)
    if side_b is not None:
        sides = sides + side_b[...].astype(F32)
    row = iota((SIDE, LANES), 0)
    is_low = low((SIDE, LANES))
    for q in range(PAIRS):
        v = inner[q * SIDE : (q + 1) * SIDE, :]
        v = v + jnp.where(row == 0, rims[q : q + 1], jnp.where(row == SIDE - 1, rims[PAIRS + q : PAIRS + q + 1], 0.0))
        if q == 0:
            v = v + jnp.where(is_low, sides, 0.0)
        if q == PAIRS - 1:
            v = v + jnp.where(is_low, 0.0, sides)
        grad_ref[:, q * LANES : (q + 1) * LANES] = v.astype(BF16)


def swap(x, axis, k):
    n = lax.axis_size(axis)
    return lax.ppermute(x, axis, [(i, i ^ k) for i in range(n)])


def shift(x, axis, by):
    n = lax.axis_size(axis)
    return lax.ppermute(x, axis, [(i, (i + by) % n) for i in range(n)])


def steps_of(n):
    ks = []
    k = n // 2
    while k:
        ks.append(k)
        k //= 2
    return ks


def slot_of(relative, ks):
    slot = jnp.zeros_like(relative)
    for bit, k in enumerate(ks):
        slot = slot + jnp.where((relative & k) != 0, 1 << bit, 0)
    return slot


def owner_of(slot, ks):
    result = jnp.zeros_like(slot)
    for bit, k in enumerate(ks):
        result = result + jnp.where((slot >> bit) & 1 != 0, k, 0)
    return result


def weights_of(fine_weight):
    wt = fine_weight.T.reshape(CHANNELS, 3, 3 * CHANNELS)
    zero = jnp.zeros((CHANNELS, CHANNELS), BF16)
    forward, backward, columns = [], [], []
    for a in range(3):
        rows = wt[:, a]
        forward.append(
            jnp.concatenate(
                [jnp.concatenate([rows, zero], axis=1), jnp.concatenate([zero, rows], axis=1)], axis=0
            )
        )
        taps = [wt[:, 2 - a, b * CHANNELS : (b + 1) * CHANNELS] for b in (2, 1, 0)]
        backward.append(
            jnp.concatenate(
                [jnp.concatenate(taps + [zero], axis=0), jnp.concatenate([zero] + taps, axis=0)], axis=1
            )
        )
        columns.append(
            jnp.concatenate(
                [
                    jnp.concatenate([rows[:, :CHANNELS], zero], axis=1),
                    jnp.concatenate([zero, rows[:, 2 * CHANNELS :]], axis=1),
                ],
                axis=0,
            )
        )
    return jnp.stack(forward), jnp.stack(backward), jnp.stack(columns)


def body(fine_input, fine_weight, fine_bias, cotangent, halo_index):
    owners = lax.axis_size("patch")
    regions = lax.axis_size("region")
    owner_id = lax.axis_index("patch")
    region_id = lax.axis_index("region")
    ks = steps_of(owners)
    blocks = 1 if regions == 2 else 2
    x = fine_input.reshape(SIDE, SIDE * CHANNELS)
    cot = cotangent.reshape(SIDE, SIDE * CHANNELS)
    pair = ((ROWS + SIDE, LANES), BF16)

    rows, cols = call(
        rim_kernel, [((SIDE, LANES), BF16)] * 2, x, scratch=[pltpu.VMEM((SIDE, LANES), F32)]
    )
    if regions == 2:
        cols = swap(cols, "region", 1)
    else:
        cols = jnp.concatenate([shift(cols, "region", 1), shift(cols, "region", -1)], axis=0)
    for k in ks:
        rows = jnp.concatenate([rows, swap(rows, "patch", k)], axis=0)

    forward, backward, columns = weights_of(fine_weight)
    bias_pair = jnp.broadcast_to(jnp.tile(fine_bias, 2)[None], (8, LANES))
    p0, p1, p2, signal = call(
        before_kernel, [pair, pair, pair, ((ROWS, LANES), F32)], x, forward, bias_pair,
        flops=2 * ROWS * 768 * 128, moved=4 * 2**20,
    )

    own = lax.dynamic_index_in_dim(halo_index, owner_id, 0, keepdims=False)
    source, within = own // (4 * SIDE), own % (4 * SIDE)
    is_row = within < 2 * SIDE
    slot = slot_of((source % owners) ^ owner_id, ks)
    after = (source // owners - region_id) % regions == 1
    column_row = within % SIDE + (0 if blocks == 1 else jnp.where(after, SIDE, 0))
    column_half = (within - 2 * SIDE) // SIDE
    place = jnp.where(is_row, slot * SIDE + within // 2, owners * SIDE + column_row)
    half = jnp.where(is_row, within % 2, column_half)

    def cells_of(v, fill):
        def padded(u):
            return jnp.concatenate([u, jnp.full((40 - PAIRS - 1,), fill, v.dtype)])

        top, bottom = v[0 : SIDE + 2], v[SIDE + 2 : 2 * SIDE + 4]
        return jnp.concatenate(
            [padded(top[0::2]), padded(top[1::2]), padded(bottom[0::2]), padded(bottom[1::2]), v[2 * SIDE + 4 :]]
        )

    hot = (cells_of(place, -1)[:, None] == jnp.arange((owners + blocks) * SIDE)[None]).astype(BF16)
    half_mask = jnp.broadcast_to(cells_of(half, 0).astype(F32)[:, None], (hot.shape[0], LANES))

    def ring(v, fill):
        edge = 2 * SIDE + 4
        pad = jnp.full((80 - SIDE - 2,), fill, v.dtype)
        left = jnp.concatenate([v[0:1], v[edge : edge + SIDE], v[SIDE + 2 : SIDE + 3], pad])
        right = jnp.concatenate([v[SIDE + 1 : SIDE + 2], v[edge + SIDE :], v[edge - 1 : edge], pad])
        return left, right

    scatter = []
    for row_of, half_of in zip(ring(column_row, -1), ring(column_half, 0)):
        for s in range(2):
            scatter.append(
                (jnp.arange(blocks * SIDE)[:, None] == jnp.where(half_of == s, row_of, -1)[None]).astype(BF16)
            )
    scatter = jnp.concatenate(scatter, axis=0)

    wanted = jnp.concatenate([halo_index[:, 1 : SIDE + 1], halo_index[:, SIDE + 3 : 2 * SIDE + 3]], axis=1)
    wanted = jnp.take(wanted, owner_id ^ owner_of(jnp.arange(owners), ks), axis=0)
    wanted = wanted - (region_id * owners + owner_id) * 4 * SIDE
    wanted = wanted.reshape(owners * SIDE, 2)
    pick = jnp.concatenate(
        [
            ((2 * jnp.arange(SIDE) + e)[:, None] == wanted[:, s][None]).astype(BF16)
            for e in range(2)
            for s in range(2)
        ],
        axis=0,
    )

    line = pltpu.VMEM((40, LANES), F32)
    grad, message, own_rows, sums = call(
        middle_kernel,
        [((ROWS, LANES), BF16), ((WROWS, LANES), BF16), ((SIDE, LANES), BF16), ((blocks * SIDE, LANES), BF16)],
        signal, cot, p0, p1, p2, rows, cols, hot, half_mask, forward, backward, columns, scatter,
        scratch=[pltpu.VMEM((ROWS, LANES), F32), line, line, line, line, pltpu.VMEM((96, LANES), F32)],
        flops=2 * ROWS * 768 * 128, moved=4 * 2**20,
    )

    if regions == 2:
        sides = [swap(sums, "region", 1)]
    else:
        sides = [shift(sums[SIDE:], "region", 1), shift(sums[:SIDE], "region", -1)]
    inner = call(
        inner_kernel, [((ROWS, LANES), F32)], grad, backward,
        scratch=[pltpu.VMEM((ROWS + SIDE, LANES), BF16)] * 3,
        flops=2 * ROWS * 768 * 128, moved=4 * 2**20,
    )[0]

    region_ks = steps_of(regions)
    for k in region_ks:
        extra = (own_rows,) if k == region_ks[-1] else ()
        size = (WROWS + SIDE * len(extra), LANES)
        message = call(join_kernel, [(size, BF16)], message, swap(message, "region", k), *extra)[0]
    for k in ks[:-1]:
        size = (2 * message.shape[0] - WROWS, LANES)
        message = call(join_kernel, [(size, BF16)], message, swap(message, "patch", k))[0]
    other = swap(message, "patch", ks[-1])
    scale = 1.0 / math.sqrt(regions * owners * SIDE * SIDE)
    kernel = functools.partial(last_kernel, scale)
    if len(sides) == 1:
        kernel = functools.partial(last_one_side, scale)
    input_grad, weight_grad, bias_grad = call(
        kernel,
        [((SIDE, SIDE * CHANNELS), BF16), ((CHANNELS, 9 * CHANNELS), F32), ((8, LANES), F32)],
        message, other, inner, pick, *sides,
    )
    return input_grad.reshape(1, SIDE, SIDE * CHANNELS), weight_grad.T, bias_grad[0, :CHANNELS]


def last_one_side(scale, mine, other, inner, pick, side_a, grad_ref, wt_ref, bias_ref):
    last_kernel(scale, mine, other, inner, pick, side_a, None, grad_ref, wt_ref, bias_ref)


def solution(mesh):
    placed = (
        P(("region", "patch"), None, None),
        P(),
        P(),
        P(("region", "patch"), None, None),
        P("region", None),
    )
    return jax.shard_map(
        body,
        mesh=mesh,
        in_specs=placed,
        out_specs=(P(("region", "patch"), None, None), P(), P()),
        check_vma=False,
    )
```

```python
import functools
import math

import jax
import jax.numpy as jnp
from jax import lax
from jax.experimental import pallas as pl
from jax.experimental.pallas import tpu as pltpu
from jax.sharding import PartitionSpec as P

CHANNELS = 64
SIDE = 64
PAIRS = SIDE // 2
LANES = 2 * CHANNELS
ROWS = PAIRS * SIDE
WROWS = 5 * CHANNELS
F32 = jnp.float32
BF16 = jnp.bfloat16


def call(kernel, outs, *args, scratch=(), flops=0, moved=0):
    whole = pl.BlockSpec(memory_space=pltpu.VMEM)
    shapes = [jax.ShapeDtypeStruct(s, d) for s, d in outs]
    return pl.pallas_call(
        kernel,
        out_shape=shapes,
        in_specs=[whole] * len(args),
        out_specs=[whole] * len(outs),
        scratch_shapes=list(scratch),
        compiler_params=pltpu.CompilerParams(vmem_limit_bytes=48 * 2**20),
        cost_estimate=pl.CostEstimate(flops=flops, bytes_accessed=moved, transcendentals=0),
    )(*args)


def iota(shape, dim):
    return lax.broadcasted_iota(jnp.int32, shape, dim)


def low(shape):
    return iota(shape, len(shape) - 1) < CHANNELS


def turn(x):
    return pltpu.roll(x, CHANNELS, 1)


def tile(q):
    return pl.ds(pl.multiple_of(q * LANES, LANES), LANES)


def block(q):
    return pl.ds(pl.multiple_of(q * SIDE, SIDE), SIDE)


def dot(a, b, dims=((1,), (0,))):
    return lax.dot_general(a, b, (dims, ((), ())), preferred_element_type=F32)


NT = ((1,), (1,))
TN = ((0,), (0,))


def shifted_copies(load, p0, p1, p2):
    is_low = low((SIDE, LANES))
    row = iota((SIDE, LANES), 0)

    def put(q, before, now):
        v = jnp.where(is_low, before, now)
        p1[block(q), :] = v.astype(BF16)
        p0[block(q), :] = jnp.where(row == 0, 0.0, pltpu.roll(v, 1, 0)).astype(BF16)
        p2[block(q), :] = jnp.where(row == SIDE - 1, 0.0, pltpu.roll(v, SIDE - 1, 0)).astype(BF16)

    def step(q, before):
        now = turn(load(q))
        put(q, before, now)
        return now

    zero = jnp.zeros((SIDE, LANES), F32)
    last = lax.fori_loop(0, PAIRS, step, zero, unroll=2)
    put(PAIRS, last, zero)


def product(p0, p1, p2, w_ref, start, n, dims):
    total = None
    for a, p in enumerate((p0, p1, p2)):
        window = jnp.concatenate([p[pl.ds(start, n), :], p[pl.ds(start + SIDE, n), :]], axis=1)
        term = dot(window, w_ref[a], dims)
        total = term if total is None else total + term
    return total


def rim_kernel(x_ref, rows_ref, cols_ref, scr):
    for q in range(PAIRS):
        lanes = slice(q * LANES, (q + 1) * LANES)
        scr[q : q + 1, :] = x_ref[0:16, lanes].astype(F32)[0:1]
        scr[PAIRS + q : PAIRS + q + 1, :] = x_ref[SIDE - 16 : SIDE, lanes].astype(F32)[15:16]
    rows_ref[...] = scr[...].astype(BF16)
    first = x_ref[:, 0:LANES].astype(F32)
    last = x_ref[:, (PAIRS - 1) * LANES :].astype(F32)
    cols_ref[...] = halves(first, last).astype(BF16)


def bits_moved(v, pairs):
    result = jnp.zeros_like(v)
    for from_bit, to_bit in pairs:
        result = result | (((v >> from_bit) & 1) << to_bit)
    return result


def plan_kernel(owners, regions, blocks, index_ref, hot_ref, half_ref, scr):
    owner = lax.axis_index("patch")
    region = lax.axis_index("region")
    bits = owners.bit_length() - 1
    index = index_ref[pl.ds(owner, 1), :]
    source, within = index >> 8, index & 255
    slot = bits_moved((source & (owners - 1)) ^ owner, slot_bits(owners))
    row = within & (SIDE - 1)
    if blocks == 2:
        row = row + jnp.where((((source >> bits) - region + regions) & (regions - 1)) == 1, SIDE, 0)
    is_row = within < 2 * SIDE
    place = jnp.where(is_row, slot * SIDE + (within >> 1), owners * SIDE + row)
    half = jnp.where(is_row, within & 1, (within >> 6) & 1)
    count = index.shape[1]
    scr[...] = jnp.full(scr.shape, -1.0, F32)
    scr[0:1, 0:count] = place.astype(F32)
    scr[1:2, 0:count] = half.astype(F32)
    column = jnp.transpose(scr[...])[0 : hot_ref.shape[0]]
    half_ref[...] = jnp.broadcast_to(column[:, 1:2], half_ref.shape)
    place = column[:, 0:1].astype(jnp.int32)
    for c in range(0, hot_ref.shape[1], LANES):
        n = min(LANES, hot_ref.shape[1] - c)
        hot_ref[:, c : c + n] = (place == iota((hot_ref.shape[0], n), 1) + c).astype(F32).astype(BF16)


def pick_kernel(owners, index_ref, pick_ref):
    owner = lax.axis_index("patch")
    base = (lax.axis_index("region") * owners + owner) * 4 * SIDE
    back = [(b, a) for a, b in slot_bits(owners)]
    want = 2 * iota((SIDE, LANES), 0)
    is_low = low((1, LANES))
    for t in range(owners // 2):
        pair = []
        for slot in (2 * t, 2 * t + 1):
            k = sum(1 << to for frm, to in back if (slot >> frm) & 1)
            line = index_ref[pl.ds(owner ^ k, 1), :]
            pair.append((line[:, 1 : SIDE + 1], line[:, SIDE + 3 : 2 * SIDE + 3]))
        for s in range(2):
            both = jnp.concatenate([pair[0][s], pair[1][s]], axis=1) - base
            for e in range(2):
                hit = (both == want + e).astype(F32).astype(BF16)
                n = 2 * e + s
                pick_ref[n * SIDE : (n + 1) * SIDE, t * LANES : (t + 1) * LANES] = hit


def weights_kernel(wt_ref, w_ref, wb_ref, wc_ref):
    wide = [wt_ref[:, t * LANES : (t + 1) * LANES].astype(F32) for t in range(4)]
    tail = wt_ref[:, 4 * LANES :].astype(F32)
    wide.append(jnp.concatenate([tail, tail], axis=1))

    def at(a, b, high):
        m = 3 * a + b
        v = wide[m // 2]
        return v if m == 8 or (m % 2 == 1) == high else turn(v)

    def pair(a, left, right):
        zero = jnp.zeros((CHANNELS, LANES), F32)
        lo = zero if left is None else at(a, left, False)
        hi = zero if right is None else at(a, right, True)
        return halves(lo, hi).astype(BF16)

    c = CHANNELS
    for a in range(3):
        w_ref[a, 0:c, 0:LANES] = pair(a, 0, 1)
        w_ref[a, 0:c, LANES:] = pair(a, 2, None)
        w_ref[a, c:, 0:LANES] = pair(a, None, 0)
        w_ref[a, c:, LANES:] = pair(a, 1, 2)
        for w, (left, right) in enumerate(((2, None), (1, 2), (0, 1), (None, 0))):
            wb_ref[2 - a, w * c : (w + 1) * c, :] = pair(a, left, right)
        wc_ref[a, 0:c, :] = pair(a, 0, None)
        wc_ref[a, c:, :] = pair(a, None, 2)


def copies_kernel(x_ref, p0, p1, p2):
    shifted_copies(lambda q: x_ref[:, tile(q)].astype(F32), p0, p1, p2)


def signal_kernel(p0, p1, p2, w_ref, bias_ref, s_ref):
    n = 4 * SIDE
    bias = jnp.concatenate([bias_ref[...], bias_ref[...]], axis=1)

    def step(c, carry):
        start = pl.multiple_of(c * n, n)
        s_ref[pl.ds(start, n), :] = product(p0, p1, p2, w_ref, start, n, NT) + bias
        return carry

    lax.fori_loop(0, ROWS // n, step, 0)


def slope_times(signal, upstream):
    sigma = 1.0 / (1.0 + jnp.exp(-signal))
    return upstream * (sigma * (1.0 + signal * (1.0 - sigma)))


def halves(even, odd):
    return jnp.where(low(even.shape), even, odd)


def middle_kernel(
    s_in, cot_ref, p0, p1, p2, rows_ref, cols_ref, hot_ref, half_ref, w_ref, wb_ref, wc_ref,
    g_ref, msg_ref, own_ref, sums_ref, s_ref, cell_scr, gt, gb, gc, own_scr,
):
    many = rows_ref.shape[0]
    cells = dot(hot_ref[:, :many], rows_ref[...]) + dot(hot_ref[:, many:], cols_ref[...])
    other = turn(cells)
    upper = half_ref[...] > 0.5
    edge = 2 * SIDE + 4
    as_low = jnp.where(upper, other, cells)
    as_high = jnp.where(upper, cells, other)
    sides = halves(as_low[edge : edge + SIDE], as_high[edge + SIDE : edge + 2 * SIDE])
    odd = iota(cells.shape, 0) % 2 == 1
    cell_scr[...] = jnp.where(odd, as_high, as_low)

    def line_of(start):
        even_cells = cell_scr[pl.ds(start, PAIRS + 1, stride=2), :]
        odd_cells = cell_scr[pl.ds(start + 1, PAIRS + 1, stride=2), :]
        both = halves(even_cells, odd_cells)
        return jnp.concatenate([both[0:PAIRS], both[1 : PAIRS + 1]], axis=1).astype(BF16)

    is_low = low((SIDE, LANES))
    row = iota((SIDE, LANES), 0)
    top = line_of(0)
    bottom = line_of(SIDE + 2)
    s_ref[...] = s_in[...]
    first = pl.ds(0, PAIRS, stride=SIDE)
    final = pl.ds(SIDE - 1, PAIRS, stride=SIDE)
    s_ref[first, :] += dot(top, w_ref[0], NT)
    s_ref[final, :] += dot(bottom, w_ref[2], NT)
    moved = (
        jnp.where(row == 0, 0.0, pltpu.roll(sides, 1, 0)),
        sides,
        jnp.where(row == SIDE - 1, 0.0, pltpu.roll(sides, SIDE - 1, 0)),
    )
    lefts = [jnp.where(is_low, m, 0.0).astype(BF16) for m in moved]
    rights = [jnp.where(is_low, 0.0, m).astype(BF16) for m in moved]
    for a in range(3):
        s_ref[0:SIDE, :] += dot(lefts[a], w_ref[a, :, 0:LANES], NT)
        s_ref[ROWS - SIDE : ROWS, :] += dot(rights[a], w_ref[a, :, LANES:], NT)

    def step(q, carry):
        bias, before = carry
        g = slope_times(s_ref[block(q), :], cot_ref[:, tile(q)].astype(F32)).astype(BF16)
        g_ref[block(q), :] = g
        wide = g.astype(F32)
        now = turn(wide)
        pair = jnp.where(is_low, before, now)
        gt[pl.ds(q, 1), :] = pair[0:1]
        gb[pl.ds(q, 1), :] = pair[SIDE - 1 :]
        s_ref[block(q), :] = wide
        return bias + jnp.sum(wide.reshape(8, 8, LANES), axis=0), now

    zero = jnp.zeros((SIDE, LANES), F32)
    bias, last = lax.fori_loop(0, PAIRS, step, (jnp.zeros((8, LANES), F32), zero), unroll=2)
    pair = jnp.where(is_low, last, 0.0)
    gt[PAIRS : PAIRS + 1, :] = pair[0:1]
    gb[PAIRS : PAIRS + 1, :] = pair[SIDE - 1 :]

    g = g_ref[...]
    g_first = s_ref[first, :].astype(BF16)
    g_final = s_ref[final, :].astype(BF16)
    terms = []
    for a, p in enumerate((p0, p1, p2)):
        for shift in (0, 1):
            t = dot(g, p[shift * SIDE : shift * SIDE + ROWS, :], TN)
            lanes = slice(shift * LANES, (shift + 1) * LANES)
            if a == 0:
                t += dot(g_first, top[:, lanes], TN)
            if a == 2:
                t += dot(g_final, bottom[:, lanes], TN)
            if shift == 0:
                t += dot(g[0:SIDE], lefts[a], TN)
            else:
                t += dot(g[ROWS - SIDE :], rights[a], TN)
            terms.append(t)

    def tap(m, high):
        a, b = m // 3, m % 3
        result = 0.0
        for e in (0, 1):
            w = e + b
            part = terms[2 * a + w // 2][e * CHANNELS : (e + 1) * CHANNELS]
            result = result + (part if (w % 2 == 1) == high else turn(part))
        return result

    total = jnp.sum(bias, axis=0, keepdims=True)
    total = total + turn(total)
    coarse = total.astype(BF16).astype(F32)
    fine = total - coarse
    for t in range(5):
        if t < 4:
            high = tap(2 * t + 1, True)
        else:
            high = jnp.where(row == 0, coarse, jnp.where(row == 1, fine, 0.0))
        msg_ref[t * SIDE : (t + 1) * SIDE, :] = halves(tap(2 * t, False), high).astype(BF16)

    lines = []
    for src, tap_row in ((gt, 2), (gb, 0)):
        window = jnp.concatenate([src[0:PAIRS, :], src[1 : PAIRS + 1, :]], axis=1).astype(BF16)
        lines.append(dot(window, wb_ref[tap_row]))
    own_scr[pl.ds(0, PAIRS, stride=2), :] = halves(lines[0], turn(lines[1]))
    own_scr[pl.ds(1, PAIRS, stride=2), :] = halves(turn(lines[0]), lines[1])
    own_ref[...] = own_scr[...].astype(BF16)

    gc[...] = jnp.zeros(gc.shape, F32)
    gc[8 : 8 + SIDE, :] = jnp.where(is_low, s_ref[0:SIDE, :], s_ref[ROWS - SIDE : ROWS, :])
    grads = dot(gc[8:88, :].astype(BF16), wc_ref[0])
    grads = grads + dot(gc[7:87, :].astype(BF16), wc_ref[1])
    grads = grads + dot(gc[6:86, :].astype(BF16), wc_ref[2])
    other = turn(grads)
    lefts = halves(grads, other)
    rights = halves(other, grads)
    cell_scr[...] = jnp.zeros(cell_scr.shape, F32)
    for at, src, first_row, n in (
        (0, lefts, 0, 1), (SIDE + 1, rights, 0, 1), (SIDE + 2, lefts, SIDE + 1, 1), (edge - 1, rights, SIDE + 1, 1),
        (edge, lefts, 1, SIDE), (edge + SIDE, rights, 1, SIDE),
    ):
        cell_scr[at : at + n, :] = src[first_row : first_row + n]
    placed = jnp.where(upper == low(cells.shape), 0.0, cell_scr[...]).astype(BF16)
    sums_ref[...] = dot(hot_ref[:, many:], placed, TN).astype(BF16)


def grad_copies_kernel(g_ref, p0, p1, p2):
    shifted_copies(lambda q: g_ref[block(q), :].astype(F32), p0, p1, p2)


def inner_kernel(p0, p1, p2, wb_ref, out_ref):
    n = 4 * SIDE

    def step(c, carry):
        start = pl.multiple_of(c * n, n)
        out_ref[pl.ds(start, n), :] = product(p0, p1, p2, wb_ref, start, n, ((1,), (0,)))
        return carry

    lax.fori_loop(0, ROWS // n, step, 0)


def added_weights(mine, other):
    total = mine[0:WROWS, :].astype(F32) + other[0:WROWS, :].astype(F32)
    tail = total[WROWS - SIDE :]
    whole = tail + pltpu.roll(tail, SIDE - 1, 0)
    return total[: WROWS - SIDE], tail, whole


def join_kernel(mine, other, *rest):
    extra, out = rest[:-1], rest[-1]
    total, tail, whole = added_weights(mine, other)
    out[0 : WROWS - SIDE, :] = total.astype(BF16)
    row = iota(tail.shape, 0)
    coarse = whole.astype(BF16).astype(F32)
    fine = pltpu.roll(whole - coarse, 1, 0)
    is_low = low(tail.shape)
    out[WROWS - SIDE : WROWS, :] = jnp.where(
        is_low, tail, jnp.where(row == 0, coarse, jnp.where(row == 1, fine, 0.0))
    ).astype(BF16)
    n = mine.shape[0] - WROWS
    if n:
        out[WROWS : WROWS + n, :] = mine[WROWS:, :]
        out[WROWS + n :, :] = other[WROWS:, :]
    if extra:
        out[WROWS:, :] = extra[0][...]


def last_kernel(scale, mine, other, inner, pick, side_a, side_b, grad_ref, wt_ref, bias_ref):
    total, tail, whole = added_weights(mine, other)
    for t in range(4):
        wt_ref[:, t * LANES : (t + 1) * LANES] = total[t * SIDE : (t + 1) * SIDE] * scale
    wt_ref[:, 4 * LANES :] = tail[:, :CHANNELS] * scale
    bias_ref[...] = turn(whole)[0:1, :CHANNELS] * scale
    n = mine.shape[0] - WROWS
    got = dot(pick[:, :n], mine[WROWS:, :]) + dot(pick[:, n:], other[WROWS:, :])
    a, b, c, d = (got[i * SIDE : (i + 1) * SIDE] for i in range(4))
    rims = halves(a + turn(b), turn(c) + d)
    sides = side_a[...].astype(F32)
    if side_b is not None:
        sides = sides + side_b[...].astype(F32)
    row = iota((SIDE, LANES), 0)
    is_low = low((SIDE, LANES))
    for q in range(PAIRS):
        v = inner[q * SIDE : (q + 1) * SIDE, :]
        v = v + jnp.where(row == 0, rims[q : q + 1], jnp.where(row == SIDE - 1, rims[PAIRS + q : PAIRS + q + 1], 0.0))
        if q == 0:
            v = v + jnp.where(is_low, sides, 0.0)
        if q == PAIRS - 1:
            v = v + jnp.where(is_low, 0.0, sides)
        grad_ref[:, q * LANES : (q + 1) * LANES] = v.astype(BF16)


def swap(x, axis, k):
    n = lax.axis_size(axis)
    return lax.ppermute(x, axis, [(i, i ^ k) for i in range(n)])


def shift(x, axis, by):
    n = lax.axis_size(axis)
    return lax.ppermute(x, axis, [(i, (i + by) % n) for i in range(n)])


def steps_of(n):
    ks = []
    k = n // 2
    while k:
        ks.append(k)
        k //= 2
    return ks


def slot_bits(owners):
    bits = owners.bit_length() - 1
    return [(bits - 1 - i, i) for i in range(bits)]


def body(fine_input, fine_weight, fine_bias, cotangent, halo_index):
    owners = lax.axis_size("patch")
    regions = lax.axis_size("region")
    owner_id = lax.axis_index("patch")
    region_id = lax.axis_index("region")
    ks = steps_of(owners)
    blocks = 1 if regions == 2 else 2
    x = fine_input.reshape(SIDE, SIDE * CHANNELS)
    cot = cotangent.reshape(SIDE, SIDE * CHANNELS)
    pair = ((ROWS + SIDE, LANES), BF16)

    rows, cols = call(
        rim_kernel, [((SIDE, LANES), BF16)] * 2, x, scratch=[pltpu.VMEM((SIDE, LANES), F32)]
    )
    if regions == 2:
        cols = swap(cols, "region", 1)
    else:
        cols = jnp.concatenate([shift(cols, "region", 1), shift(cols, "region", -1)], axis=0)
    for k in ks:
        rows = jnp.concatenate([rows, swap(rows, "patch", k)], axis=0)

    cells = 272
    hot, half_mask = call(
        functools.partial(plan_kernel, owners, regions, blocks),
        [((cells, (owners + blocks) * SIDE), BF16), ((cells, LANES), F32)],
        halo_index, scratch=[pltpu.VMEM((8, 384), F32)],
    )
    forward, backward, columns = call(
        weights_kernel,
        [((3, LANES, 2 * LANES), BF16), ((3, 2 * LANES, LANES), BF16), ((3, LANES, LANES), BF16)],
        fine_weight.T,
    )
    copies = call(copies_kernel, [pair] * 3, x, moved=2 * 2**20)
    signal = call(
        signal_kernel, [((ROWS, LANES), F32)], *copies, forward, fine_bias.reshape(1, CHANNELS),
        flops=2 * ROWS * 768 * 128, moved=3 * 2**20,
    )[0]

    line = pltpu.VMEM((40, LANES), F32)
    grad, message, own_rows, sums = call(
        middle_kernel,
        [((ROWS, LANES), BF16), ((WROWS, LANES), BF16), ((SIDE, LANES), BF16), ((blocks * SIDE, LANES), BF16)],
        signal, cot, *copies, rows, cols, hot, half_mask, forward, backward, columns,
        scratch=[
            pltpu.VMEM((ROWS, LANES), F32), pltpu.VMEM((cells, LANES), F32), line, line,
            pltpu.VMEM((96, LANES), F32), pltpu.VMEM((SIDE, LANES), F32),
        ],
        flops=2 * ROWS * 768 * 128, moved=4 * 2**20,
    )

    if regions == 2:
        sides = [swap(sums, "region", 1)]
    else:
        sides = [shift(sums[SIDE:], "region", 1), shift(sums[:SIDE], "region", -1)]
    pick = call(
        functools.partial(pick_kernel, owners), [((4 * SIDE, owners * SIDE), BF16)], halo_index
    )[0]
    grad_copies = call(grad_copies_kernel, [pair] * 3, grad, moved=2 * 2**20)
    inner = call(
        inner_kernel, [((ROWS, LANES), F32)], *grad_copies, backward, flops=2 * ROWS * 768 * 128, moved=3 * 2**20
    )[0]

    region_ks = steps_of(regions)
    for k in region_ks:
        extra = (own_rows,) if k == region_ks[-1] else ()
        size = (WROWS + SIDE * len(extra), LANES)
        message = call(join_kernel, [(size, BF16)], message, swap(message, "region", k), *extra)[0]
    for k in ks[:-1]:
        size = (2 * message.shape[0] - WROWS, LANES)
        message = call(join_kernel, [(size, BF16)], message, swap(message, "patch", k))[0]
    other = swap(message, "patch", ks[-1])
    scale = 1.0 / math.sqrt(regions * owners * SIDE * SIDE)
    kernel = functools.partial(last_kernel, scale)
    if len(sides) == 1:
        kernel = functools.partial(last_one_side, scale)
    input_grad, weight_grad, bias_grad = call(
        kernel,
        [((SIDE, SIDE * CHANNELS), BF16), ((CHANNELS, 9 * CHANNELS), F32), ((1, CHANNELS), F32)],
        message, other, inner, pick, *sides,
    )
    return input_grad.reshape(1, SIDE, SIDE * CHANNELS), weight_grad.T, bias_grad.reshape(CHANNELS)


def last_one_side(scale, mine, other, inner, pick, side_a, grad_ref, wt_ref, bias_ref):
    last_kernel(scale, mine, other, inner, pick, side_a, None, grad_ref, wt_ref, bias_ref)


def solution(mesh):
    placed = (
        P(("region", "patch"), None, None),
        P(),
        P(),
        P(("region", "patch"), None, None),
        P("region", None),
    )
    return jax.shard_map(
        body,
        mesh=mesh,
        in_specs=placed,
        out_specs=(P(("region", "patch"), None, None), P(), P()),
        check_vma=False,
    )
```

```python
import functools
import math

import jax
import jax.numpy as jnp
from jax import lax
from jax.experimental import pallas as pl
from jax.experimental.pallas import tpu as pltpu
from jax.sharding import PartitionSpec as P

CHANNELS = 64
SIDE = 64
PAIRS = SIDE // 2
LANES = 2 * CHANNELS
ROWS = PAIRS * SIDE
WROWS = 5 * CHANNELS // 2
F32 = jnp.float32
BF16 = jnp.bfloat16


def call(kernel, outs, *args, scratch=(), flops=0, moved=0, space=pltpu.VMEM):
    whole = pl.BlockSpec(memory_space=pltpu.VMEM)
    shapes = [jax.ShapeDtypeStruct(s, d) for s, d in outs]
    return pl.pallas_call(
        kernel,
        out_shape=shapes,
        in_specs=[pl.BlockSpec(memory_space=space)] * len(args),
        out_specs=[whole] * len(outs),
        scratch_shapes=list(scratch),
        compiler_params=pltpu.CompilerParams(vmem_limit_bytes=48 * 2**20),
        cost_estimate=pl.CostEstimate(flops=flops, bytes_accessed=moved, transcendentals=0),
    )(*args)


def iota(shape, dim):
    return lax.broadcasted_iota(jnp.int32, shape, dim)


def low(shape):
    return iota(shape, len(shape) - 1) < CHANNELS


def turn(x):
    return pltpu.roll(x, CHANNELS, 1)


def tile(q):
    return pl.ds(pl.multiple_of(q * LANES, LANES), LANES)


def block(q):
    return pl.ds(pl.multiple_of(q * SIDE, SIDE), SIDE)


def dot(a, b, dims=((1,), (0,))):
    return lax.dot_general(a, b, (dims, ((), ())), preferred_element_type=F32)


NT = ((1,), (1,))
TN = ((0,), (0,))


def shifted_copies(load, p0, p1, p2):
    is_low = low((SIDE, LANES))
    row = iota((SIDE, LANES), 0)

    def put(q, before, now):
        v = jnp.where(is_low, before, now)
        p1[block(q), :] = v.astype(BF16)
        p0[block(q), :] = jnp.where(row == 0, 0.0, pltpu.roll(v, 1, 0)).astype(BF16)
        p2[block(q), :] = jnp.where(row == SIDE - 1, 0.0, pltpu.roll(v, SIDE - 1, 0)).astype(BF16)

    def step(q, before):
        now = turn(load(q))
        put(q, before, now)
        return now

    zero = jnp.zeros((SIDE, LANES), F32)
    last = lax.fori_loop(0, PAIRS, step, zero, unroll=2)
    put(PAIRS, last, zero)


def product(p0, p1, p2, w_ref, start, n, dims):
    total = None
    for a, p in enumerate((p0, p1, p2)):
        window = jnp.concatenate([p[pl.ds(start, n), :], p[pl.ds(start + SIDE, n), :]], axis=1)
        term = dot(window, w_ref[a], dims)
        total = term if total is None else total + term
    return total


def rim_kernel(x_hbm, rows_ref, cols_ref, top, bottom, left, right, scr, sems):
    copies = [
        pltpu.make_async_copy(x_hbm.at[0:16, :], top, sems.at[0]),
        pltpu.make_async_copy(x_hbm.at[SIDE - 16 : SIDE, :], bottom, sems.at[1]),
        pltpu.make_async_copy(x_hbm.at[:, 0:LANES], left, sems.at[2]),
        pltpu.make_async_copy(x_hbm.at[:, (PAIRS - 1) * LANES :], right, sems.at[3]),
    ]
    for copy in copies:
        copy.start()
    for copy in copies:
        copy.wait()
    for q in range(PAIRS):
        lanes = slice(q * LANES, (q + 1) * LANES)
        scr[q : q + 1, :] = top[:, lanes].astype(F32)[0:1]
        scr[PAIRS + q : PAIRS + q + 1, :] = bottom[:, lanes].astype(F32)[15:16]
    rows_ref[...] = scr[...].astype(BF16)
    cols_ref[...] = halves(left[...].astype(F32), right[...].astype(F32)).astype(BF16)


def bits_moved(v, pairs):
    result = jnp.zeros_like(v)
    for from_bit, to_bit in pairs:
        result = result | (((v >> from_bit) & 1) << to_bit)
    return result


def plan_kernel(owners, regions, blocks, index_ref, hot_ref, half_ref, scr):
    owner = lax.axis_index("patch")
    region = lax.axis_index("region")
    bits = owners.bit_length() - 1
    index = index_ref[pl.ds(owner, 1), :]
    source, within = index >> 8, index & 255
    relative = (source & (owners - 1)) ^ owner
    even, odd = (bits_moved(relative, slot_bits(owners, core)) for core in range(2))
    slot = jnp.where((region & 1) == 1, odd, even)
    row = within & (SIDE - 1)
    if blocks == 2:
        row = row + jnp.where((((source >> bits) - region + regions) & (regions - 1)) == 1, SIDE, 0)
    is_row = within < 2 * SIDE
    place = jnp.where(is_row, slot * SIDE + (within >> 1), owners * SIDE + row)
    half = jnp.where(is_row, within & 1, (within >> 6) & 1)
    count = index.shape[1]
    scr[...] = jnp.full(scr.shape, -1.0, F32)
    scr[0:1, 0:count] = place.astype(F32)
    scr[1:2, 0:count] = half.astype(F32)
    column = jnp.transpose(scr[...])[0 : hot_ref.shape[0]]
    half_ref[...] = jnp.broadcast_to(column[:, 1:2], half_ref.shape)
    place = column[:, 0:1].astype(jnp.int32)
    for c in range(0, hot_ref.shape[1], LANES):
        n = min(LANES, hot_ref.shape[1] - c)
        hot_ref[:, c : c + n] = (place == iota((hot_ref.shape[0], n), 1) + c).astype(F32).astype(BF16)


def pick_kernel(owners, index_ref, pick_ref):
    owner, region = lax.axis_index("patch"), lax.axis_index("region")
    base = (region * owners + owner) * 4 * SIDE
    want = 2 * iota((SIDE, LANES), 0)
    for t in range(owners // 2):
        pair = []
        for slot in (2 * t, 2 * t + 1):
            even, odd = (
                sum(1 << frm for frm, to in slot_bits(owners, core) if (slot >> to) & 1) for core in range(2)
            )
            line = index_ref[pl.ds(owner ^ jnp.where((region & 1) == 1, odd, even), 1), :]
            pair.append((line[:, 1 : SIDE + 1], line[:, SIDE + 3 : 2 * SIDE + 3]))
        for s in range(2):
            both = jnp.concatenate([pair[0][s], pair[1][s]], axis=1) - base
            for e in range(2):
                hit = (both == want + e).astype(F32).astype(BF16)
                n = 2 * e + s
                pick_ref[n * SIDE : (n + 1) * SIDE, t * LANES : (t + 1) * LANES] = hit


def weights_kernel(wt_ref, w_ref, wb_ref, wc_ref):
    wide = [wt_ref[:, t * LANES : (t + 1) * LANES].astype(F32) for t in range(4)]
    tail = wt_ref[:, 4 * LANES :].astype(F32)
    wide.append(jnp.concatenate([tail, tail], axis=1))

    def at(a, b, high):
        m = 3 * a + b
        v = wide[m // 2]
        return v if m == 8 or (m % 2 == 1) == high else turn(v)

    def pair(a, left, right):
        zero = jnp.zeros((CHANNELS, LANES), F32)
        lo = zero if left is None else at(a, left, False)
        hi = zero if right is None else at(a, right, True)
        return halves(lo, hi).astype(BF16)

    c = CHANNELS
    for a in range(3):
        w_ref[a, 0:c, 0:LANES] = pair(a, 0, 1)
        w_ref[a, 0:c, LANES:] = pair(a, 2, None)
        w_ref[a, c:, 0:LANES] = pair(a, None, 0)
        w_ref[a, c:, LANES:] = pair(a, 1, 2)
        for w, (left, right) in enumerate(((2, None), (1, 2), (0, 1), (None, 0))):
            wb_ref[2 - a, w * c : (w + 1) * c, :] = pair(a, left, right)
        wc_ref[a, 0:c, :] = pair(a, 0, None)
        wc_ref[a, c:, :] = pair(a, None, 2)


def copies_kernel(x_ref, p0, p1, p2):
    shifted_copies(lambda q: x_ref[:, tile(q)].astype(F32), p0, p1, p2)


def signal_kernel(p0, p1, p2, w_ref, bias_ref, s_ref):
    n = 4 * SIDE
    bias = jnp.concatenate([bias_ref[...], bias_ref[...]], axis=1)

    def step(c, carry):
        start = pl.multiple_of(c * n, n)
        s_ref[pl.ds(start, n), :] = product(p0, p1, p2, w_ref, start, n, NT) + bias
        return carry

    lax.fori_loop(0, ROWS // n, step, 0)


def slope_times(signal, upstream):
    sigma = 1.0 / (1.0 + jnp.exp(-signal))
    return upstream * (sigma * (1.0 + signal * (1.0 - sigma)))


def halves(even, odd):
    return jnp.where(low(even.shape), even, odd)


def middle_kernel(
    s_in, cot_ref, p0, p1, p2, rows_ref, cols_ref, hot_ref, half_ref, w_ref, wb_ref, wc_ref,
    g_ref, keep_ref, send_ref, own_ref, sums_ref, s_ref, cell_scr, gt, gb, gc, own_scr, msg,
):
    many = rows_ref.shape[0]
    cells = dot(hot_ref[:, :many], rows_ref[...]) + dot(hot_ref[:, many:], cols_ref[...])
    other = turn(cells)
    upper = half_ref[...] > 0.5
    edge = 2 * SIDE + 4
    as_low = jnp.where(upper, other, cells)
    as_high = jnp.where(upper, cells, other)
    sides = halves(as_low[edge : edge + SIDE], as_high[edge + SIDE : edge + 2 * SIDE])
    odd = iota(cells.shape, 0) % 2 == 1
    cell_scr[...] = jnp.where(odd, as_high, as_low)

    def line_of(start):
        even_cells = cell_scr[pl.ds(start, PAIRS + 1, stride=2), :]
        odd_cells = cell_scr[pl.ds(start + 1, PAIRS + 1, stride=2), :]
        both = halves(even_cells, odd_cells)
        return jnp.concatenate([both[0:PAIRS], both[1 : PAIRS + 1]], axis=1).astype(BF16)

    is_low = low((SIDE, LANES))
    row = iota((SIDE, LANES), 0)
    top = line_of(0)
    bottom = line_of(SIDE + 2)
    s_ref[...] = s_in[...]
    first = pl.ds(0, PAIRS, stride=SIDE)
    final = pl.ds(SIDE - 1, PAIRS, stride=SIDE)
    s_ref[first, :] += dot(top, w_ref[0], NT)
    s_ref[final, :] += dot(bottom, w_ref[2], NT)
    moved = (
        jnp.where(row == 0, 0.0, pltpu.roll(sides, 1, 0)),
        sides,
        jnp.where(row == SIDE - 1, 0.0, pltpu.roll(sides, SIDE - 1, 0)),
    )
    lefts = [jnp.where(is_low, m, 0.0).astype(BF16) for m in moved]
    rights = [jnp.where(is_low, 0.0, m).astype(BF16) for m in moved]
    for a in range(3):
        s_ref[0:SIDE, :] += dot(lefts[a], w_ref[a, :, 0:LANES], NT)
        s_ref[ROWS - SIDE : ROWS, :] += dot(rights[a], w_ref[a, :, LANES:], NT)

    def step(q, carry):
        bias, before = carry
        g = slope_times(s_ref[block(q), :], cot_ref[:, tile(q)].astype(F32)).astype(BF16)
        g_ref[block(q), :] = g
        wide = g.astype(F32)
        now = turn(wide)
        pair = jnp.where(is_low, before, now)
        gt[pl.ds(q, 1), :] = pair[0:1]
        gb[pl.ds(q, 1), :] = pair[SIDE - 1 :]
        s_ref[block(q), :] = wide
        return bias + jnp.sum(wide.reshape(8, 8, LANES), axis=0), now

    zero = jnp.zeros((SIDE, LANES), F32)
    bias, last = lax.fori_loop(0, PAIRS, step, (jnp.zeros((8, LANES), F32), zero), unroll=2)
    pair = jnp.where(is_low, last, 0.0)
    gt[PAIRS : PAIRS + 1, :] = pair[0:1]
    gb[PAIRS : PAIRS + 1, :] = pair[SIDE - 1 :]

    g = g_ref[...]
    g_first = s_ref[first, :].astype(BF16)
    g_final = s_ref[final, :].astype(BF16)
    terms = []
    for a, p in enumerate((p0, p1, p2)):
        for shift in (0, 1):
            t = dot(g, p[shift * SIDE : shift * SIDE + ROWS, :], TN)
            lanes = slice(shift * LANES, (shift + 1) * LANES)
            if a == 0:
                t += dot(g_first, top[:, lanes], TN)
            if a == 2:
                t += dot(g_final, bottom[:, lanes], TN)
            if shift == 0:
                t += dot(g[0:SIDE], lefts[a], TN)
            else:
                t += dot(g[ROWS - SIDE :], rights[a], TN)
            terms.append(t)

    def tap(m, high):
        a, b = m // 3, m % 3
        result = 0.0
        for e in (0, 1):
            w = e + b
            part = terms[2 * a + w // 2][e * CHANNELS : (e + 1) * CHANNELS]
            result = result + (part if (w % 2 == 1) == high else turn(part))
        return result

    total = jnp.sum(bias, axis=0, keepdims=True)
    total = total + turn(total)
    coarse = total.astype(BF16).astype(F32)
    fine = total - coarse
    for t in range(5):
        if t < 4:
            high = tap(2 * t + 1, True)
        else:
            high = jnp.where(row == 0, coarse, jnp.where(row == 1, fine, 0.0))
        msg[t * SIDE : (t + 1) * SIDE, :] = halves(tap(2 * t, False), high)
    core = lax.axis_index("region") & 1
    keep_ref[...] = msg[pl.ds(pl.multiple_of(core * WROWS, WROWS), WROWS), :].astype(BF16)
    send_ref[...] = msg[pl.ds(pl.multiple_of((1 - core) * WROWS, WROWS), WROWS), :].astype(BF16)

    lines = []
    for src, tap_row in ((gt, 2), (gb, 0)):
        window = jnp.concatenate([src[0:PAIRS, :], src[1 : PAIRS + 1, :]], axis=1).astype(BF16)
        lines.append(dot(window, wb_ref[tap_row]))
    own_scr[pl.ds(0, PAIRS, stride=2), :] = halves(lines[0], turn(lines[1]))
    own_scr[pl.ds(1, PAIRS, stride=2), :] = halves(turn(lines[0]), lines[1])
    own_ref[...] = own_scr[...].astype(BF16)

    gc[...] = jnp.zeros(gc.shape, F32)
    gc[8 : 8 + SIDE, :] = jnp.where(is_low, s_ref[0:SIDE, :], s_ref[ROWS - SIDE : ROWS, :])
    grads = dot(gc[8:88, :].astype(BF16), wc_ref[0])
    grads = grads + dot(gc[7:87, :].astype(BF16), wc_ref[1])
    grads = grads + dot(gc[6:86, :].astype(BF16), wc_ref[2])
    other = turn(grads)
    lefts = halves(grads, other)
    rights = halves(other, grads)
    cell_scr[...] = jnp.zeros(cell_scr.shape, F32)
    for at, src, first_row, n in (
        (0, lefts, 0, 1), (SIDE + 1, rights, 0, 1), (SIDE + 2, lefts, SIDE + 1, 1), (edge - 1, rights, SIDE + 1, 1),
        (edge, lefts, 1, SIDE), (edge + SIDE, rights, 1, SIDE),
    ):
        cell_scr[at : at + n, :] = src[first_row : first_row + n]
    placed = jnp.where(upper == low(cells.shape), 0.0, cell_scr[...]).astype(BF16)
    sums_ref[...] = dot(hot_ref[:, many:], placed, TN).astype(BF16)


def grad_copies_kernel(g_ref, p0, p1, p2):
    shifted_copies(lambda q: g_ref[block(q), :].astype(F32), p0, p1, p2)


def inner_kernel(p0, p1, p2, wb_ref, out_ref):
    n = 4 * SIDE

    def step(c, carry):
        start = pl.multiple_of(c * n, n)
        out_ref[pl.ds(start, n), :] = product(p0, p1, p2, wb_ref, start, n, ((1,), (0,)))
        return carry

    lax.fori_loop(0, ROWS // n, step, 0)


def added_weights(mine, other):
    total = mine[0:WROWS, :].astype(F32) + other[0:WROWS, :].astype(F32)
    tail = total[WROWS - SIDE :]
    return total, tail + pltpu.roll(tail, SIDE - 1, 0)


def bias_lanes(shape):
    return jnp.logical_and(jnp.logical_not(low(shape)), (lax.axis_index("region") & 1) == 1)


def join_kernel(mine, other, *rest):
    extra, out = rest[:-1], rest[-1]
    total, whole = added_weights(mine, other)
    out[0 : WROWS - SIDE, :] = total[: WROWS - SIDE].astype(BF16)
    row = iota(whole.shape, 0)
    coarse = whole.astype(BF16).astype(F32)
    fine = pltpu.roll(whole - coarse, 1, 0)
    out[WROWS - SIDE : WROWS, :] = jnp.where(
        bias_lanes(whole.shape),
        jnp.where(row == 0, coarse, jnp.where(row == 1, fine, 0.0)),
        total[WROWS - SIDE :],
    ).astype(BF16)
    n = mine.shape[0] - WROWS
    if n:
        out[WROWS : WROWS + n, :] = mine[WROWS:, :]
        out[WROWS + n :, :] = other[WROWS:, :]
    if extra:
        out[WROWS:, :] = extra[0][...]


def close_kernel(scale, mine, other, out):
    total, whole = added_weights(mine, other)
    out[0 : WROWS - SIDE, :] = total[: WROWS - SIDE] * scale
    out[WROWS - SIDE :, :] = jnp.where(bias_lanes(whole.shape), whole, total[WROWS - SIDE :]) * scale


def weight_kernel(mine, other, wt_ref, bias_ref):
    odd = (lax.axis_index("region") & 1) == 1
    a, b = mine[...], other[...]
    full = jnp.concatenate([jnp.where(odd, b, a), jnp.where(odd, a, b)], axis=0)
    for t in range(4):
        wt_ref[:, t * LANES : (t + 1) * LANES] = full[t * SIDE : (t + 1) * SIDE]
    wt_ref[:, 4 * LANES :] = full[4 * SIDE :, :CHANNELS]
    bias_ref[...] = turn(full[4 * SIDE : 4 * SIDE + 8])[0:1, :CHANNELS]


def last_kernel(mine, other, inner, pick, *rest):
    side_refs, grad_ref = rest[:-1], rest[-1]
    n = mine.shape[0] - WROWS
    got = dot(pick[:, :n], mine[WROWS:, :]) + dot(pick[:, n:], other[WROWS:, :])
    a, b, c, d = (got[i * SIDE : (i + 1) * SIDE] for i in range(4))
    rims = halves(a + turn(b), turn(c) + d)
    sides = side_refs[0][...].astype(F32)
    for ref in side_refs[1:]:
        sides = sides + ref[...].astype(F32)
    row = iota((SIDE, LANES), 0)
    is_low = low((SIDE, LANES))
    for q in range(PAIRS):
        v = inner[q * SIDE : (q + 1) * SIDE, :]
        v = v + jnp.where(row == 0, rims[q : q + 1], jnp.where(row == SIDE - 1, rims[PAIRS + q : PAIRS + q + 1], 0.0))
        if q == 0:
            v = v + jnp.where(is_low, sides, 0.0)
        if q == PAIRS - 1:
            v = v + jnp.where(is_low, 0.0, sides)
        grad_ref[:, q * LANES : (q + 1) * LANES] = v.astype(BF16)


def swap(x, axis, k):
    n = lax.axis_size(axis)
    return lax.ppermute(x, axis, [(i, i ^ k) for i in range(n)])


def shift(x, axis, by):
    n = lax.axis_size(axis)
    return lax.ppermute(x, axis, [(i, (i + by) % n) for i in range(n)])


def steps_of(n):
    ks = []
    k = n // 2
    while k:
        ks.append(k)
        k //= 2
    return ks


def order_of(owners, core):
    bits = list(range(owners.bit_length() - 1))[::-1]
    return bits if core == 0 else bits[-1:] + bits[:-1]


def slot_bits(owners, core):
    return [(bit, step) for step, bit in enumerate(order_of(owners, core))]


def exchange(x, step):
    regions, owners = lax.axis_size("region"), lax.axis_size("patch")
    pairs = []
    for r in range(regions):
        k = 1 << order_of(owners, r % 2)[step]
        pairs += [(r * owners + i, r * owners + (i ^ k)) for i in range(owners)]
    return lax.ppermute(x, ("region", "patch"), pairs)


def body(fine_input, fine_weight, fine_bias, cotangent, halo_index):
    owners = lax.axis_size("patch")
    regions = lax.axis_size("region")
    steps = owners.bit_length() - 1
    blocks = 1 if regions == 2 else 2
    x = fine_input.reshape(SIDE, SIDE * CHANNELS)
    cot = cotangent.reshape(SIDE, SIDE * CHANNELS)
    pair = ((ROWS + SIDE, LANES), BF16)

    rows, cols = call(
        rim_kernel,
        [((SIDE, LANES), BF16)] * 2,
        x,
        scratch=[
            pltpu.VMEM((16, SIDE * CHANNELS), BF16), pltpu.VMEM((16, SIDE * CHANNELS), BF16),
            pltpu.VMEM((SIDE, LANES), BF16), pltpu.VMEM((SIDE, LANES), BF16),
            pltpu.VMEM((SIDE, LANES), F32), pltpu.SemaphoreType.DMA((4,)),
        ],
        space=pl.ANY,
    )
    if regions == 2:
        cols = swap(cols, "region", 1)
    else:
        cols = jnp.concatenate([shift(cols, "region", 1), shift(cols, "region", -1)], axis=0)
    for step in range(steps):
        rows = jnp.concatenate([rows, exchange(rows, step)], axis=0)

    cells = 272
    hot, half_mask = call(
        functools.partial(plan_kernel, owners, regions, blocks),
        [((cells, (owners + blocks) * SIDE), BF16), ((cells, LANES), F32)],
        halo_index, scratch=[pltpu.VMEM((8, 384), F32)],
    )
    forward, backward, columns = call(
        weights_kernel,
        [((3, LANES, 2 * LANES), BF16), ((3, 2 * LANES, LANES), BF16), ((3, LANES, LANES), BF16)],
        fine_weight.T,
    )
    copies = call(copies_kernel, [pair] * 3, x, moved=2 * 2**20)
    signal = call(
        signal_kernel, [((ROWS, LANES), F32)], *copies, forward, fine_bias.reshape(1, CHANNELS),
        flops=2 * ROWS * 768 * 128, moved=3 * 2**20,
    )[0]

    line = pltpu.VMEM((40, LANES), F32)
    grad, message, sent, own_rows, sums = call(
        middle_kernel,
        [((ROWS, LANES), BF16), ((WROWS, LANES), BF16), ((WROWS, LANES), BF16), ((SIDE, LANES), BF16), ((blocks * SIDE, LANES), BF16)],
        signal, cot, *copies, rows, cols, hot, half_mask, forward, backward, columns,
        scratch=[
            pltpu.VMEM((ROWS, LANES), F32), pltpu.VMEM((cells, LANES), F32), line, line,
            pltpu.VMEM((96, LANES), F32), pltpu.VMEM((SIDE, LANES), F32), pltpu.VMEM((2 * WROWS, LANES), F32),
        ],
        flops=2 * ROWS * 768 * 128, moved=4 * 2**20,
    )

    if regions == 2:
        sides = [swap(sums, "region", 1)]
    else:
        sides = [shift(sums[SIDE:], "region", 1), shift(sums[:SIDE], "region", -1)]
    pick = call(
        functools.partial(pick_kernel, owners), [((4 * SIDE, owners * SIDE), BF16)], halo_index
    )[0]
    grad_copies = call(grad_copies_kernel, [pair] * 3, grad, moved=2 * 2**20)
    inner = call(
        inner_kernel, [((ROWS, LANES), F32)], *grad_copies, backward, flops=2 * ROWS * 768 * 128, moved=3 * 2**20
    )[0]

    region_ks = [1] + [k for k in steps_of(regions) if k > 1]
    for k in region_ks:
        extra = (own_rows,) if k == region_ks[-1] else ()
        size = (WROWS + SIDE * len(extra), LANES)
        other = swap(sent if k == 1 else message, "region", k)
        message = call(join_kernel, [(size, BF16)], message, other, *extra)[0]
    for step in range(steps - 1):
        size = (2 * message.shape[0] - WROWS, LANES)
        message = call(join_kernel, [(size, BF16)], message, exchange(message, step))[0]
    other = exchange(message, steps - 1)
    scale = 1.0 / math.sqrt(regions * owners * SIDE * SIDE)
    part = call(functools.partial(close_kernel, scale), [((WROWS, LANES), F32)], message, other)[0]
    other_part = swap(part, "region", 1)
    input_grad = call(
        last_kernel, [((SIDE, SIDE * CHANNELS), BF16)], message, other, inner, pick, *sides, moved=2 * 2**20
    )[0]
    weight_grad, bias_grad = call(
        weight_kernel, [((CHANNELS, 9 * CHANNELS), F32), ((1, CHANNELS), F32)], part, other_part
    )
    return input_grad.reshape(1, SIDE, SIDE * CHANNELS), weight_grad.T, bias_grad.reshape(CHANNELS)


def solution(mesh):
    placed = (
        P(("region", "patch"), None, None),
        P(),
        P(),
        P(("region", "patch"), None, None),
        P("region", None),
    )
    return jax.shard_map(
        body,
        mesh=mesh,
        in_specs=placed,
        out_specs=(P(("region", "patch"), None, None), P(), P()),
        check_vma=False,
    )
```

```python
import functools
import math

import jax
import jax.numpy as jnp
from jax import lax
from jax.experimental import pallas as pl
from jax.experimental.pallas import tpu as pltpu
from jax.sharding import PartitionSpec as P

CHANNELS = 64
SIDE = 64
PAIRS = SIDE // 2
LANES = 2 * CHANNELS
ROWS = PAIRS * SIDE
WROWS = 5 * CHANNELS // 2
F32 = jnp.float32
BF16 = jnp.bfloat16


def call(kernel, outs, *args, scratch=(), flops=0, moved=0, space=pltpu.VMEM, limit=48):
    whole = pl.BlockSpec(memory_space=pltpu.VMEM)
    shapes = [jax.ShapeDtypeStruct(s, d) for s, d in outs]
    return pl.pallas_call(
        kernel,
        out_shape=shapes,
        in_specs=[pl.BlockSpec(memory_space=space)] * len(args),
        out_specs=[whole] * len(outs),
        scratch_shapes=list(scratch),
        compiler_params=pltpu.CompilerParams(vmem_limit_bytes=limit * 2**20),
        cost_estimate=pl.CostEstimate(flops=flops, bytes_accessed=moved, transcendentals=0),
    )(*args)


def iota(shape, dim):
    return lax.broadcasted_iota(jnp.int32, shape, dim)


def low(shape):
    return iota(shape, len(shape) - 1) < CHANNELS


def turn(x):
    return pltpu.roll(x, CHANNELS, 1)


def tile(q):
    return pl.ds(pl.multiple_of(q * LANES, LANES), LANES)


def block(q):
    return pl.ds(pl.multiple_of(q * SIDE, SIDE), SIDE)


def dot(a, b, dims=((1,), (0,))):
    return lax.dot_general(a, b, (dims, ((), ())), preferred_element_type=F32)


NT = ((1,), (1,))
TN = ((0,), (0,))


def shifted_copies(load, p0, p1, p2):
    is_low = low((SIDE, LANES))
    row = iota((SIDE, LANES), 0)

    def put(q, before, now):
        v = jnp.where(is_low, before, now)
        p1[block(q), :] = v.astype(BF16)
        p0[block(q), :] = jnp.where(row == 0, 0.0, pltpu.roll(v, 1, 0)).astype(BF16)
        p2[block(q), :] = jnp.where(row == SIDE - 1, 0.0, pltpu.roll(v, SIDE - 1, 0)).astype(BF16)

    def step(q, before):
        now = turn(load(q))
        put(q, before, now)
        return now

    zero = jnp.zeros((SIDE, LANES), F32)
    last = lax.fori_loop(0, PAIRS, step, zero, unroll=2)
    put(PAIRS, last, zero)


def product(p0, p1, p2, w_ref, start, n, dims):
    total = None
    for a, p in enumerate((p0, p1, p2)):
        window = jnp.concatenate([p[pl.ds(start, n), :], p[pl.ds(start + SIDE, n), :]], axis=1)
        term = dot(window, w_ref[a], dims)
        total = term if total is None else total + term
    return total


def rim_kernel(x_hbm, rows_ref, cols_ref, top, bottom, left, right, scr, sems):
    copies = [
        pltpu.make_async_copy(x_hbm.at[0:16, :], top, sems.at[0]),
        pltpu.make_async_copy(x_hbm.at[SIDE - 16 : SIDE, :], bottom, sems.at[1]),
        pltpu.make_async_copy(x_hbm.at[:, 0:LANES], left, sems.at[2]),
        pltpu.make_async_copy(x_hbm.at[:, (PAIRS - 1) * LANES :], right, sems.at[3]),
    ]
    for copy in copies:
        copy.start()
    for copy in copies:
        copy.wait()
    for q in range(PAIRS):
        lanes = slice(q * LANES, (q + 1) * LANES)
        scr[q : q + 1, :] = top[:, lanes].astype(F32)[0:1]
        scr[PAIRS + q : PAIRS + q + 1, :] = bottom[:, lanes].astype(F32)[15:16]
    rows_ref[...] = scr[...].astype(BF16)
    cols_ref[...] = halves(left[...].astype(F32), right[...].astype(F32)).astype(BF16)


def bits_moved(v, pairs):
    result = jnp.zeros_like(v)
    for from_bit, to_bit in pairs:
        result = result | (((v >> from_bit) & 1) << to_bit)
    return result


def plan_kernel(owners, regions, blocks, index_ref, hot_ref, half_ref, scr):
    owner = lax.axis_index("patch")
    region = lax.axis_index("region")
    bits = owners.bit_length() - 1
    index = index_ref[pl.ds(owner, 1), :]
    source, within = index >> 8, index & 255
    relative = (source & (owners - 1)) ^ owner
    even, odd = (bits_moved(relative, slot_bits(owners, core)) for core in range(2))
    slot = jnp.where((region & 1) == 1, odd, even)
    row = within & (SIDE - 1)
    if blocks == 2:
        row = row + jnp.where((((source >> bits) - region + regions) & (regions - 1)) == 1, SIDE, 0)
    is_row = within < 2 * SIDE
    place = jnp.where(is_row, slot * SIDE + (within >> 1), owners * SIDE + row)
    half = jnp.where(is_row, within & 1, (within >> 6) & 1)
    count = index.shape[1]
    scr[...] = jnp.full(scr.shape, -1.0, F32)
    scr[0:1, 0:count] = place.astype(F32)
    scr[1:2, 0:count] = half.astype(F32)
    column = jnp.transpose(scr[...])[0 : hot_ref.shape[0]]
    half_ref[...] = jnp.broadcast_to(column[:, 1:2], half_ref.shape)
    place = column[:, 0:1].astype(jnp.int32)
    for c in range(0, hot_ref.shape[1], LANES):
        n = min(LANES, hot_ref.shape[1] - c)
        hot_ref[:, c : c + n] = (place == iota((hot_ref.shape[0], n), 1) + c).astype(F32).astype(BF16)


def pick_kernel(owners, index_ref, pick_ref):
    owner, region = lax.axis_index("patch"), lax.axis_index("region")
    base = (region * owners + owner) * 4 * SIDE
    want = 2 * iota((SIDE, LANES), 0)
    for t in range(owners // 2):
        pair = []
        for slot in (2 * t, 2 * t + 1):
            even, odd = (
                sum(1 << frm for frm, to in slot_bits(owners, core) if (slot >> to) & 1) for core in range(2)
            )
            line = index_ref[pl.ds(owner ^ jnp.where((region & 1) == 1, odd, even), 1), :]
            pair.append((line[:, 1 : SIDE + 1], line[:, SIDE + 3 : 2 * SIDE + 3]))
        for s in range(2):
            both = jnp.concatenate([pair[0][s], pair[1][s]], axis=1) - base
            for e in range(2):
                hit = (both == want + e).astype(F32).astype(BF16)
                n = 2 * e + s
                pick_ref[n * SIDE : (n + 1) * SIDE, t * LANES : (t + 1) * LANES] = hit


def weights_kernel(wt_ref, w_ref, wb_ref, wc_ref):
    wide = [wt_ref[:, t * LANES : (t + 1) * LANES].astype(F32) for t in range(4)]
    tail = wt_ref[:, 4 * LANES :].astype(F32)
    wide.append(jnp.concatenate([tail, tail], axis=1))

    def at(a, b, high):
        m = 3 * a + b
        v = wide[m // 2]
        return v if m == 8 or (m % 2 == 1) == high else turn(v)

    def pair(a, left, right):
        zero = jnp.zeros((CHANNELS, LANES), F32)
        lo = zero if left is None else at(a, left, False)
        hi = zero if right is None else at(a, right, True)
        return halves(lo, hi).astype(BF16)

    c = CHANNELS
    for a in range(3):
        w_ref[a, 0:c, 0:LANES] = pair(a, 0, 1)
        w_ref[a, 0:c, LANES:] = pair(a, 2, None)
        w_ref[a, c:, 0:LANES] = pair(a, None, 0)
        w_ref[a, c:, LANES:] = pair(a, 1, 2)
        for w, (left, right) in enumerate(((2, None), (1, 2), (0, 1), (None, 0))):
            wb_ref[2 - a, w * c : (w + 1) * c, :] = pair(a, left, right)
        wc_ref[a, 0:c, :] = pair(a, 0, None)
        wc_ref[a, c:, :] = pair(a, None, 2)


def copies_kernel(x_ref, p0, p1, p2):
    shifted_copies(lambda q: x_ref[:, tile(q)].astype(F32), p0, p1, p2)


def signal_kernel(p0, p1, p2, w_ref, bias_ref, s_ref):
    n = 4 * SIDE
    bias = jnp.concatenate([bias_ref[...], bias_ref[...]], axis=1)

    def step(c, carry):
        start = pl.multiple_of(c * n, n)
        s_ref[pl.ds(start, n), :] = product(p0, p1, p2, w_ref, start, n, NT) + bias
        return carry

    lax.fori_loop(0, ROWS // n, step, 0)


def slope_times(signal, upstream):
    sigma = 1.0 / (1.0 + jnp.exp(-signal))
    return upstream * (sigma * (1.0 + signal * (1.0 - sigma)))


def halves(even, odd):
    return jnp.where(low(even.shape), even, odd)


def middle_kernel(
    s_in, cot_ref, p0, p1, p2, rows_ref, cols_ref, hot_ref, half_ref, w_ref, wb_ref, wc_ref,
    g_ref, keep_ref, send_ref, own_ref, s_ref, cell_scr, gt, gb, gc, own_scr, msg,
):
    many = rows_ref.shape[0]
    cells = dot(hot_ref[:, :many], rows_ref[...]) + dot(hot_ref[:, many:], cols_ref[...])
    other = turn(cells)
    upper = half_ref[...] > 0.5
    edge = 2 * SIDE + 4
    as_low = jnp.where(upper, other, cells)
    as_high = jnp.where(upper, cells, other)
    sides = halves(as_low[edge : edge + SIDE], as_high[edge + SIDE : edge + 2 * SIDE])
    odd = iota(cells.shape, 0) % 2 == 1
    cell_scr[...] = jnp.where(odd, as_high, as_low)

    def line_of(start):
        even_cells = cell_scr[pl.ds(start, PAIRS + 1, stride=2), :]
        odd_cells = cell_scr[pl.ds(start + 1, PAIRS + 1, stride=2), :]
        both = halves(even_cells, odd_cells)
        return jnp.concatenate([both[0:PAIRS], both[1 : PAIRS + 1]], axis=1).astype(BF16)

    is_low = low((SIDE, LANES))
    row = iota((SIDE, LANES), 0)
    top = line_of(0)
    bottom = line_of(SIDE + 2)
    s_ref[...] = s_in[...]
    first = pl.ds(0, PAIRS, stride=SIDE)
    final = pl.ds(SIDE - 1, PAIRS, stride=SIDE)
    s_ref[first, :] += dot(top, w_ref[0], NT)
    s_ref[final, :] += dot(bottom, w_ref[2], NT)
    moved = (
        jnp.where(row == 0, 0.0, pltpu.roll(sides, 1, 0)),
        sides,
        jnp.where(row == SIDE - 1, 0.0, pltpu.roll(sides, SIDE - 1, 0)),
    )
    lefts = [jnp.where(is_low, m, 0.0).astype(BF16) for m in moved]
    rights = [jnp.where(is_low, 0.0, m).astype(BF16) for m in moved]
    for a in range(3):
        s_ref[0:SIDE, :] += dot(lefts[a], w_ref[a, :, 0:LANES], NT)
        s_ref[ROWS - SIDE : ROWS, :] += dot(rights[a], w_ref[a, :, LANES:], NT)

    def step(q, carry):
        bias, before = carry
        g = slope_times(s_ref[block(q), :], cot_ref[:, tile(q)].astype(F32)).astype(BF16)
        g_ref[block(q), :] = g
        wide = g.astype(F32)
        now = turn(wide)
        pair = jnp.where(is_low, before, now)
        gt[pl.ds(q, 1), :] = pair[0:1]
        gb[pl.ds(q, 1), :] = pair[SIDE - 1 :]
        s_ref[block(q), :] = wide
        return bias + jnp.sum(wide.reshape(8, 8, LANES), axis=0), now

    zero = jnp.zeros((SIDE, LANES), F32)
    bias, last = lax.fori_loop(0, PAIRS, step, (jnp.zeros((8, LANES), F32), zero), unroll=2)
    pair = jnp.where(is_low, last, 0.0)
    gt[PAIRS : PAIRS + 1, :] = pair[0:1]
    gb[PAIRS : PAIRS + 1, :] = pair[SIDE - 1 :]

    g = g_ref[...]
    g_first = s_ref[first, :].astype(BF16)
    g_final = s_ref[final, :].astype(BF16)
    terms = []
    for a, p in enumerate((p0, p1, p2)):
        for shift in (0, 1):
            t = dot(g, p[shift * SIDE : shift * SIDE + ROWS, :], TN)
            lanes = slice(shift * LANES, (shift + 1) * LANES)
            if a == 0:
                t += dot(g_first, top[:, lanes], TN)
            if a == 2:
                t += dot(g_final, bottom[:, lanes], TN)
            if shift == 0:
                t += dot(g[0:SIDE], lefts[a], TN)
            else:
                t += dot(g[ROWS - SIDE :], rights[a], TN)
            terms.append(t)

    def tap(m, high):
        a, b = m // 3, m % 3
        result = 0.0
        for e in (0, 1):
            w = e + b
            part = terms[2 * a + w // 2][e * CHANNELS : (e + 1) * CHANNELS]
            result = result + (part if (w % 2 == 1) == high else turn(part))
        return result

    total = jnp.sum(bias, axis=0, keepdims=True)
    total = total + turn(total)
    coarse = total.astype(BF16).astype(F32)
    fine = total - coarse
    for t in range(5):
        if t < 4:
            high = tap(2 * t + 1, True)
        else:
            high = jnp.where(row == 0, coarse, jnp.where(row == 1, fine, 0.0))
        msg[t * SIDE : (t + 1) * SIDE, :] = halves(tap(2 * t, False), high)
    core = lax.axis_index("region") & 1
    keep_ref[...] = msg[pl.ds(pl.multiple_of(core * WROWS, WROWS), WROWS), :].astype(BF16)
    send_ref[0:WROWS, :] = msg[pl.ds(pl.multiple_of((1 - core) * WROWS, WROWS), WROWS), :].astype(BF16)

    lines = []
    for src, tap_row in ((gt, 2), (gb, 0)):
        window = jnp.concatenate([src[0:PAIRS, :], src[1 : PAIRS + 1, :]], axis=1).astype(BF16)
        lines.append(dot(window, wb_ref[tap_row]))
    own_scr[pl.ds(0, PAIRS, stride=2), :] = halves(lines[0], turn(lines[1]))
    own_scr[pl.ds(1, PAIRS, stride=2), :] = halves(turn(lines[0]), lines[1])
    own_ref[...] = own_scr[...].astype(BF16)

    gc[...] = jnp.zeros(gc.shape, F32)
    gc[8 : 8 + SIDE, :] = jnp.where(is_low, s_ref[0:SIDE, :], s_ref[ROWS - SIDE : ROWS, :])
    grads = dot(gc[8:88, :].astype(BF16), wc_ref[0])
    grads = grads + dot(gc[7:87, :].astype(BF16), wc_ref[1])
    grads = grads + dot(gc[6:86, :].astype(BF16), wc_ref[2])
    other = turn(grads)
    lefts = halves(grads, other)
    rights = halves(other, grads)
    cell_scr[...] = jnp.zeros(cell_scr.shape, F32)
    for at, src, first_row, n in (
        (0, lefts, 0, 1), (SIDE + 1, rights, 0, 1), (SIDE + 2, lefts, SIDE + 1, 1), (edge - 1, rights, SIDE + 1, 1),
        (edge, lefts, 1, SIDE), (edge + SIDE, rights, 1, SIDE),
    ):
        cell_scr[at : at + n, :] = src[first_row : first_row + n]
    placed = jnp.where(upper == low(cells.shape), 0.0, cell_scr[...]).astype(BF16)
    send_ref[WROWS:, :] = dot(hot_ref[:, many:], placed, TN).astype(BF16)


def grad_copies_kernel(g_ref, p0, p1, p2):
    shifted_copies(lambda q: g_ref[block(q), :].astype(F32), p0, p1, p2)


def inner_kernel(p0, p1, p2, wb_ref, out_ref):
    n = 4 * SIDE

    def step(c, carry):
        start = pl.multiple_of(c * n, n)
        out_ref[pl.ds(start, n), :] = product(p0, p1, p2, wb_ref, start, n, ((1,), (0,)))
        return carry

    lax.fori_loop(0, ROWS // n, step, 0)


def added_weights(mine, other):
    total = mine[0:WROWS, :].astype(F32) + other[0:WROWS, :].astype(F32)
    tail = total[WROWS - SIDE :]
    return total, tail + pltpu.roll(tail, SIDE - 1, 0)


def bias_lanes(shape):
    return jnp.logical_and(jnp.logical_not(low(shape)), (lax.axis_index("region") & 1) == 1)


def join_kernel(mine, other, *rest):
    extra, out = rest[:-1], rest[-1]
    total, whole = added_weights(mine, other)
    out[0 : WROWS - SIDE, :] = total[: WROWS - SIDE].astype(BF16)
    row = iota(whole.shape, 0)
    coarse = whole.astype(BF16).astype(F32)
    fine = pltpu.roll(whole - coarse, 1, 0)
    out[WROWS - SIDE : WROWS, :] = jnp.where(
        bias_lanes(whole.shape),
        jnp.where(row == 0, coarse, jnp.where(row == 1, fine, 0.0)),
        total[WROWS - SIDE :],
    ).astype(BF16)
    n = mine.shape[0] - WROWS
    if n:
        out[WROWS : WROWS + n, :] = mine[WROWS:, :]
        out[WROWS + n :, :] = other[WROWS:, :]
    if extra:
        out[WROWS:, :] = extra[0][...]


def close_kernel(scale, mine, other, out):
    total, whole = added_weights(mine, other)
    out[0 : WROWS - SIDE, :] = total[: WROWS - SIDE] * scale
    out[WROWS - SIDE :, :] = jnp.where(bias_lanes(whole.shape), whole, total[WROWS - SIDE :]) * scale


def weight_kernel(mine, other, wt_ref, bias_ref):
    odd = (lax.axis_index("region") & 1) == 1
    a, b = mine[...], other[...]
    full = jnp.concatenate([jnp.where(odd, b, a), jnp.where(odd, a, b)], axis=0)
    for t in range(4):
        wt_ref[:, t * LANES : (t + 1) * LANES] = full[t * SIDE : (t + 1) * SIDE]
    wt_ref[:, 4 * LANES :] = full[4 * SIDE :, :CHANNELS]
    bias_ref[...] = turn(full[4 * SIDE : 4 * SIDE + 8])[0:1, :CHANNELS]


def last_kernel(mine, other, inner, pick, *rest):
    side_refs, grad_ref = rest[:-1], rest[-1]
    n = mine.shape[0] - WROWS
    got = dot(pick[:, :n], mine[WROWS:, :]) + dot(pick[:, n:], other[WROWS:, :])
    a, b, c, d = (got[i * SIDE : (i + 1) * SIDE] for i in range(4))
    rims = halves(a + turn(b), turn(c) + d)
    sides = side_refs[0][side_refs[0].shape[0] - SIDE :, :].astype(F32)
    for ref in side_refs[1:]:
        sides = sides + ref[...].astype(F32)
    row = iota((SIDE, LANES), 0)
    is_low = low((SIDE, LANES))
    for q in range(PAIRS):
        v = inner[q * SIDE : (q + 1) * SIDE, :]
        v = v + jnp.where(row == 0, rims[q : q + 1], jnp.where(row == SIDE - 1, rims[PAIRS + q : PAIRS + q + 1], 0.0))
        if q == 0:
            v = v + jnp.where(is_low, sides, 0.0)
        if q == PAIRS - 1:
            v = v + jnp.where(is_low, 0.0, sides)
        grad_ref[:, q * LANES : (q + 1) * LANES] = v.astype(BF16)


def swap(x, axis, k):
    n = lax.axis_size(axis)
    return lax.ppermute(x, axis, [(i, i ^ k) for i in range(n)])


def shift(x, axis, by):
    n = lax.axis_size(axis)
    return lax.ppermute(x, axis, [(i, (i + by) % n) for i in range(n)])


def steps_of(n):
    ks = []
    k = n // 2
    while k:
        ks.append(k)
        k //= 2
    return ks


def order_of(owners, core):
    bits = list(range(owners.bit_length() - 1))[::-1]
    return bits if core == 0 else bits[-1:] + bits[:-1]


def slot_bits(owners, core):
    return [(bit, step) for step, bit in enumerate(order_of(owners, core))]


def exchange(x, step):
    regions, owners = lax.axis_size("region"), lax.axis_size("patch")
    pairs = []
    for r in range(regions):
        k = 1 << order_of(owners, r % 2)[step]
        pairs += [(r * owners + i, r * owners + (i ^ k)) for i in range(owners)]
    return lax.ppermute(x, ("region", "patch"), pairs)


def body(fine_input, fine_weight, fine_bias, cotangent, halo_index):
    owners = lax.axis_size("patch")
    regions = lax.axis_size("region")
    steps = owners.bit_length() - 1
    blocks = 1 if regions == 2 else 2
    x = fine_input.reshape(SIDE, SIDE * CHANNELS)
    cot = cotangent.reshape(SIDE, SIDE * CHANNELS)
    pair = ((ROWS + SIDE, LANES), BF16)

    rows, cols = call(
        rim_kernel,
        [((SIDE, LANES), BF16)] * 2,
        x,
        scratch=[
            pltpu.VMEM((16, SIDE * CHANNELS), BF16), pltpu.VMEM((16, SIDE * CHANNELS), BF16),
            pltpu.VMEM((SIDE, LANES), BF16), pltpu.VMEM((SIDE, LANES), BF16),
            pltpu.VMEM((SIDE, LANES), F32), pltpu.SemaphoreType.DMA((4,)),
        ],
        space=pl.ANY,
        limit=60,
    )
    if regions == 2:
        cols = swap(cols, "region", 1)
    else:
        cols = jnp.concatenate([shift(cols, "region", 1), shift(cols, "region", -1)], axis=0)
    count = 272
    both = ((ROWS, LANES), F32)
    work = dict(flops=2 * ROWS * 768 * 128, moved=3 * 2**20)

    other = exchange(rows, 0)
    copies = call(copies_kernel, [pair] * 3, x, moved=2 * 2**20)
    forward, backward, columns = call(
        weights_kernel,
        [((3, LANES, 2 * LANES), BF16), ((3, 2 * LANES, LANES), BF16), ((3, LANES, LANES), BF16)],
        fine_weight.T,
    )
    other, copies, forward = lax.optimization_barrier((other, copies, forward))
    rows = jnp.concatenate([rows, other], axis=0)
    other = exchange(rows, 1)
    signal = call(signal_kernel, [both], *copies, forward, fine_bias.reshape(1, CHANNELS), **work)[0]
    other, signal, index = lax.optimization_barrier((other, signal, halo_index))
    rows = jnp.concatenate([rows, other], axis=0)
    other = exchange(rows, 2)
    hot, half_mask = call(
        functools.partial(plan_kernel, owners, regions, blocks),
        [((count, (owners + blocks) * SIDE), BF16), ((count, LANES), F32)],
        index, scratch=[pltpu.VMEM((8, 384), F32)],
    )
    pick = call(functools.partial(pick_kernel, owners), [((4 * SIDE, owners * SIDE), BF16)], index)[0]
    other, hot, half_mask, pick = lax.optimization_barrier((other, hot, half_mask, pick))
    rows = jnp.concatenate([rows, other], axis=0)
    for step in range(3, steps):
        rows = jnp.concatenate([rows, exchange(rows, step)], axis=0)

    line = pltpu.VMEM((40, LANES), F32)
    grad, message, sent, own_rows = call(
        middle_kernel,
        [((ROWS, LANES), BF16), ((WROWS, LANES), BF16), ((WROWS + blocks * SIDE, LANES), BF16), ((SIDE, LANES), BF16)],
        signal, cot, *copies, rows, cols, hot, half_mask, forward, backward, columns,
        scratch=[
            pltpu.VMEM((ROWS, LANES), F32), pltpu.VMEM((count, LANES), F32), line, line,
            pltpu.VMEM((96, LANES), F32), pltpu.VMEM((SIDE, LANES), F32), pltpu.VMEM((2 * WROWS, LANES), F32),
        ],
        **work,
    )

    if regions > 2:
        upper, lower = sent[WROWS + SIDE :], sent[WROWS : WROWS + SIDE]
        sides = [shift(upper, "region", 1), shift(lower, "region", -1)]
        sent = sent[:WROWS]
    other = swap(sent, "region", 1)
    if regions == 2:
        sides = [other]
    far = [k for k in steps_of(regions) if k > 1]
    for k in [1] + far:
        extra = () if k != ([1] + far)[-1] else (own_rows,)
        size = (WROWS + SIDE * len(extra), LANES)
        message = call(join_kernel, [(size, BF16)], message, other if k == 1 else swap(message, "region", k), *extra)[0]
    beside = grad
    for step in range(steps):
        message, beside = lax.optimization_barrier((message, beside))
        other = exchange(message, step)
        if step == 0:
            beside = call(grad_copies_kernel, [pair] * 3, beside, moved=2 * 2**20)
        if step == 1:
            beside = call(inner_kernel, [both], *beside, backward, **work)[0]
        other, beside = lax.optimization_barrier((other, beside))
        if step < steps - 1:
            size = (2 * message.shape[0] - WROWS, LANES)
            message = call(join_kernel, [(size, BF16)], message, other)[0]
    scale = 1.0 / math.sqrt(regions * owners * SIDE * SIDE)
    part = call(functools.partial(close_kernel, scale), [((WROWS, LANES), F32)], message, other)[0]
    other_part = swap(part, "region", 1)
    input_grad = call(
        last_kernel, [((SIDE, SIDE * CHANNELS), BF16)], message, other, beside, pick, *sides, moved=2 * 2**20
    )[0]
    weight_grad, bias_grad = call(
        weight_kernel, [((CHANNELS, 9 * CHANNELS), F32), ((1, CHANNELS), F32)], part, other_part
    )
    return input_grad.reshape(1, SIDE, SIDE * CHANNELS), weight_grad.T, bias_grad.reshape(CHANNELS)


def solution(mesh):
    placed = (
        P(("region", "patch"), None, None),
        P(),
        P(),
        P(("region", "patch"), None, None),
        P("region", None),
    )
    return jax.shard_map(
        body,
        mesh=mesh,
        in_specs=placed,
        out_specs=(P(("region", "patch"), None, None), P(), P()),
        check_vma=False,
    )
```

```python
import functools
import math

import jax
import jax.numpy as jnp
from jax import lax
from jax.experimental import pallas as pl
from jax.experimental.pallas import tpu as pltpu
from jax.sharding import PartitionSpec as P

CHANNELS = 64
SIDE = 64
PAIRS = SIDE // 2
LANES = 2 * CHANNELS
ROWS = PAIRS * SIDE
WROWS = 5 * CHANNELS // 2
F32 = jnp.float32
BF16 = jnp.bfloat16


def call(kernel, outs, *args, scratch=(), flops=0, moved=0, space=pltpu.VMEM, limit=48):
    whole = pl.BlockSpec(memory_space=pltpu.VMEM)
    shapes = [jax.ShapeDtypeStruct(s, d) for s, d in outs]
    return pl.pallas_call(
        kernel,
        out_shape=shapes,
        in_specs=[pl.BlockSpec(memory_space=space)] * len(args),
        out_specs=[whole] * len(outs),
        scratch_shapes=list(scratch),
        compiler_params=pltpu.CompilerParams(vmem_limit_bytes=limit * 2**20),
        cost_estimate=pl.CostEstimate(flops=flops, bytes_accessed=moved, transcendentals=0),
    )(*args)


def iota(shape, dim):
    return lax.broadcasted_iota(jnp.int32, shape, dim)


def low(shape):
    return iota(shape, len(shape) - 1) < CHANNELS


def turn(x):
    return pltpu.roll(x, CHANNELS, 1)


def tile(q):
    return pl.ds(pl.multiple_of(q * LANES, LANES), LANES)


def block(q):
    return pl.ds(pl.multiple_of(q * SIDE, SIDE), SIDE)


def dot(a, b, dims=((1,), (0,))):
    return lax.dot_general(a, b, (dims, ((), ())), preferred_element_type=F32)


NT = ((1,), (1,))
TN = ((0,), (0,))


def shifted_copies(load, p0, p1, p2):
    is_low = low((SIDE, LANES))
    row = iota((SIDE, LANES), 0)

    def put(q, before, now):
        v = jnp.where(is_low, before, now)
        p1[block(q), :] = v.astype(BF16)
        p0[block(q), :] = jnp.where(row == 0, 0.0, pltpu.roll(v, 1, 0)).astype(BF16)
        p2[block(q), :] = jnp.where(row == SIDE - 1, 0.0, pltpu.roll(v, SIDE - 1, 0)).astype(BF16)

    def step(q, before):
        now = turn(load(q))
        put(q, before, now)
        return now

    zero = jnp.zeros((SIDE, LANES), F32)
    last = lax.fori_loop(0, PAIRS, step, zero, unroll=2)
    put(PAIRS, last, zero)


def product(p0, p1, p2, w_ref, start, n, dims):
    total = None
    for a, p in enumerate((p0, p1, p2)):
        window = jnp.concatenate([p[pl.ds(start, n), :], p[pl.ds(start + SIDE, n), :]], axis=1)
        term = dot(window, w_ref[a], dims)
        total = term if total is None else total + term
    return total


def rim_kernel(x_ref, rows_ref, cols_ref, scr):
    for q in range(PAIRS):
        lanes = slice(q * LANES, (q + 1) * LANES)
        scr[q : q + 1, :] = x_ref[0:16, lanes].astype(F32)[0:1]
        scr[PAIRS + q : PAIRS + q + 1, :] = x_ref[SIDE - 16 : SIDE, lanes].astype(F32)[15:16]
    rows_ref[...] = scr[...].astype(BF16)
    first = x_ref[:, 0:LANES].astype(F32)
    last = x_ref[:, (PAIRS - 1) * LANES :].astype(F32)
    cols_ref[...] = halves(first, last).astype(BF16)


def rows_kernel(mine, other, out):
    n = mine.shape[0]
    out[0:n, :] = mine[...]
    out[n:, :] = other[...]


def bits_moved(v, pairs):
    result = jnp.zeros_like(v)
    for from_bit, to_bit in pairs:
        result = result | (((v >> from_bit) & 1) << to_bit)
    return result


def plan_kernel(owners, regions, blocks, index_ref, hot_ref, half_ref, scr):
    owner = lax.axis_index("patch")
    region = lax.axis_index("region")
    bits = owners.bit_length() - 1
    index = index_ref[pl.ds(owner, 1), :]
    source, within = index >> 8, index & 255
    slot = bits_moved((source & (owners - 1)) ^ owner, slot_bits(owners))
    row = within & (SIDE - 1)
    if blocks == 2:
        row = row + jnp.where((((source >> bits) - region + regions) & (regions - 1)) == 1, SIDE, 0)
    is_row = within < 2 * SIDE
    place = jnp.where(is_row, slot * SIDE + (within >> 1), owners * SIDE + row)
    half = jnp.where(is_row, within & 1, (within >> 6) & 1)
    count = index.shape[1]
    scr[...] = jnp.full(scr.shape, -1.0, F32)
    scr[0:1, 0:count] = place.astype(F32)
    scr[1:2, 0:count] = half.astype(F32)
    column = jnp.transpose(scr[...])[0 : hot_ref.shape[0]]
    half_ref[...] = jnp.broadcast_to(column[:, 1:2], half_ref.shape)
    place = column[:, 0:1].astype(jnp.int32)
    for c in range(0, hot_ref.shape[1], LANES):
        n = min(LANES, hot_ref.shape[1] - c)
        hot_ref[:, c : c + n] = (place == iota((hot_ref.shape[0], n), 1) + c).astype(F32).astype(BF16)


def pick_kernel(owners, index_ref, pick_ref):
    owner, region = lax.axis_index("patch"), lax.axis_index("region")
    base = (region * owners + owner) * 4 * SIDE
    want = 2 * iota((SIDE, LANES), 0)
    for t in range(owners // 2):
        pair = []
        for slot in (2 * t, 2 * t + 1):
            relative = sum(1 << bit for bit, to in slot_bits(owners) if (slot >> to) & 1)
            line = index_ref[pl.ds(owner ^ relative, 1), :]
            pair.append((line[:, 1 : SIDE + 1], line[:, SIDE + 3 : 2 * SIDE + 3]))
        for s in range(2):
            both = jnp.concatenate([pair[0][s], pair[1][s]], axis=1) - base
            for e in range(2):
                hit = (both == want + e).astype(F32).astype(BF16)
                n = 2 * e + s
                pick_ref[n * SIDE : (n + 1) * SIDE, t * LANES : (t + 1) * LANES] = hit


def weights_kernel(wt_ref, w_ref, wb_ref, wc_ref):
    wide = [wt_ref[:, t * LANES : (t + 1) * LANES].astype(F32) for t in range(4)]
    tail = wt_ref[:, 4 * LANES :].astype(F32)
    wide.append(jnp.concatenate([tail, tail], axis=1))

    def at(a, b, high):
        m = 3 * a + b
        v = wide[m // 2]
        return v if m == 8 or (m % 2 == 1) == high else turn(v)

    def pair(a, left, right):
        zero = jnp.zeros((CHANNELS, LANES), F32)
        lo = zero if left is None else at(a, left, False)
        hi = zero if right is None else at(a, right, True)
        return halves(lo, hi).astype(BF16)

    c = CHANNELS
    for a in range(3):
        w_ref[a, 0:c, 0:LANES] = pair(a, 0, 1)
        w_ref[a, 0:c, LANES:] = pair(a, 2, None)
        w_ref[a, c:, 0:LANES] = pair(a, None, 0)
        w_ref[a, c:, LANES:] = pair(a, 1, 2)
        for w, (left, right) in enumerate(((2, None), (1, 2), (0, 1), (None, 0))):
            wb_ref[2 - a, w * c : (w + 1) * c, :] = pair(a, left, right)
        wc_ref[a, 0:c, :] = pair(a, 0, None)
        wc_ref[a, c:, :] = pair(a, None, 2)


def copies_kernel(x_ref, p0, p1, p2):
    shifted_copies(lambda q: x_ref[:, tile(q)].astype(F32), p0, p1, p2)


def signal_kernel(p0, p1, p2, w_ref, bias_ref, s_ref):
    n = 4 * SIDE
    bias = jnp.concatenate([bias_ref[...], bias_ref[...]], axis=1)

    def step(c, carry):
        start = pl.multiple_of(c * n, n)
        s_ref[pl.ds(start, n), :] = product(p0, p1, p2, w_ref, start, n, NT) + bias
        return carry

    lax.fori_loop(0, ROWS // n, step, 0)


def slope_times(signal, upstream):
    sigma = 1.0 / (1.0 + jnp.exp(-signal))
    return upstream * (sigma * (1.0 + signal * (1.0 - sigma)))


def halves(even, odd):
    return jnp.where(low(even.shape), even, odd)


def middle_kernel(
    s_in, cot_ref, p0, p1, p2, rows_a, rows_b, rows_c, rows_d, cols_ref, hot_ref, half_ref, w_ref, wb_ref, wc_ref,
    g_ref, keep_ref, send_ref, own_ref, s_ref, cell_scr, gt, gb, gc, own_scr, msg,
):
    n = rows_a.shape[0]
    many = 4 * n
    cells = dot(hot_ref[:, many:], cols_ref[...])
    for i, ref in enumerate((rows_a, rows_b, rows_c, rows_d)):
        cells = cells + dot(hot_ref[:, i * n : (i + 1) * n], ref[...])
    other = turn(cells)
    upper = half_ref[...] > 0.5
    edge = 2 * SIDE + 4
    as_low = jnp.where(upper, other, cells)
    as_high = jnp.where(upper, cells, other)
    sides = halves(as_low[edge : edge + SIDE], as_high[edge + SIDE : edge + 2 * SIDE])
    odd = iota(cells.shape, 0) % 2 == 1
    cell_scr[...] = jnp.where(odd, as_high, as_low)

    def line_of(start):
        even_cells = cell_scr[pl.ds(start, PAIRS + 1, stride=2), :]
        odd_cells = cell_scr[pl.ds(start + 1, PAIRS + 1, stride=2), :]
        both = halves(even_cells, odd_cells)
        return jnp.concatenate([both[0:PAIRS], both[1 : PAIRS + 1]], axis=1).astype(BF16)

    is_low = low((SIDE, LANES))
    row = iota((SIDE, LANES), 0)
    top = line_of(0)
    bottom = line_of(SIDE + 2)
    s_ref[...] = s_in[...]
    first = pl.ds(0, PAIRS, stride=SIDE)
    final = pl.ds(SIDE - 1, PAIRS, stride=SIDE)
    s_ref[first, :] += dot(top, w_ref[0], NT)
    s_ref[final, :] += dot(bottom, w_ref[2], NT)
    moved = (
        jnp.where(row == 0, 0.0, pltpu.roll(sides, 1, 0)),
        sides,
        jnp.where(row == SIDE - 1, 0.0, pltpu.roll(sides, SIDE - 1, 0)),
    )
    lefts = [jnp.where(is_low, m, 0.0).astype(BF16) for m in moved]
    rights = [jnp.where(is_low, 0.0, m).astype(BF16) for m in moved]
    for a in range(3):
        s_ref[0:SIDE, :] += dot(lefts[a], w_ref[a, :, 0:LANES], NT)
        s_ref[ROWS - SIDE : ROWS, :] += dot(rights[a], w_ref[a, :, LANES:], NT)

    def step(q, carry):
        bias, before = carry
        g = slope_times(s_ref[block(q), :], cot_ref[:, tile(q)].astype(F32)).astype(BF16)
        g_ref[block(q), :] = g
        wide = g.astype(F32)
        now = turn(wide)
        pair = jnp.where(is_low, before, now)
        gt[pl.ds(q, 1), :] = pair[0:1]
        gb[pl.ds(q, 1), :] = pair[SIDE - 1 :]
        s_ref[block(q), :] = wide
        return bias + jnp.sum(wide.reshape(8, 8, LANES), axis=0), now

    zero = jnp.zeros((SIDE, LANES), F32)
    bias, last = lax.fori_loop(0, PAIRS, step, (jnp.zeros((8, LANES), F32), zero), unroll=2)
    pair = jnp.where(is_low, last, 0.0)
    gt[PAIRS : PAIRS + 1, :] = pair[0:1]
    gb[PAIRS : PAIRS + 1, :] = pair[SIDE - 1 :]

    g = g_ref[...]
    g_first = s_ref[first, :].astype(BF16)
    g_final = s_ref[final, :].astype(BF16)
    terms = []
    for a, p in enumerate((p0, p1, p2)):
        for shift in (0, 1):
            t = dot(g, p[shift * SIDE : shift * SIDE + ROWS, :], TN)
            lanes = slice(shift * LANES, (shift + 1) * LANES)
            if a == 0:
                t += dot(g_first, top[:, lanes], TN)
            if a == 2:
                t += dot(g_final, bottom[:, lanes], TN)
            if shift == 0:
                t += dot(g[0:SIDE], lefts[a], TN)
            else:
                t += dot(g[ROWS - SIDE :], rights[a], TN)
            terms.append(t)

    def tap(m, high):
        a, b = m // 3, m % 3
        result = 0.0
        for e in (0, 1):
            w = e + b
            part = terms[2 * a + w // 2][e * CHANNELS : (e + 1) * CHANNELS]
            result = result + (part if (w % 2 == 1) == high else turn(part))
        return result

    total = jnp.sum(bias, axis=0, keepdims=True)
    total = total + turn(total)
    coarse = total.astype(BF16).astype(F32)
    fine = total - coarse
    for t in range(5):
        if t < 4:
            high = tap(2 * t + 1, True)
        else:
            high = jnp.where(row == 0, coarse, jnp.where(row == 1, fine, 0.0))
        msg[t * SIDE : (t + 1) * SIDE, :] = halves(tap(2 * t, False), high)
    core = lax.axis_index("region") & 1
    keep_ref[...] = msg[pl.ds(pl.multiple_of(core * WROWS, WROWS), WROWS), :].astype(BF16)
    send_ref[0:WROWS, :] = msg[pl.ds(pl.multiple_of((1 - core) * WROWS, WROWS), WROWS), :].astype(BF16)

    lines = []
    for src, tap_row in ((gt, 2), (gb, 0)):
        window = jnp.concatenate([src[0:PAIRS, :], src[1 : PAIRS + 1, :]], axis=1).astype(BF16)
        lines.append(dot(window, wb_ref[tap_row]))
    own_scr[pl.ds(0, PAIRS, stride=2), :] = halves(lines[0], turn(lines[1]))
    own_scr[pl.ds(1, PAIRS, stride=2), :] = halves(turn(lines[0]), lines[1])
    own_ref[...] = own_scr[...].astype(BF16)

    gc[...] = jnp.zeros(gc.shape, F32)
    gc[8 : 8 + SIDE, :] = jnp.where(is_low, s_ref[0:SIDE, :], s_ref[ROWS - SIDE : ROWS, :])
    grads = dot(gc[8:88, :].astype(BF16), wc_ref[0])
    grads = grads + dot(gc[7:87, :].astype(BF16), wc_ref[1])
    grads = grads + dot(gc[6:86, :].astype(BF16), wc_ref[2])
    other = turn(grads)
    lefts = halves(grads, other)
    rights = halves(other, grads)
    cell_scr[...] = jnp.zeros(cell_scr.shape, F32)
    for at, src, first_row, n in (
        (0, lefts, 0, 1), (SIDE + 1, rights, 0, 1), (SIDE + 2, lefts, SIDE + 1, 1), (edge - 1, rights, SIDE + 1, 1),
        (edge, lefts, 1, SIDE), (edge + SIDE, rights, 1, SIDE),
    ):
        cell_scr[at : at + n, :] = src[first_row : first_row + n]
    placed = jnp.where(upper == low(cells.shape), 0.0, cell_scr[...]).astype(BF16)
    send_ref[WROWS:, :] = dot(hot_ref[:, many:], placed, TN).astype(BF16)


def grad_copies_kernel(g_ref, p0, p1, p2):
    shifted_copies(lambda q: g_ref[block(q), :].astype(F32), p0, p1, p2)


def inner_kernel(p0, p1, p2, wb_ref, out_ref):
    n = 4 * SIDE

    def step(c, carry):
        start = pl.multiple_of(c * n, n)
        out_ref[pl.ds(start, n), :] = product(p0, p1, p2, wb_ref, start, n, ((1,), (0,)))
        return carry

    lax.fori_loop(0, ROWS // n, step, 0)


def added_weights(mine, other):
    total = mine[0:WROWS, :].astype(F32) + other[0:WROWS, :].astype(F32)
    tail = total[WROWS - SIDE :]
    return total, tail + pltpu.roll(tail, SIDE - 1, 0)


def bias_lanes(shape):
    return jnp.logical_and(jnp.logical_not(low(shape)), (lax.axis_index("region") & 1) == 1)


def join_kernel(mine, other, *rest):
    extra, out = rest[:-1], rest[-1]
    total, whole = added_weights(mine, other)
    out[0 : WROWS - SIDE, :] = total[: WROWS - SIDE].astype(BF16)
    row = iota(whole.shape, 0)
    coarse = whole.astype(BF16).astype(F32)
    fine = pltpu.roll(whole - coarse, 1, 0)
    out[WROWS - SIDE : WROWS, :] = jnp.where(
        bias_lanes(whole.shape),
        jnp.where(row == 0, coarse, jnp.where(row == 1, fine, 0.0)),
        total[WROWS - SIDE :],
    ).astype(BF16)
    n = mine.shape[0] - WROWS
    if n:
        out[WROWS : WROWS + n, :] = mine[WROWS:, :]
        out[WROWS + n :, :] = other[WROWS:, :]
    if extra:
        out[WROWS:, :] = extra[0][...]


def close_kernel(scale, a, b, c, d, out):
    left, _ = added_weights(a, b)
    right, _ = added_weights(c, d)
    total = left + right
    tail = total[WROWS - SIDE :]
    whole = tail + pltpu.roll(tail, SIDE - 1, 0)
    out[0 : WROWS - SIDE, :] = total[: WROWS - SIDE] * scale
    out[WROWS - SIDE :, :] = jnp.where(bias_lanes(whole.shape), whole, total[WROWS - SIDE :]) * scale


def weight_kernel(mine, other, wt_ref, bias_ref):
    odd = (lax.axis_index("region") & 1) == 1
    a, b = mine[...], other[...]
    full = jnp.concatenate([jnp.where(odd, b, a), jnp.where(odd, a, b)], axis=0)
    for t in range(4):
        wt_ref[:, t * LANES : (t + 1) * LANES] = full[t * SIDE : (t + 1) * SIDE]
    wt_ref[:, 4 * LANES :] = full[4 * SIDE :, :CHANNELS]
    bias_ref[...] = turn(full[4 * SIDE : 4 * SIDE + 8])[0:1, :CHANNELS]


def last_kernel(row_a, row_b, row_c, row_d, inner, pick, *rest):
    side_refs, grad_ref = rest[:-1], rest[-1]
    n = row_a.shape[0] - WROWS
    got = 0.0
    for i, ref in enumerate((row_a, row_b, row_c, row_d)):
        got = got + dot(pick[:, i * n : (i + 1) * n], ref[WROWS:, :])
    a, b, c, d = (got[i * SIDE : (i + 1) * SIDE] for i in range(4))
    rims = halves(a + turn(b), turn(c) + d)
    sides = side_refs[0][side_refs[0].shape[0] - SIDE :, :].astype(F32)
    for ref in side_refs[1:]:
        sides = sides + ref[...].astype(F32)
    row = iota((SIDE, LANES), 0)
    is_low = low((SIDE, LANES))
    for q in range(PAIRS):
        v = inner[q * SIDE : (q + 1) * SIDE, :]
        v = v + jnp.where(row == 0, rims[q : q + 1], jnp.where(row == SIDE - 1, rims[PAIRS + q : PAIRS + q + 1], 0.0))
        if q == 0:
            v = v + jnp.where(is_low, sides, 0.0)
        if q == PAIRS - 1:
            v = v + jnp.where(is_low, 0.0, sides)
        grad_ref[:, q * LANES : (q + 1) * LANES] = v.astype(BF16)


def swap(x, axis, k):
    n = lax.axis_size(axis)
    return lax.ppermute(x, axis, [(i, i ^ k) for i in range(n)])


def shift(x, axis, by):
    n = lax.axis_size(axis)
    return lax.ppermute(x, axis, [(i, (i + by) % n) for i in range(n)])


def steps_of(n):
    ks = []
    k = n // 2
    while k:
        ks.append(k)
        k //= 2
    return ks


def slot_bits(owners):
    high = range(2, owners.bit_length() - 1)
    count = len(high)
    return [(bit, step) for step, bit in enumerate(high)] + [(0, count), (1, count + 1)]


def exchange(x, k):
    return swap(x, "patch", k)


def three_partners(x):
    got = {k: exchange(x, k) for k in (3, 2, 1)}
    return [got[k] for k in (1, 2, 3)]


def body(fine_input, fine_weight, fine_bias, cotangent, halo_index):
    owners = lax.axis_size("patch")
    regions = lax.axis_size("region")
    high = [1 << bit for bit in range(2, owners.bit_length() - 1)]
    blocks = 1 if regions == 2 else 2
    x = fine_input.reshape(SIDE, SIDE * CHANNELS)
    cot = cotangent.reshape(SIDE, SIDE * CHANNELS)
    pair = ((ROWS + SIDE, LANES), BF16)

    rows, cols = call(rim_kernel, [((SIDE, LANES), BF16)] * 2, x, scratch=[pltpu.VMEM((SIDE, LANES), F32)])
    if regions == 2:
        cols = swap(cols, "region", 1)
    else:
        cols = jnp.concatenate([shift(cols, "region", 1), shift(cols, "region", -1)], axis=0)
    count = 272
    both = ((ROWS, LANES), F32)
    work = dict(flops=2 * ROWS * 768 * 128, moved=3 * 2**20)

    def joined(rows, other):
        return call(rows_kernel, [((2 * rows.shape[0], LANES), BF16)], rows, other)[0]

    other = exchange(rows, high[0])
    copies = call(copies_kernel, [pair] * 3, x, moved=2 * 2**20)
    forward, backward, columns = call(
        weights_kernel,
        [((3, LANES, 2 * LANES), BF16), ((3, 2 * LANES, LANES), BF16), ((3, LANES, LANES), BF16)],
        fine_weight.T,
    )
    other, copies, forward = lax.optimization_barrier((other, copies, forward))
    rows = joined(rows, other)
    other = exchange(rows, high[1])
    signal = call(signal_kernel, [both], *copies, forward, fine_bias.reshape(1, CHANNELS), **work)[0]
    other, signal, index = lax.optimization_barrier((other, signal, halo_index))
    rows = joined(rows, other)
    for k in high[2:]:
        rows = joined(rows, exchange(rows, k))
    others = three_partners(rows)
    hot, half_mask = call(
        functools.partial(plan_kernel, owners, regions, blocks),
        [((count, (owners + blocks) * SIDE), BF16), ((count, LANES), F32)],
        index, scratch=[pltpu.VMEM((8, 384), F32)],
    )
    pick = call(functools.partial(pick_kernel, owners), [((4 * SIDE, owners * SIDE), BF16)], index)[0]
    others, hot, half_mask, pick = lax.optimization_barrier((others, hot, half_mask, pick))

    line = pltpu.VMEM((40, LANES), F32)
    grad, message, sent, own_rows = call(
        middle_kernel,
        [((ROWS, LANES), BF16), ((WROWS, LANES), BF16), ((WROWS + blocks * SIDE, LANES), BF16), ((SIDE, LANES), BF16)],
        signal, cot, *copies, rows, *others, cols, hot, half_mask, forward, backward, columns,
        scratch=[
            pltpu.VMEM((ROWS, LANES), F32), pltpu.VMEM((count, LANES), F32), line, line,
            pltpu.VMEM((96, LANES), F32), pltpu.VMEM((SIDE, LANES), F32), pltpu.VMEM((2 * WROWS, LANES), F32),
        ],
        **work,
    )

    if regions > 2:
        upper, lower = sent[WROWS + SIDE :], sent[WROWS : WROWS + SIDE]
        sides = [shift(upper, "region", 1), shift(lower, "region", -1)]
        sent = sent[:WROWS]
    other = swap(sent, "region", 1)
    if regions == 2:
        sides = [other]
    far = [k for k in steps_of(regions) if k > 1]
    for k in [1] + far:
        extra = () if k != ([1] + far)[-1] else (own_rows,)
        size = (WROWS + SIDE * len(extra), LANES)
        message = call(join_kernel, [(size, BF16)], message, other if k == 1 else swap(message, "region", k), *extra)[0]
    beside = grad
    for step, k in enumerate(high):
        message, beside = lax.optimization_barrier((message, beside))
        other = exchange(message, k)
        if step == 1:
            beside = call(grad_copies_kernel, [pair] * 3, beside, moved=2 * 2**20)
        other, beside = lax.optimization_barrier((other, beside))
        size = (2 * message.shape[0] - WROWS, LANES)
        message = call(join_kernel, [(size, BF16)], message, other)[0]
    message, beside = lax.optimization_barrier((message, beside))
    others = three_partners(message)
    beside = call(inner_kernel, [both], *beside, backward, **work)[0]
    others, beside = lax.optimization_barrier((others, beside))
    scale = 1.0 / math.sqrt(regions * owners * SIDE * SIDE)
    part = call(functools.partial(close_kernel, scale), [((WROWS, LANES), F32)], message, *others)[0]
    other_part = swap(part, "region", 1)
    input_grad = call(
        last_kernel, [((SIDE, SIDE * CHANNELS), BF16)], message, *others, beside, pick, *sides, moved=2 * 2**20
    )[0]
    weight_grad, bias_grad = call(
        weight_kernel, [((CHANNELS, 9 * CHANNELS), F32), ((1, CHANNELS), F32)], part, other_part
    )
    return input_grad.reshape(1, SIDE, SIDE * CHANNELS), weight_grad.T, bias_grad.reshape(CHANNELS)


def solution(mesh):
    placed = (
        P(("region", "patch"), None, None),
        P(),
        P(),
        P(("region", "patch"), None, None),
        P("region", None),
    )
    return jax.shard_map(
        body,
        mesh=mesh,
        in_specs=placed,
        out_specs=(P(("region", "patch"), None, None), P(), P()),
        check_vma=False,
    )
```

```python
import functools
import math

import jax
import jax.numpy as jnp
from jax import lax
from jax.experimental import pallas as pl
from jax.experimental.pallas import tpu as pltpu
from jax.sharding import PartitionSpec as P

CHANNELS = 64
SIDE = 64
PAIRS = SIDE // 2
LANES = 2 * CHANNELS
ROWS = PAIRS * SIDE
WROWS = 5 * CHANNELS // 2
F32 = jnp.float32
BF16 = jnp.bfloat16


def call(kernel, outs, *args, scratch=(), flops=0, moved=0, space=pltpu.VMEM, limit=48):
    whole = pl.BlockSpec(memory_space=pltpu.VMEM)
    shapes = [jax.ShapeDtypeStruct(s, d) for s, d in outs]
    return pl.pallas_call(
        kernel,
        out_shape=shapes,
        in_specs=[pl.BlockSpec(memory_space=space)] * len(args),
        out_specs=[whole] * len(outs),
        scratch_shapes=list(scratch),
        compiler_params=pltpu.CompilerParams(vmem_limit_bytes=limit * 2**20),
        cost_estimate=pl.CostEstimate(flops=flops, bytes_accessed=moved, transcendentals=0),
    )(*args)


def iota(shape, dim):
    return lax.broadcasted_iota(jnp.int32, shape, dim)


def low(shape):
    return iota(shape, len(shape) - 1) < CHANNELS


def turn(x):
    return pltpu.roll(x, CHANNELS, 1)


def tile(q):
    return pl.ds(pl.multiple_of(q * LANES, LANES), LANES)


def block(q):
    return pl.ds(pl.multiple_of(q * SIDE, SIDE), SIDE)


def dot(a, b, dims=((1,), (0,))):
    return lax.dot_general(a, b, (dims, ((), ())), preferred_element_type=F32)


NT = ((1,), (1,))
TN = ((0,), (0,))


def shifted_copies(load, p0, p1, p2, lines=None):
    is_low = low((SIDE, LANES))
    row = iota((SIDE, LANES), 0)

    def put(q, before, now):
        v = jnp.where(is_low, before, now)
        p1[block(q), :] = v.astype(BF16)
        if lines is not None:
            for i, r in enumerate((0, 1, SIDE - 2, SIDE - 1)):
                lines[i, pl.ds(q, 1), :] = v[r : r + 1]
        p0[block(q), :] = jnp.where(row == 0, 0.0, pltpu.roll(v, 1, 0)).astype(BF16)
        p2[block(q), :] = jnp.where(row == SIDE - 1, 0.0, pltpu.roll(v, SIDE - 1, 0)).astype(BF16)

    def step(q, before):
        now = turn(load(q))
        put(q, before, now)
        return now

    zero = jnp.zeros((SIDE, LANES), F32)
    last = lax.fori_loop(0, PAIRS, step, zero, unroll=2)
    put(PAIRS, last, zero)


def product(p0, p1, p2, w_ref, start, n, dims):
    total = None
    for a, p in enumerate((p0, p1, p2)):
        window = jnp.concatenate([p[pl.ds(start, n), :], p[pl.ds(start + SIDE, n), :]], axis=1)
        term = dot(window, w_ref[a], dims)
        total = term if total is None else total + term
    return total


def rim_kernel(x_ref, rows_ref, cols_ref, scr):
    for q in range(PAIRS):
        lanes = slice(q * LANES, (q + 1) * LANES)
        scr[q : q + 1, :] = x_ref[0:16, lanes].astype(F32)[0:1]
        scr[PAIRS + q : PAIRS + q + 1, :] = x_ref[SIDE - 16 : SIDE, lanes].astype(F32)[15:16]
    rows_ref[...] = scr[...].astype(BF16)
    first = x_ref[:, 0:LANES].astype(F32)
    last = x_ref[:, (PAIRS - 1) * LANES :].astype(F32)
    cols_ref[...] = halves(first, last).astype(BF16)


def rows_kernel(mine, other, out):
    n = mine.shape[0]
    out[0:n, :] = mine[...]
    out[n:, :] = other[...]


def bits_moved(v, pairs):
    result = jnp.zeros_like(v)
    for from_bit, to_bit in pairs:
        result = result | (((v >> from_bit) & 1) << to_bit)
    return result


def plan_kernel(owners, regions, blocks, index_ref, hot_ref, half_ref, scr):
    owner = lax.axis_index("patch")
    region = lax.axis_index("region")
    bits = owners.bit_length() - 1
    index = index_ref[pl.ds(owner, 1), :]
    source, within = index >> 8, index & 255
    slot = bits_moved((source & (owners - 1)) ^ owner, slot_bits(owners))
    row = within & (SIDE - 1)
    if blocks == 2:
        row = row + jnp.where((((source >> bits) - region + regions) & (regions - 1)) == 1, SIDE, 0)
    is_row = within < 2 * SIDE
    place = jnp.where(is_row, slot * SIDE + (within >> 1), owners * SIDE + row)
    half = jnp.where(is_row, within & 1, (within >> 6) & 1)
    count = index.shape[1]
    scr[...] = jnp.full(scr.shape, -1.0, F32)
    scr[0:1, 0:count] = place.astype(F32)
    scr[1:2, 0:count] = half.astype(F32)
    column = jnp.transpose(scr[...])[0 : hot_ref.shape[0]]
    half_ref[...] = jnp.broadcast_to(column[:, 1:2], half_ref.shape)
    place = column[:, 0:1].astype(jnp.int32)
    for c in range(0, hot_ref.shape[1], LANES):
        n = min(LANES, hot_ref.shape[1] - c)
        hot_ref[:, c : c + n] = (place == iota((hot_ref.shape[0], n), 1) + c).astype(F32).astype(BF16)


def pick_kernel(owners, index_ref, pick_ref):
    owner, region = lax.axis_index("patch"), lax.axis_index("region")
    base = (region * owners + owner) * 4 * SIDE
    want = 2 * iota((SIDE, LANES), 0)
    for t in range(owners // 2):
        pair = []
        for slot in (2 * t, 2 * t + 1):
            relative = sum(1 << bit for bit, to in slot_bits(owners) if (slot >> to) & 1)
            line = index_ref[pl.ds(owner ^ relative, 1), :]
            pair.append((line[:, 1 : SIDE + 1], line[:, SIDE + 3 : 2 * SIDE + 3]))
        for s in range(2):
            both = jnp.concatenate([pair[0][s], pair[1][s]], axis=1) - base
            for e in range(2):
                hit = (both == want + e).astype(F32).astype(BF16)
                n = 2 * e + s
                pick_ref[n * SIDE : (n + 1) * SIDE, t * LANES : (t + 1) * LANES] = hit


def weights_kernel(wt_ref, w_ref, wb_ref, wc_ref):
    wide = [wt_ref[:, t * LANES : (t + 1) * LANES].astype(F32) for t in range(4)]
    tail = wt_ref[:, 4 * LANES :].astype(F32)
    wide.append(jnp.concatenate([tail, tail], axis=1))

    def at(a, b, high):
        m = 3 * a + b
        v = wide[m // 2]
        return v if m == 8 or (m % 2 == 1) == high else turn(v)

    def pair(a, left, right):
        zero = jnp.zeros((CHANNELS, LANES), F32)
        lo = zero if left is None else at(a, left, False)
        hi = zero if right is None else at(a, right, True)
        return halves(lo, hi).astype(BF16)

    c = CHANNELS
    for a in range(3):
        w_ref[a, 0:c, 0:LANES] = pair(a, 0, 1)
        w_ref[a, 0:c, LANES:] = pair(a, 2, None)
        w_ref[a, c:, 0:LANES] = pair(a, None, 0)
        w_ref[a, c:, LANES:] = pair(a, 1, 2)
        for w, (left, right) in enumerate(((2, None), (1, 2), (0, 1), (None, 0))):
            wb_ref[2 - a, w * c : (w + 1) * c, :] = pair(a, left, right)
        wc_ref[a, 0:c, :] = pair(a, 0, None)
        wc_ref[a, c:, :] = pair(a, None, 2)


def copies_kernel(x_ref, p0, p1, p2, lines):
    shifted_copies(lambda q: x_ref[:, tile(q)].astype(F32), p0, p1, p2, lines)


def signal_kernel(p0, p1, p2, w_ref, bias_ref, s_ref):
    n = 4 * SIDE
    bias = jnp.concatenate([bias_ref[...], bias_ref[...]], axis=1)

    def step(c, carry):
        start = pl.multiple_of(c * n, n)
        s_ref[pl.ds(start, n), :] = product(p0, p1, p2, w_ref, start, n, NT) + bias
        return carry

    lax.fori_loop(0, ROWS // n, step, 0)


def slope_times(signal, upstream):
    sigma = 1.0 / (1.0 + jnp.exp(-signal))
    return upstream * (sigma * (1.0 + signal * (1.0 - sigma)))


def halves(even, odd):
    return jnp.where(low(even.shape), even, odd)


def inside_kernel(s_ref, cot_ref, p0, p1, p2, g_ref, terms_ref, bias_ref, cot_lines):
    row = iota((SIDE, LANES), 0)
    border = jnp.logical_or(row == 0, row == SIDE - 1)

    def step(q, bias):
        upstream = cot_ref[:, tile(q)].astype(F32)
        g = jnp.where(border, 0.0, slope_times(s_ref[block(q), :], upstream)).astype(BF16)
        g_ref[block(q), :] = g
        cot_lines[pl.ds(q, 1), :] = upstream[0:1]
        cot_lines[pl.ds(PAIRS + q, 1), :] = upstream[SIDE - 1 :]
        return bias + jnp.sum(g.astype(F32).reshape(8, 8, LANES), axis=0)

    cot_lines[...] = jnp.zeros(cot_lines.shape, F32)
    bias_ref[...] = lax.fori_loop(1, PAIRS - 1, step, jnp.zeros((8, LANES), F32), unroll=2)
    g_ref[0:SIDE, :] = jnp.zeros((SIDE, LANES), BF16)
    g_ref[ROWS - SIDE :, :] = jnp.zeros((SIDE, LANES), BF16)
    g = g_ref[SIDE : ROWS - SIDE, :]
    for a, p in enumerate((p0, p1, p2)):
        for shift in (0, 1):
            start = (1 + shift) * SIDE
            terms_ref[a, :, shift * LANES : (shift + 1) * LANES] = dot(g, p[start : start + ROWS - 2 * SIDE, :], TN)


def middle_kernel(
    s_ref, cot_ref, p0, p1, p2, lines, terms_ref, bias_ref, cot_lines, rows_a, rows_b, rows_c, rows_d, cols_ref,
    hot_ref, half_ref, w_ref, wb_ref, wc_ref,
    g_lines, g_sides, keep_ref, send_ref, own_ref, cell_scr, gt, gb, gc, own_scr, msg,
):
    n = rows_a.shape[0]
    many = 4 * n
    cells = dot(hot_ref[:, many:], cols_ref[...])
    for i, ref in enumerate((rows_a, rows_b, rows_c, rows_d)):
        cells = cells + dot(hot_ref[:, i * n : (i + 1) * n], ref[...])
    other = turn(cells)
    upper = half_ref[...] > 0.5
    edge = 2 * SIDE + 4
    as_low = jnp.where(upper, other, cells)
    as_high = jnp.where(upper, cells, other)
    sides = halves(as_low[edge : edge + SIDE], as_high[edge + SIDE : edge + 2 * SIDE])
    odd = iota(cells.shape, 0) % 2 == 1
    cell_scr[...] = jnp.where(odd, as_high, as_low)

    def windows(both):
        return jnp.concatenate([both[0:PAIRS], both[1 : PAIRS + 1]], axis=1)

    def line_of(start):
        even_cells = cell_scr[pl.ds(start, PAIRS + 1, stride=2), :]
        odd_cells = cell_scr[pl.ds(start + 1, PAIRS + 1, stride=2), :]
        return windows(halves(even_cells, odd_cells))

    is_low = low((SIDE, LANES))
    row = iota((SIDE, LANES), 0)
    top = line_of(0)
    bottom = line_of(SIDE + 2)
    moved = (
        jnp.where(row == 0, 0.0, pltpu.roll(sides, 1, 0)),
        sides,
        jnp.where(row == SIDE - 1, 0.0, pltpu.roll(sides, SIDE - 1, 0)),
    )
    lefts = [jnp.where(is_low, m, 0.0) for m in moved]
    rights = [jnp.where(is_low, 0.0, m) for m in moved]
    top_signal = dot(top.astype(BF16), w_ref[0], NT)
    bottom_signal = dot(bottom.astype(BF16), w_ref[2], NT)

    def side_grad(q, columns, lanes):
        signal = s_ref[q * SIDE : (q + 1) * SIDE, :]
        for a in range(3):
            signal = signal + dot(columns[a].astype(BF16), w_ref[a, :, lanes], NT)
        signal = signal + jnp.where(row == 0, top_signal[q : q + 1], 0.0)
        signal = signal + jnp.where(row == SIDE - 1, bottom_signal[q : q + 1], 0.0)
        upstream = cot_ref[:, q * LANES : (q + 1) * LANES].astype(F32)
        return slope_times(signal, upstream).astype(BF16).astype(F32)

    end = PAIRS - 1
    g_left = side_grad(0, lefts, slice(0, LANES))
    g_right = side_grad(end, rights, slice(LANES, 2 * LANES))
    pair = iota((PAIRS, LANES), 0)
    ends = jnp.logical_or(pair == 0, pair == end)

    def line_grad(first_row, halo_signal):
        signal = s_ref[pl.ds(first_row, PAIRS, stride=SIDE), :] + halo_signal
        upstream = cot_lines[0:PAIRS, :] if first_row == 0 else cot_lines[PAIRS:, :]
        g = jnp.where(ends, 0.0, slope_times(signal, upstream)).astype(BF16).astype(F32)
        r = slice(first_row, first_row + 1)
        return g, jnp.where(pair == 0, g_left[r], jnp.where(pair == end, g_right[r], g))

    inner_top, all_top = line_grad(0, top_signal)
    inner_bottom, all_bottom = line_grad(SIDE - 1, bottom_signal)
    g_lines[0:PAIRS, :] = all_top
    g_lines[PAIRS:, :] = all_bottom
    g_sides[0:SIDE, :] = g_left.astype(BF16)
    g_sides[SIDE:, :] = g_right.astype(BF16)
    border = jnp.concatenate([inner_top, inner_bottom, g_left, g_right], axis=0)
    bias = jnp.sum(bias_ref[...], axis=0, keepdims=True) + jnp.sum(border, axis=0, keepdims=True)
    border = border.astype(BF16)
    kept = [windows(lines[i]) for i in range(4)]
    none = jnp.zeros((SIDE, LANES), F32)
    wide_row = iota((SIDE, 2 * LANES), 0)

    def side_window(a, p, q, columns):
        parts = [p[(q + i) * SIDE : (q + i + 1) * SIDE, :].astype(F32) for i in range(2)]
        window = jnp.concatenate(parts, axis=1) + columns
        if a == 0:
            window = window + jnp.where(wide_row == 0, top[q : q + 1], 0.0)
        if a == 2:
            window = window + jnp.where(wide_row == SIDE - 1, bottom[q : q + 1], 0.0)
        return window

    terms = []
    over = (top, kept[0], kept[1])
    under = (kept[2], kept[3], bottom)
    for a, p in enumerate((p0, p1, p2)):
        window = jnp.concatenate(
            [
                over[a],
                under[a],
                side_window(a, p, 0, jnp.concatenate([lefts[a], none], axis=1)),
                side_window(a, p, end, jnp.concatenate([none, rights[a]], axis=1)),
            ],
            axis=0,
        ).astype(BF16)
        t = terms_ref[a] + dot(border, window, TN)
        terms += [t[:, :LANES], t[:, LANES:]]
    for scr, line in ((gt, all_top), (gb, all_bottom)):
        turned = turn(line)
        scr[...] = jnp.zeros(scr.shape, F32)
        scr[1 : PAIRS + 1, :] = jnp.where(low(line.shape), turned, 0.0)
        scr[0:PAIRS, :] += jnp.where(low(line.shape), 0.0, turned)

    def tap(m, high):
        a, b = m // 3, m % 3
        result = 0.0
        for e in (0, 1):
            w = e + b
            part = terms[2 * a + w // 2][e * CHANNELS : (e + 1) * CHANNELS]
            result = result + (part if (w % 2 == 1) == high else turn(part))
        return result

    total = bias + turn(bias)
    coarse = total.astype(BF16).astype(F32)
    fine = total - coarse
    for t in range(5):
        if t < 4:
            high = tap(2 * t + 1, True)
        else:
            high = jnp.where(row == 0, coarse, jnp.where(row == 1, fine, 0.0))
        msg[t * SIDE : (t + 1) * SIDE, :] = halves(tap(2 * t, False), high)
    core = lax.axis_index("region") & 1
    keep_ref[...] = msg[pl.ds(pl.multiple_of(core * WROWS, WROWS), WROWS), :].astype(BF16)
    send_ref[0:WROWS, :] = msg[pl.ds(pl.multiple_of((1 - core) * WROWS, WROWS), WROWS), :].astype(BF16)

    lines = []
    for src, tap_row in ((gt, 2), (gb, 0)):
        window = jnp.concatenate([src[0:PAIRS, :], src[1 : PAIRS + 1, :]], axis=1).astype(BF16)
        lines.append(dot(window, wb_ref[tap_row]))
    own_scr[pl.ds(0, PAIRS, stride=2), :] = halves(lines[0], turn(lines[1]))
    own_scr[pl.ds(1, PAIRS, stride=2), :] = halves(turn(lines[0]), lines[1])
    own_ref[...] = own_scr[...].astype(BF16)

    gc[...] = jnp.zeros(gc.shape, F32)
    gc[8 : 8 + SIDE, :] = halves(g_left, g_right)
    grads = dot(gc[8:88, :].astype(BF16), wc_ref[0])
    grads = grads + dot(gc[7:87, :].astype(BF16), wc_ref[1])
    grads = grads + dot(gc[6:86, :].astype(BF16), wc_ref[2])
    other = turn(grads)
    lefts = halves(grads, other)
    rights = halves(other, grads)
    cell_scr[...] = jnp.zeros(cell_scr.shape, F32)
    for at, src, first_row, n in (
        (0, lefts, 0, 1), (SIDE + 1, rights, 0, 1), (SIDE + 2, lefts, SIDE + 1, 1), (edge - 1, rights, SIDE + 1, 1),
        (edge, lefts, 1, SIDE), (edge + SIDE, rights, 1, SIDE),
    ):
        cell_scr[at : at + n, :] = src[first_row : first_row + n]
    placed = jnp.where(upper == low(cells.shape), 0.0, cell_scr[...]).astype(BF16)
    send_ref[WROWS:, :] = dot(hot_ref[:, many:], placed, TN).astype(BF16)


def grad_copies_kernel(g_ref, g_lines, g_sides, p0, p1, p2):
    row = iota((SIDE, LANES), 0)
    left = g_sides[0:SIDE, :].astype(F32)
    right = g_sides[SIDE:, :].astype(F32)

    def load(q):
        g = g_ref[block(q), :].astype(F32)
        g = jnp.where(row == 0, g_lines[pl.ds(q, 1), :], g)
        g = jnp.where(row == SIDE - 1, g_lines[pl.ds(PAIRS + q, 1), :], g)
        return jnp.where(q == 0, left, jnp.where(q == PAIRS - 1, right, g))

    shifted_copies(load, p0, p1, p2)


def inner_kernel(p0, p1, p2, wb_ref, out_ref):
    n = 4 * SIDE

    def step(c, carry):
        start = pl.multiple_of(c * n, n)
        out_ref[pl.ds(start, n), :] = product(p0, p1, p2, wb_ref, start, n, ((1,), (0,)))
        return carry

    lax.fori_loop(0, ROWS // n, step, 0)


def added_weights(mine, other):
    total = mine[0:WROWS, :].astype(F32) + other[0:WROWS, :].astype(F32)
    tail = total[WROWS - SIDE :]
    return total, tail + pltpu.roll(tail, SIDE - 1, 0)


def bias_lanes(shape):
    return jnp.logical_and(jnp.logical_not(low(shape)), (lax.axis_index("region") & 1) == 1)


def join_kernel(mine, other, *rest):
    extra, out = rest[:-1], rest[-1]
    total, whole = added_weights(mine, other)
    out[0 : WROWS - SIDE, :] = total[: WROWS - SIDE].astype(BF16)
    row = iota(whole.shape, 0)
    coarse = whole.astype(BF16).astype(F32)
    fine = pltpu.roll(whole - coarse, 1, 0)
    out[WROWS - SIDE : WROWS, :] = jnp.where(
        bias_lanes(whole.shape),
        jnp.where(row == 0, coarse, jnp.where(row == 1, fine, 0.0)),
        total[WROWS - SIDE :],
    ).astype(BF16)
    n = mine.shape[0] - WROWS
    if n:
        out[WROWS : WROWS + n, :] = mine[WROWS:, :]
        out[WROWS + n :, :] = other[WROWS:, :]
    if extra:
        out[WROWS:, :] = extra[0][...]


def close_kernel(scale, a, b, c, d, out):
    left, _ = added_weights(a, b)
    right, _ = added_weights(c, d)
    total = left + right
    tail = total[WROWS - SIDE :]
    whole = tail + pltpu.roll(tail, SIDE - 1, 0)
    out[0 : WROWS - SIDE, :] = total[: WROWS - SIDE] * scale
    out[WROWS - SIDE :, :] = jnp.where(bias_lanes(whole.shape), whole, total[WROWS - SIDE :]) * scale


def weight_kernel(mine, other, wt_ref, bias_ref):
    odd = (lax.axis_index("region") & 1) == 1
    a, b = mine[...], other[...]
    full = jnp.concatenate([jnp.where(odd, b, a), jnp.where(odd, a, b)], axis=0)
    for t in range(4):
        wt_ref[:, t * LANES : (t + 1) * LANES] = full[t * SIDE : (t + 1) * SIDE]
    wt_ref[:, 4 * LANES :] = full[4 * SIDE :, :CHANNELS]
    bias_ref[...] = turn(full[4 * SIDE : 4 * SIDE + 8])[0:1, :CHANNELS]


def last_kernel(row_a, row_b, row_c, row_d, inner, pick, *rest):
    side_refs, grad_ref = rest[:-1], rest[-1]
    n = row_a.shape[0] - WROWS
    got = 0.0
    for i, ref in enumerate((row_a, row_b, row_c, row_d)):
        got = got + dot(pick[:, i * n : (i + 1) * n], ref[WROWS:, :])
    a, b, c, d = (got[i * SIDE : (i + 1) * SIDE] for i in range(4))
    rims = halves(a + turn(b), turn(c) + d)
    sides = side_refs[0][side_refs[0].shape[0] - SIDE :, :].astype(F32)
    for ref in side_refs[1:]:
        sides = sides + ref[...].astype(F32)
    row = iota((SIDE, LANES), 0)
    is_low = low((SIDE, LANES))
    for q in range(PAIRS):
        v = inner[q * SIDE : (q + 1) * SIDE, :]
        v = v + jnp.where(row == 0, rims[q : q + 1], jnp.where(row == SIDE - 1, rims[PAIRS + q : PAIRS + q + 1], 0.0))
        if q == 0:
            v = v + jnp.where(is_low, sides, 0.0)
        if q == PAIRS - 1:
            v = v + jnp.where(is_low, 0.0, sides)
        grad_ref[:, q * LANES : (q + 1) * LANES] = v.astype(BF16)


def swap(x, axis, k):
    n = lax.axis_size(axis)
    return lax.ppermute(x, axis, [(i, i ^ k) for i in range(n)])


def shift(x, axis, by):
    n = lax.axis_size(axis)
    return lax.ppermute(x, axis, [(i, (i + by) % n) for i in range(n)])


def steps_of(n):
    ks = []
    k = n // 2
    while k:
        ks.append(k)
        k //= 2
    return ks


def slot_bits(owners):
    high = range(2, owners.bit_length() - 1)
    count = len(high)
    return [(bit, step) for step, bit in enumerate(high)] + [(0, count), (1, count + 1)]


def exchange(x, k):
    return swap(x, "patch", k)


def three_partners(x):
    got = {k: exchange(x, k) for k in (3, 2, 1)}
    return [got[k] for k in (1, 2, 3)]


def body(fine_input, fine_weight, fine_bias, cotangent, halo_index):
    owners = lax.axis_size("patch")
    regions = lax.axis_size("region")
    high = [1 << bit for bit in range(2, owners.bit_length() - 1)]
    blocks = 1 if regions == 2 else 2
    x = fine_input.reshape(SIDE, SIDE * CHANNELS)
    cot = cotangent.reshape(SIDE, SIDE * CHANNELS)
    pair = ((ROWS + SIDE, LANES), BF16)

    rows, cols = call(rim_kernel, [((SIDE, LANES), BF16)] * 2, x, scratch=[pltpu.VMEM((SIDE, LANES), F32)])
    if regions == 2:
        cols = swap(cols, "region", 1)
    else:
        cols = jnp.concatenate([shift(cols, "region", 1), shift(cols, "region", -1)], axis=0)
    count = 272
    both = ((ROWS, LANES), F32)
    work = dict(flops=2 * ROWS * 768 * 128, moved=3 * 2**20)

    def joined(rows, other):
        return call(rows_kernel, [((2 * rows.shape[0], LANES), BF16)], rows, other)[0]

    other = exchange(rows, high[0])
    *copies, lines = call(copies_kernel, [pair] * 3 + [((4, 40, LANES), F32)], x, moved=2 * 2**20)
    forward, backward, columns = call(
        weights_kernel,
        [((3, LANES, 2 * LANES), BF16), ((3, 2 * LANES, LANES), BF16), ((3, LANES, LANES), BF16)],
        fine_weight.T,
    )
    other, copies, lines, forward = lax.optimization_barrier((other, copies, lines, forward))
    rows = joined(rows, other)
    other = exchange(rows, high[1])
    signal = call(signal_kernel, [both], *copies, forward, fine_bias.reshape(1, CHANNELS), **work)[0]
    other, signal, index = lax.optimization_barrier((other, signal, halo_index))
    rows = joined(rows, other)
    for k in high[2:]:
        rows = joined(rows, exchange(rows, k))
    others = three_partners(rows)
    hot, half_mask = call(
        functools.partial(plan_kernel, owners, regions, blocks),
        [((count, (owners + blocks) * SIDE), BF16), ((count, LANES), F32)],
        index, scratch=[pltpu.VMEM((8, 384), F32)],
    )
    pick = call(functools.partial(pick_kernel, owners), [((4 * SIDE, owners * SIDE), BF16)], index)[0]
    inside = call(
        inside_kernel,
        [((ROWS, LANES), BF16), ((3, LANES, 2 * LANES), F32), ((8, LANES), F32), ((SIDE, LANES), F32)],
        signal, cot, *copies, **work,
    )
    others, hot, half_mask, pick, inside = lax.optimization_barrier((others, hot, half_mask, pick, inside))
    grad, *inside = inside

    line = pltpu.VMEM((40, LANES), F32)
    g_lines, g_sides, message, sent, own_rows = call(
        middle_kernel,
        [
            ((SIDE, LANES), F32), ((2 * SIDE, LANES), BF16),
            ((WROWS, LANES), BF16), ((WROWS + blocks * SIDE, LANES), BF16), ((SIDE, LANES), BF16),
        ],
        signal, cot, *copies, lines, *inside, rows, *others, cols, hot, half_mask, forward, backward, columns,
        scratch=[
            pltpu.VMEM((count, LANES), F32), line, line,
            pltpu.VMEM((96, LANES), F32), pltpu.VMEM((SIDE, LANES), F32), pltpu.VMEM((2 * WROWS, LANES), F32),
        ],
        moved=2**20,
    )

    if regions > 2:
        upper, lower = sent[WROWS + SIDE :], sent[WROWS : WROWS + SIDE]
        sides = [shift(upper, "region", 1), shift(lower, "region", -1)]
        sent = sent[:WROWS]
    other = swap(sent, "region", 1)
    if regions == 2:
        sides = [other]
    far = [k for k in steps_of(regions) if k > 1]
    for k in [1] + far:
        extra = () if k != ([1] + far)[-1] else (own_rows,)
        size = (WROWS + SIDE * len(extra), LANES)
        message = call(join_kernel, [(size, BF16)], message, other if k == 1 else swap(message, "region", k), *extra)[0]
    beside = [grad, g_lines, g_sides]
    for step, k in enumerate(high):
        message, beside = lax.optimization_barrier((message, beside))
        other = exchange(message, k)
        if step == 1:
            beside = call(grad_copies_kernel, [pair] * 3, *beside, moved=2 * 2**20)
        other, beside = lax.optimization_barrier((other, beside))
        size = (2 * message.shape[0] - WROWS, LANES)
        message = call(join_kernel, [(size, BF16)], message, other)[0]
    message, beside = lax.optimization_barrier((message, beside))
    others = three_partners(message)
    beside = call(inner_kernel, [both], *beside, backward, **work)[0]
    others, beside = lax.optimization_barrier((others, beside))
    scale = 1.0 / math.sqrt(regions * owners * SIDE * SIDE)
    part = call(functools.partial(close_kernel, scale), [((WROWS, LANES), F32)], message, *others)[0]
    other_part = swap(part, "region", 1)
    input_grad = call(
        last_kernel, [((SIDE, SIDE * CHANNELS), BF16)], message, *others, beside, pick, *sides, moved=2 * 2**20
    )[0]
    weight_grad, bias_grad = call(
        weight_kernel, [((CHANNELS, 9 * CHANNELS), F32), ((1, CHANNELS), F32)], part, other_part
    )
    return input_grad.reshape(1, SIDE, SIDE * CHANNELS), weight_grad.T, bias_grad.reshape(CHANNELS)


def solution(mesh):
    placed = (
        P(("region", "patch"), None, None),
        P(),
        P(),
        P(("region", "patch"), None, None),
        P("region", None),
    )
    return jax.shard_map(
        body,
        mesh=mesh,
        in_specs=placed,
        out_specs=(P(("region", "patch"), None, None), P(), P()),
        check_vma=False,
    )
```

```python
import functools
import math

import jax
import jax.numpy as jnp
from jax import lax
from jax.experimental import pallas as pl
from jax.experimental.pallas import tpu as pltpu
from jax.sharding import PartitionSpec as P

CHANNELS = 64
SIDE = 64
PAIRS = SIDE // 2
LANES = 2 * CHANNELS
ROWS = PAIRS * SIDE
WROWS = 5 * CHANNELS // 2
F32 = jnp.float32
BF16 = jnp.bfloat16


def call(kernel, outs, *args, scratch=(), flops=0, moved=0, space=pltpu.VMEM, limit=48):
    whole = pl.BlockSpec(memory_space=pltpu.VMEM)
    shapes = [jax.ShapeDtypeStruct(s, d) for s, d in outs]
    return pl.pallas_call(
        kernel,
        out_shape=shapes,
        in_specs=[pl.BlockSpec(memory_space=space)] * len(args),
        out_specs=[whole] * len(outs),
        scratch_shapes=list(scratch),
        compiler_params=pltpu.CompilerParams(vmem_limit_bytes=limit * 2**20),
        cost_estimate=pl.CostEstimate(flops=flops, bytes_accessed=moved, transcendentals=0),
    )(*args)


def iota(shape, dim):
    return lax.broadcasted_iota(jnp.int32, shape, dim)


def low(shape):
    return iota(shape, len(shape) - 1) < CHANNELS


def turn(x):
    return pltpu.roll(x, CHANNELS, 1)


def tile(q):
    return pl.ds(pl.multiple_of(q * LANES, LANES), LANES)


def block(q):
    return pl.ds(pl.multiple_of(q * SIDE, SIDE), SIDE)


def dot(a, b, dims=((1,), (0,))):
    return lax.dot_general(a, b, (dims, ((), ())), preferred_element_type=F32)


NT = ((1,), (1,))
TN = ((0,), (0,))


def shifted_copies(load, p0, p1, p2, lines=None):
    is_low = low((SIDE, LANES))
    row = iota((SIDE, LANES), 0)

    def put(q, before, now):
        v = jnp.where(is_low, before, now)
        p1[block(q), :] = v.astype(BF16)
        if lines is not None:
            for i, r in enumerate((0, 1, SIDE - 2, SIDE - 1)):
                lines[i, pl.ds(q, 1), :] = v[r : r + 1]
        p0[block(q), :] = jnp.where(row == 0, 0.0, pltpu.roll(v, 1, 0)).astype(BF16)
        p2[block(q), :] = jnp.where(row == SIDE - 1, 0.0, pltpu.roll(v, SIDE - 1, 0)).astype(BF16)

    def step(q, before):
        now = turn(load(q))
        put(q, before, now)
        return now

    zero = jnp.zeros((SIDE, LANES), F32)
    last = lax.fori_loop(0, PAIRS, step, zero, unroll=2)
    put(PAIRS, last, zero)


def product(p0, p1, p2, w_ref, start, n, dims):
    total = None
    for a, p in enumerate((p0, p1, p2)):
        window = jnp.concatenate([p[pl.ds(start, n), :], p[pl.ds(start + SIDE, n), :]], axis=1)
        term = dot(window, w_ref[a], dims)
        total = term if total is None else total + term
    return total


def rim_kernel(x_ref, rows_ref, cols_ref, scr):
    for q in range(PAIRS):
        lanes = slice(q * LANES, (q + 1) * LANES)
        scr[q : q + 1, :] = x_ref[0:16, lanes].astype(F32)[0:1]
        scr[PAIRS + q : PAIRS + q + 1, :] = x_ref[SIDE - 16 : SIDE, lanes].astype(F32)[15:16]
    rows_ref[...] = scr[...].astype(BF16)
    first = x_ref[:, 0:LANES].astype(F32)
    last = x_ref[:, (PAIRS - 1) * LANES :].astype(F32)
    cols_ref[...] = halves(first, last).astype(BF16)


def rows_kernel(*refs):
    parts, out = refs[:-1], refs[-1]
    n = parts[0].shape[0]
    for i, part in enumerate(parts):
        out[i * n : (i + 1) * n, :] = part[...]


def bits_moved(v, pairs):
    result = jnp.zeros_like(v)
    for from_bit, to_bit in pairs:
        result = result | (((v >> from_bit) & 1) << to_bit)
    return result


def plan_kernel(owners, regions, blocks, index_ref, hot_ref, half_ref, scr):
    owner = lax.axis_index("patch")
    region = lax.axis_index("region")
    bits = owners.bit_length() - 1
    index = index_ref[pl.ds(owner, 1), :]
    source, within = index >> 8, index & 255
    slot = bits_moved((source & (owners - 1)) ^ owner, slot_bits(owners))
    row = within & (SIDE - 1)
    if blocks == 2:
        row = row + jnp.where((((source >> bits) - region + regions) & (regions - 1)) == 1, SIDE, 0)
    is_row = within < 2 * SIDE
    place = jnp.where(is_row, slot * SIDE + (within >> 1), owners * SIDE + row)
    half = jnp.where(is_row, within & 1, (within >> 6) & 1)
    count = index.shape[1]
    scr[...] = jnp.full(scr.shape, -1.0, F32)
    scr[0:1, 0:count] = place.astype(F32)
    scr[1:2, 0:count] = half.astype(F32)
    column = jnp.transpose(scr[...])[0 : hot_ref.shape[0]]
    half_ref[...] = jnp.broadcast_to(column[:, 1:2], half_ref.shape)
    place = column[:, 0:1].astype(jnp.int32)
    for c in range(0, hot_ref.shape[1], LANES):
        n = min(LANES, hot_ref.shape[1] - c)
        hot_ref[:, c : c + n] = (place == iota((hot_ref.shape[0], n), 1) + c).astype(F32).astype(BF16)


def pick_kernel(owners, index_ref, pick_ref):
    owner, region = lax.axis_index("patch"), lax.axis_index("region")
    base = (region * owners + owner) * 4 * SIDE
    want = 2 * iota((SIDE, LANES), 0)
    for t in range(owners // 2):
        pair = []
        for slot in (2 * t, 2 * t + 1):
            relative = sum(1 << bit for bit, to in slot_bits(owners) if (slot >> to) & 1)
            line = index_ref[pl.ds(owner ^ relative, 1), :]
            pair.append((line[:, 1 : SIDE + 1], line[:, SIDE + 3 : 2 * SIDE + 3]))
        for s in range(2):
            both = jnp.concatenate([pair[0][s], pair[1][s]], axis=1) - base
            for e in range(2):
                hit = (both == want + e).astype(F32).astype(BF16)
                n = 2 * e + s
                pick_ref[n * SIDE : (n + 1) * SIDE, t * LANES : (t + 1) * LANES] = hit


def weights_kernel(wt_ref, w_ref, wb_ref, wc_ref):
    wide = [wt_ref[:, t * LANES : (t + 1) * LANES].astype(F32) for t in range(4)]
    tail = wt_ref[:, 4 * LANES :].astype(F32)
    wide.append(jnp.concatenate([tail, tail], axis=1))

    def at(a, b, high):
        m = 3 * a + b
        v = wide[m // 2]
        return v if m == 8 or (m % 2 == 1) == high else turn(v)

    def pair(a, left, right):
        zero = jnp.zeros((CHANNELS, LANES), F32)
        lo = zero if left is None else at(a, left, False)
        hi = zero if right is None else at(a, right, True)
        return halves(lo, hi).astype(BF16)

    c = CHANNELS
    for a in range(3):
        w_ref[a, 0:c, 0:LANES] = pair(a, 0, 1)
        w_ref[a, 0:c, LANES:] = pair(a, 2, None)
        w_ref[a, c:, 0:LANES] = pair(a, None, 0)
        w_ref[a, c:, LANES:] = pair(a, 1, 2)
        for w, (left, right) in enumerate(((2, None), (1, 2), (0, 1), (None, 0))):
            wb_ref[2 - a, w * c : (w + 1) * c, :] = pair(a, left, right)
        wc_ref[a, 0:c, :] = pair(a, 0, None)
        wc_ref[a, c:, :] = pair(a, None, 2)


def copies_kernel(x_ref, p0, p1, p2, lines):
    shifted_copies(lambda q: x_ref[:, tile(q)].astype(F32), p0, p1, p2, lines)


def signal_kernel(p0, p1, p2, w_ref, bias_ref, s_ref):
    n = 4 * SIDE
    bias = jnp.concatenate([bias_ref[...], bias_ref[...]], axis=1)

    def step(c, carry):
        start = pl.multiple_of(c * n, n)
        s_ref[pl.ds(start, n), :] = product(p0, p1, p2, w_ref, start, n, NT) + bias
        return carry

    lax.fori_loop(0, ROWS // n, step, 0)


def slope_times(signal, upstream):
    sigma = 1.0 / (1.0 + jnp.exp(-signal))
    return upstream * (sigma * (1.0 + signal * (1.0 - sigma)))


def halves(even, odd):
    return jnp.where(low(even.shape), even, odd)


def inside_kernel(s_ref, cot_ref, p0, p1, p2, g_ref, terms_ref, bias_ref, cot_lines):
    row = iota((SIDE, LANES), 0)
    border = jnp.logical_or(row == 0, row == SIDE - 1)

    def step(q, bias):
        upstream = cot_ref[:, tile(q)].astype(F32)
        g = jnp.where(border, 0.0, slope_times(s_ref[block(q), :], upstream)).astype(BF16)
        g_ref[block(q), :] = g
        cot_lines[pl.ds(q, 1), :] = upstream[0:1]
        cot_lines[pl.ds(PAIRS + q, 1), :] = upstream[SIDE - 1 :]
        return bias + jnp.sum(g.astype(F32).reshape(8, 8, LANES), axis=0)

    cot_lines[...] = jnp.zeros(cot_lines.shape, F32)
    bias_ref[...] = lax.fori_loop(1, PAIRS - 1, step, jnp.zeros((8, LANES), F32), unroll=2)
    g_ref[0:SIDE, :] = jnp.zeros((SIDE, LANES), BF16)
    g_ref[ROWS - SIDE :, :] = jnp.zeros((SIDE, LANES), BF16)
    g = g_ref[SIDE : ROWS - SIDE, :]
    for a, p in enumerate((p0, p1, p2)):
        for shift in (0, 1):
            start = (1 + shift) * SIDE
            terms_ref[a, :, shift * LANES : (shift + 1) * LANES] = dot(g, p[start : start + ROWS - 2 * SIDE, :], TN)


def middle_kernel(
    s_ref, cot_ref, p0, p1, p2, lines, terms_ref, bias_ref, cot_lines, rows_a, rows_b, rows_c, rows_d, cols_ref,
    hot_ref, half_ref, w_ref, wb_ref, wc_ref,
    g_lines, g_sides, keep_ref, send_ref, own_ref, cell_scr, gt, gb, gc, own_scr, msg,
):
    n = rows_a.shape[0]
    many = 4 * n
    cells = dot(hot_ref[:, many:], cols_ref[...])
    for i, ref in enumerate((rows_a, rows_b, rows_c, rows_d)):
        cells = cells + dot(hot_ref[:, i * n : (i + 1) * n], ref[...])
    other = turn(cells)
    upper = half_ref[...] > 0.5
    edge = 2 * SIDE + 4
    as_low = jnp.where(upper, other, cells)
    as_high = jnp.where(upper, cells, other)
    sides = halves(as_low[edge : edge + SIDE], as_high[edge + SIDE : edge + 2 * SIDE])
    odd = iota(cells.shape, 0) % 2 == 1
    cell_scr[...] = jnp.where(odd, as_high, as_low)

    def windows(both):
        return jnp.concatenate([both[0:PAIRS], both[1 : PAIRS + 1]], axis=1)

    def line_of(start):
        even_cells = cell_scr[pl.ds(start, PAIRS + 1, stride=2), :]
        odd_cells = cell_scr[pl.ds(start + 1, PAIRS + 1, stride=2), :]
        return windows(halves(even_cells, odd_cells))

    is_low = low((SIDE, LANES))
    row = iota((SIDE, LANES), 0)
    top = line_of(0)
    bottom = line_of(SIDE + 2)
    moved = (
        jnp.where(row == 0, 0.0, pltpu.roll(sides, 1, 0)),
        sides,
        jnp.where(row == SIDE - 1, 0.0, pltpu.roll(sides, SIDE - 1, 0)),
    )
    lefts = [jnp.where(is_low, m, 0.0) for m in moved]
    rights = [jnp.where(is_low, 0.0, m) for m in moved]
    top_signal = dot(top.astype(BF16), w_ref[0], NT)
    bottom_signal = dot(bottom.astype(BF16), w_ref[2], NT)

    def side_grad(q, columns, lanes):
        signal = s_ref[q * SIDE : (q + 1) * SIDE, :]
        for a in range(3):
            signal = signal + dot(columns[a].astype(BF16), w_ref[a, :, lanes], NT)
        signal = signal + jnp.where(row == 0, top_signal[q : q + 1], 0.0)
        signal = signal + jnp.where(row == SIDE - 1, bottom_signal[q : q + 1], 0.0)
        upstream = cot_ref[:, q * LANES : (q + 1) * LANES].astype(F32)
        return slope_times(signal, upstream).astype(BF16).astype(F32)

    end = PAIRS - 1
    g_left = side_grad(0, lefts, slice(0, LANES))
    g_right = side_grad(end, rights, slice(LANES, 2 * LANES))
    pair = iota((PAIRS, LANES), 0)
    ends = jnp.logical_or(pair == 0, pair == end)

    def line_grad(first_row, halo_signal):
        signal = s_ref[pl.ds(first_row, PAIRS, stride=SIDE), :] + halo_signal
        upstream = cot_lines[0:PAIRS, :] if first_row == 0 else cot_lines[PAIRS:, :]
        g = jnp.where(ends, 0.0, slope_times(signal, upstream)).astype(BF16).astype(F32)
        r = slice(first_row, first_row + 1)
        return g, jnp.where(pair == 0, g_left[r], jnp.where(pair == end, g_right[r], g))

    inner_top, all_top = line_grad(0, top_signal)
    inner_bottom, all_bottom = line_grad(SIDE - 1, bottom_signal)
    g_lines[0:PAIRS, :] = all_top
    g_lines[PAIRS:, :] = all_bottom
    g_sides[0:SIDE, :] = g_left.astype(BF16)
    g_sides[SIDE:, :] = g_right.astype(BF16)
    border = jnp.concatenate([inner_top, inner_bottom, g_left, g_right], axis=0)
    bias = jnp.sum(bias_ref[...], axis=0, keepdims=True) + jnp.sum(border, axis=0, keepdims=True)
    border = border.astype(BF16)
    kept = [windows(lines[i]) for i in range(4)]
    none = jnp.zeros((SIDE, LANES), F32)
    wide_row = iota((SIDE, 2 * LANES), 0)

    def side_window(a, p, q, columns):
        parts = [p[(q + i) * SIDE : (q + i + 1) * SIDE, :].astype(F32) for i in range(2)]
        window = jnp.concatenate(parts, axis=1) + columns
        if a == 0:
            window = window + jnp.where(wide_row == 0, top[q : q + 1], 0.0)
        if a == 2:
            window = window + jnp.where(wide_row == SIDE - 1, bottom[q : q + 1], 0.0)
        return window

    terms = []
    over = (top, kept[0], kept[1])
    under = (kept[2], kept[3], bottom)
    for a, p in enumerate((p0, p1, p2)):
        window = jnp.concatenate(
            [
                over[a],
                under[a],
                side_window(a, p, 0, jnp.concatenate([lefts[a], none], axis=1)),
                side_window(a, p, end, jnp.concatenate([none, rights[a]], axis=1)),
            ],
            axis=0,
        ).astype(BF16)
        t = terms_ref[a] + dot(border, window, TN)
        terms += [t[:, :LANES], t[:, LANES:]]
    for scr, line in ((gt, all_top), (gb, all_bottom)):
        turned = turn(line)
        scr[...] = jnp.zeros(scr.shape, F32)
        scr[1 : PAIRS + 1, :] = jnp.where(low(line.shape), turned, 0.0)
        scr[0:PAIRS, :] += jnp.where(low(line.shape), 0.0, turned)

    def tap(m, high):
        a, b = m // 3, m % 3
        result = 0.0
        for e in (0, 1):
            w = e + b
            part = terms[2 * a + w // 2][e * CHANNELS : (e + 1) * CHANNELS]
            result = result + (part if (w % 2 == 1) == high else turn(part))
        return result

    total = bias + turn(bias)
    coarse = total.astype(BF16).astype(F32)
    fine = total - coarse
    for t in range(5):
        if t < 4:
            high = tap(2 * t + 1, True)
        else:
            high = jnp.where(row == 0, coarse, jnp.where(row == 1, fine, 0.0))
        msg[t * SIDE : (t + 1) * SIDE, :] = halves(tap(2 * t, False), high)
    core = lax.axis_index("region") & 1
    keep_ref[...] = msg[pl.ds(pl.multiple_of(core * WROWS, WROWS), WROWS), :].astype(BF16)
    send_ref[0:WROWS, :] = msg[pl.ds(pl.multiple_of((1 - core) * WROWS, WROWS), WROWS), :].astype(BF16)

    lines = []
    for src, tap_row in ((gt, 2), (gb, 0)):
        window = jnp.concatenate([src[0:PAIRS, :], src[1 : PAIRS + 1, :]], axis=1).astype(BF16)
        lines.append(dot(window, wb_ref[tap_row]))
    own_scr[pl.ds(0, PAIRS, stride=2), :] = halves(lines[0], turn(lines[1]))
    own_scr[pl.ds(1, PAIRS, stride=2), :] = halves(turn(lines[0]), lines[1])
    own_ref[...] = own_scr[...].astype(BF16)

    gc[...] = jnp.zeros(gc.shape, F32)
    gc[8 : 8 + SIDE, :] = halves(g_left, g_right)
    grads = dot(gc[8:88, :].astype(BF16), wc_ref[0])
    grads = grads + dot(gc[7:87, :].astype(BF16), wc_ref[1])
    grads = grads + dot(gc[6:86, :].astype(BF16), wc_ref[2])
    other = turn(grads)
    lefts = halves(grads, other)
    rights = halves(other, grads)
    cell_scr[...] = jnp.zeros(cell_scr.shape, F32)
    for at, src, first_row, n in (
        (0, lefts, 0, 1), (SIDE + 1, rights, 0, 1), (SIDE + 2, lefts, SIDE + 1, 1), (edge - 1, rights, SIDE + 1, 1),
        (edge, lefts, 1, SIDE), (edge + SIDE, rights, 1, SIDE),
    ):
        cell_scr[at : at + n, :] = src[first_row : first_row + n]
    placed = jnp.where(upper == low(cells.shape), 0.0, cell_scr[...]).astype(BF16)
    send_ref[WROWS:, :] = dot(hot_ref[:, many:], placed, TN).astype(BF16)


def grad_copies_kernel(g_ref, g_lines, g_sides, p0, p1, p2):
    row = iota((SIDE, LANES), 0)
    left = g_sides[0:SIDE, :].astype(F32)
    right = g_sides[SIDE:, :].astype(F32)

    def load(q):
        g = g_ref[block(q), :].astype(F32)
        g = jnp.where(row == 0, g_lines[pl.ds(q, 1), :], g)
        g = jnp.where(row == SIDE - 1, g_lines[pl.ds(PAIRS + q, 1), :], g)
        return jnp.where(q == 0, left, jnp.where(q == PAIRS - 1, right, g))

    shifted_copies(load, p0, p1, p2)


def inner_kernel(p0, p1, p2, wb_ref, out_ref):
    n = 4 * SIDE

    def step(c, carry):
        start = pl.multiple_of(c * n, n)
        out_ref[pl.ds(start, n), :] = product(p0, p1, p2, wb_ref, start, n, ((1,), (0,)))
        return carry

    lax.fori_loop(0, ROWS // n, step, 0)


def added_weights(parts):
    terms = [part[0:WROWS, :].astype(F32) for part in parts]
    while len(terms) > 1:
        terms = [terms[i] + terms[i + 1] for i in range(0, len(terms), 2)]
    tail = terms[0][WROWS - SIDE :]
    return terms[0], tail + pltpu.roll(tail, SIDE - 1, 0)


def bias_lanes(shape):
    return jnp.logical_and(jnp.logical_not(low(shape)), (lax.axis_index("region") & 1) == 1)


def put_weights(parts, out):
    total, whole = added_weights(parts)
    out[0 : WROWS - SIDE, :] = total[: WROWS - SIDE].astype(BF16)
    row = iota(whole.shape, 0)
    coarse = whole.astype(BF16).astype(F32)
    fine = pltpu.roll(whole - coarse, 1, 0)
    out[WROWS - SIDE : WROWS, :] = jnp.where(
        bias_lanes(whole.shape),
        jnp.where(row == 0, coarse, jnp.where(row == 1, fine, 0.0)),
        total[WROWS - SIDE :],
    ).astype(BF16)


def first_join_kernel(mine, other, *rest):
    extra, out = rest[:-1], rest[-1]
    put_weights((mine, other), out)
    if extra:
        out[WROWS:, :] = extra[0][...]


def join_kernel(*refs):
    parts, out = refs[:-1], refs[-1]
    put_weights(parts, out)
    n = parts[0].shape[0] - WROWS
    for i, part in enumerate(parts):
        out[WROWS + i * n : WROWS + (i + 1) * n, :] = part[WROWS:, :]


def close_kernel(scale, *refs):
    parts, out = refs[:-1], refs[-1]
    total, whole = added_weights(parts)
    out[0 : WROWS - SIDE, :] = total[: WROWS - SIDE] * scale
    out[WROWS - SIDE :, :] = jnp.where(bias_lanes(whole.shape), whole, total[WROWS - SIDE :]) * scale


def weight_kernel(mine, other, wt_ref, bias_ref):
    odd = (lax.axis_index("region") & 1) == 1
    a, b = mine[...], other[...]
    full = jnp.concatenate([jnp.where(odd, b, a), jnp.where(odd, a, b)], axis=0)
    for t in range(4):
        wt_ref[:, t * LANES : (t + 1) * LANES] = full[t * SIDE : (t + 1) * SIDE]
    wt_ref[:, 4 * LANES :] = full[4 * SIDE :, :CHANNELS]
    bias_ref[...] = turn(full[4 * SIDE : 4 * SIDE + 8])[0:1, :CHANNELS]


def last_kernel(row_a, row_b, row_c, row_d, inner, pick, *rest):
    side_refs, grad_ref = rest[:-1], rest[-1]
    n = row_a.shape[0] - WROWS
    got = 0.0
    for i, ref in enumerate((row_a, row_b, row_c, row_d)):
        got = got + dot(pick[:, i * n : (i + 1) * n], ref[WROWS:, :])
    a, b, c, d = (got[i * SIDE : (i + 1) * SIDE] for i in range(4))
    rims = halves(a + turn(b), turn(c) + d)
    sides = side_refs[0][side_refs[0].shape[0] - SIDE :, :].astype(F32)
    for ref in side_refs[1:]:
        sides = sides + ref[...].astype(F32)
    row = iota((SIDE, LANES), 0)
    is_low = low((SIDE, LANES))
    for q in range(PAIRS):
        v = inner[q * SIDE : (q + 1) * SIDE, :]
        v = v + jnp.where(row == 0, rims[q : q + 1], jnp.where(row == SIDE - 1, rims[PAIRS + q : PAIRS + q + 1], 0.0))
        if q == 0:
            v = v + jnp.where(is_low, sides, 0.0)
        if q == PAIRS - 1:
            v = v + jnp.where(is_low, 0.0, sides)
        grad_ref[:, q * LANES : (q + 1) * LANES] = v.astype(BF16)


def swap(x, axis, k):
    n = lax.axis_size(axis)
    return lax.ppermute(x, axis, [(i, i ^ k) for i in range(n)])


def shift(x, axis, by):
    n = lax.axis_size(axis)
    return lax.ppermute(x, axis, [(i, (i + by) % n) for i in range(n)])


def steps_of(n):
    ks = []
    k = n // 2
    while k:
        ks.append(k)
        k //= 2
    return ks


def rounds_of(owners):
    count = owners.bit_length() - 1
    pairs = [(bit, bit + 1) for bit in range(count % 2, count, 2)][::-1]
    if count % 2:
        pairs = [tuple(b - 1 for b in p) for p in pairs]
        return [(count - 1,)] + pairs
    return pairs


def slot_bits(owners):
    bits = [bit for bits in rounds_of(owners) for bit in bits]
    return [(bit, to) for to, bit in enumerate(bits)]


def exchange(x, bits):
    ks = [sum(1 << bits[i] for i in range(len(bits)) if (n >> i) & 1) for n in range(1, 1 << len(bits))]
    got = {k: swap(x, "patch", k) for k in ks[::-1]}
    return [got[k] for k in ks]


def body(fine_input, fine_weight, fine_bias, cotangent, halo_index):
    owners = lax.axis_size("patch")
    regions = lax.axis_size("region")
    rounds = rounds_of(owners)
    blocks = 1 if regions == 2 else 2
    x = fine_input.reshape(SIDE, SIDE * CHANNELS)
    cot = cotangent.reshape(SIDE, SIDE * CHANNELS)
    pair = ((ROWS + SIDE, LANES), BF16)

    rows, cols = call(rim_kernel, [((SIDE, LANES), BF16)] * 2, x, scratch=[pltpu.VMEM((SIDE, LANES), F32)])
    if regions == 2:
        cols = swap(cols, "region", 1)
    else:
        cols = jnp.concatenate([shift(cols, "region", 1), shift(cols, "region", -1)], axis=0)
    count = 272
    both = ((ROWS, LANES), F32)
    work = dict(flops=2 * ROWS * 768 * 128, moved=3 * 2**20)

    others = exchange(rows, rounds[0])
    *copies, lines = call(copies_kernel, [pair] * 3 + [((4, 40, LANES), F32)], x, moved=2 * 2**20)
    forward, backward, columns = call(
        weights_kernel,
        [((3, LANES, 2 * LANES), BF16), ((3, 2 * LANES, LANES), BF16), ((3, LANES, LANES), BF16)],
        fine_weight.T,
    )
    signal = call(signal_kernel, [both], *copies, forward, fine_bias.reshape(1, CHANNELS), **work)[0]
    others, signal, index = lax.optimization_barrier((others, signal, halo_index))
    for bits in rounds[1:]:
        size = ((len(others) + 1) * rows.shape[0], LANES)
        rows = call(rows_kernel, [(size, BF16)], rows, *others)[0]
        others = exchange(rows, bits)
    hot, half_mask = call(
        functools.partial(plan_kernel, owners, regions, blocks),
        [((count, (owners + blocks) * SIDE), BF16), ((count, LANES), F32)],
        index, scratch=[pltpu.VMEM((8, 384), F32)],
    )
    pick = call(functools.partial(pick_kernel, owners), [((4 * SIDE, owners * SIDE), BF16)], index)[0]
    inside = call(
        inside_kernel,
        [((ROWS, LANES), BF16), ((3, LANES, 2 * LANES), F32), ((8, LANES), F32), ((SIDE, LANES), F32)],
        signal, cot, *copies, **work,
    )
    others, hot, half_mask, pick, inside = lax.optimization_barrier((others, hot, half_mask, pick, inside))
    grad, *inside = inside

    line = pltpu.VMEM((40, LANES), F32)
    g_lines, g_sides, message, sent, own_rows = call(
        middle_kernel,
        [
            ((SIDE, LANES), F32), ((2 * SIDE, LANES), BF16),
            ((WROWS, LANES), BF16), ((WROWS + blocks * SIDE, LANES), BF16), ((SIDE, LANES), BF16),
        ],
        signal, cot, *copies, lines, *inside, rows, *others, cols, hot, half_mask, forward, backward, columns,
        scratch=[
            pltpu.VMEM((count, LANES), F32), line, line,
            pltpu.VMEM((96, LANES), F32), pltpu.VMEM((SIDE, LANES), F32), pltpu.VMEM((2 * WROWS, LANES), F32),
        ],
        moved=2**20,
    )

    if regions > 2:
        upper, lower = sent[WROWS + SIDE :], sent[WROWS : WROWS + SIDE]
        sides = [shift(upper, "region", 1), shift(lower, "region", -1)]
        sent = sent[:WROWS]
    other = swap(sent, "region", 1)
    if regions == 2:
        sides = [other]
    far = [k for k in steps_of(regions) if k > 1]
    for k in [1] + far:
        extra = () if k != ([1] + far)[-1] else (own_rows,)
        size = (WROWS + SIDE * len(extra), LANES)
        got = other if k == 1 else swap(message, "region", k)
        message = call(first_join_kernel, [(size, BF16)], message, got, *extra)[0]
    beside = [grad, g_lines, g_sides]
    for bits in rounds[:-1]:
        message, beside = lax.optimization_barrier((message, beside))
        others = exchange(message, bits)
        if bits == rounds[-2]:
            beside = call(grad_copies_kernel, [pair] * 3, *beside, moved=2 * 2**20)
        others, beside = lax.optimization_barrier((others, beside))
        size = (WROWS + (len(others) + 1) * (message.shape[0] - WROWS), LANES)
        message = call(join_kernel, [(size, BF16)], message, *others)[0]
    message, beside = lax.optimization_barrier((message, beside))
    others = exchange(message, rounds[-1])
    beside = call(inner_kernel, [both], *beside, backward, **work)[0]
    others, beside = lax.optimization_barrier((others, beside))
    scale = 1.0 / math.sqrt(regions * owners * SIDE * SIDE)
    part = call(functools.partial(close_kernel, scale), [((WROWS, LANES), F32)], message, *others)[0]
    other_part = swap(part, "region", 1)
    input_grad = call(
        last_kernel, [((SIDE, SIDE * CHANNELS), BF16)], message, *others, beside, pick, *sides, moved=2 * 2**20
    )[0]
    weight_grad, bias_grad = call(
        weight_kernel, [((CHANNELS, 9 * CHANNELS), F32), ((1, CHANNELS), F32)], part, other_part
    )
    return input_grad.reshape(1, SIDE, SIDE * CHANNELS), weight_grad.T, bias_grad.reshape(CHANNELS)


def solution(mesh):
    placed = (
        P(("region", "patch"), None, None),
        P(),
        P(),
        P(("region", "patch"), None, None),
        P("region", None),
    )
    return jax.shard_map(
        body,
        mesh=mesh,
        in_specs=placed,
        out_specs=(P(("region", "patch"), None, None), P(), P()),
        check_vma=False,
    )
```

```python
import functools
import math

import jax
import jax.numpy as jnp
from jax import lax
from jax.experimental import pallas as pl
from jax.experimental.pallas import tpu as pltpu
from jax.sharding import PartitionSpec as P

CHANNELS = 64
SIDE = 64
PAIRS = SIDE // 2
LANES = 2 * CHANNELS
ROWS = PAIRS * SIDE
WROWS = 5 * CHANNELS // 2
F32 = jnp.float32
BF16 = jnp.bfloat16


def call(kernel, outs, *args, scratch=(), flops=0, moved=0, limit=48):
    whole = pl.BlockSpec(memory_space=pltpu.VMEM)
    shapes = [jax.ShapeDtypeStruct(s, d) for s, d in outs]
    return pl.pallas_call(
        kernel,
        out_shape=shapes,
        in_specs=[whole] * len(args),
        out_specs=[whole] * len(outs),
        scratch_shapes=list(scratch),
        compiler_params=pltpu.CompilerParams(vmem_limit_bytes=limit * 2**20),
        cost_estimate=pl.CostEstimate(flops=flops, bytes_accessed=moved, transcendentals=0),
    )(*args)


def iota(shape, dim):
    return lax.broadcasted_iota(jnp.int32, shape, dim)


def low(shape):
    return iota(shape, len(shape) - 1) < CHANNELS


def turn(x):
    return pltpu.roll(x, CHANNELS, 1)


def tile(q):
    return pl.ds(pl.multiple_of(q * LANES, LANES), LANES)


def block(q):
    return pl.ds(pl.multiple_of(q * SIDE, SIDE), SIDE)


def dot(a, b, dims=((1,), (0,))):
    return lax.dot_general(a, b, (dims, ((), ())), preferred_element_type=F32)


NT = ((1,), (1,))
TN = ((0,), (0,))


def shifted_copies(load, p0, p1, p2, lines=None):
    is_low = low((SIDE, LANES))
    row = iota((SIDE, LANES), 0)

    def put(q, before, now):
        v = jnp.where(is_low, before, now)
        p1[block(q), :] = v.astype(BF16)
        if lines is not None:
            for i, r in enumerate((0, 1, SIDE - 2, SIDE - 1)):
                lines[i, pl.ds(q, 1), :] = v[r : r + 1]
        p0[block(q), :] = jnp.where(row == 0, 0.0, pltpu.roll(v, 1, 0)).astype(BF16)
        p2[block(q), :] = jnp.where(row == SIDE - 1, 0.0, pltpu.roll(v, SIDE - 1, 0)).astype(BF16)

    def step(q, before):
        now = turn(load(q))
        put(q, before, now)
        return now

    zero = jnp.zeros((SIDE, LANES), F32)
    last = lax.fori_loop(0, PAIRS, step, zero, unroll=4)
    put(PAIRS, last, zero)


def product(p0, p1, p2, w_ref, dims):
    total = None
    for a, p in enumerate((p0, p1, p2)):
        window = jnp.concatenate([p[0:ROWS, :], p[SIDE : ROWS + SIDE, :]], axis=1)
        term = dot(window, w_ref[a], dims)
        total = term if total is None else total + term
    return total


def rim_kernel(x_ref, rows_ref, cols_ref, scr):
    for q in range(PAIRS):
        lanes = slice(q * LANES, (q + 1) * LANES)
        scr[q : q + 1, :] = x_ref[0:16, lanes].astype(F32)[0:1]
        scr[PAIRS + q : PAIRS + q + 1, :] = x_ref[SIDE - 16 : SIDE, lanes].astype(F32)[15:16]
    rows_ref[...] = scr[...].astype(BF16)
    first = x_ref[:, 0:LANES].astype(F32)
    last = x_ref[:, (PAIRS - 1) * LANES :].astype(F32)
    cols_ref[...] = halves(first, last).astype(BF16)


def rows_kernel(*refs):
    parts, out = refs[:-1], refs[-1]
    n = parts[0].shape[0]
    for i, part in enumerate(parts):
        out[i * n : (i + 1) * n, :] = part[...]


def bits_moved(v, pairs):
    result = jnp.zeros_like(v)
    for from_bit, to_bit in pairs:
        result = result | (((v >> from_bit) & 1) << to_bit)
    return result


def plan_kernel(owners, regions, blocks, index_ref, hot_ref, half_ref, scr):
    owner = lax.axis_index("patch")
    region = lax.axis_index("region")
    bits = owners.bit_length() - 1
    index = index_ref[pl.ds(owner, 1), :]
    source, within = index >> 8, index & 255
    slot = bits_moved((source & (owners - 1)) ^ owner, slot_bits(owners))
    row = within & (SIDE - 1)
    if blocks == 2:
        row = row + jnp.where((((source >> bits) - region + regions) & (regions - 1)) == 1, SIDE, 0)
    is_row = within < 2 * SIDE
    place = jnp.where(is_row, slot * SIDE + (within >> 1), owners * SIDE + row)
    half = jnp.where(is_row, within & 1, (within >> 6) & 1)
    count = index.shape[1]
    scr[...] = jnp.full(scr.shape, -1.0, F32)
    scr[0:1, 0:count] = place.astype(F32)
    scr[1:2, 0:count] = half.astype(F32)
    column = jnp.transpose(scr[...])[0 : hot_ref.shape[0]]
    half_ref[...] = jnp.broadcast_to(column[:, 1:2], half_ref.shape)
    place = column[:, 0:1].astype(jnp.int32)
    for c in range(0, hot_ref.shape[1], LANES):
        n = min(LANES, hot_ref.shape[1] - c)
        hot_ref[:, c : c + n] = (place == iota((hot_ref.shape[0], n), 1) + c).astype(F32).astype(BF16)


def pick_kernel(owners, index_ref, pick_ref):
    owner, region = lax.axis_index("patch"), lax.axis_index("region")
    base = (region * owners + owner) * 4 * SIDE
    want = 2 * iota((SIDE, LANES), 0)
    for t in range(owners // 2):
        pair = []
        for slot in (2 * t, 2 * t + 1):
            relative = sum(1 << bit for bit, to in slot_bits(owners) if (slot >> to) & 1)
            line = index_ref[pl.ds(owner ^ relative, 1), :]
            pair.append((line[:, 1 : SIDE + 1], line[:, SIDE + 3 : 2 * SIDE + 3]))
        for s in range(2):
            both = jnp.concatenate([pair[0][s], pair[1][s]], axis=1) - base
            for e in range(2):
                hit = (both == want + e).astype(F32).astype(BF16)
                n = 2 * e + s
                pick_ref[n * SIDE : (n + 1) * SIDE, t * LANES : (t + 1) * LANES] = hit


def weights_kernel(wt_ref, w_ref, wb_ref, wc_ref):
    wide = [wt_ref[:, t * LANES : (t + 1) * LANES].astype(F32) for t in range(4)]
    tail = wt_ref[:, 4 * LANES :].astype(F32)
    wide.append(jnp.concatenate([tail, tail], axis=1))

    def at(a, b, high):
        m = 3 * a + b
        v = wide[m // 2]
        return v if m == 8 or (m % 2 == 1) == high else turn(v)

    def pair(a, left, right):
        zero = jnp.zeros((CHANNELS, LANES), F32)
        lo = zero if left is None else at(a, left, False)
        hi = zero if right is None else at(a, right, True)
        return halves(lo, hi).astype(BF16)

    c = CHANNELS
    for a in range(3):
        w_ref[a, 0:c, 0:LANES] = pair(a, 0, 1)
        w_ref[a, 0:c, LANES:] = pair(a, 2, None)
        w_ref[a, c:, 0:LANES] = pair(a, None, 0)
        w_ref[a, c:, LANES:] = pair(a, 1, 2)
        for w, (left, right) in enumerate(((2, None), (1, 2), (0, 1), (None, 0))):
            wb_ref[2 - a, w * c : (w + 1) * c, :] = pair(a, left, right)
        wc_ref[a, 0:c, :] = pair(a, 0, None)
        wc_ref[a, c:, :] = pair(a, None, 2)


def copies_kernel(x_ref, p0, p1, p2, lines):
    shifted_copies(lambda q: x_ref[:, tile(q)].astype(F32), p0, p1, p2, lines)


def signal_kernel(p0, p1, p2, w_ref, s_ref):
    s_ref[...] = product(p0, p1, p2, w_ref, NT)


def slope_times(signal, upstream):
    sigma = 1.0 / (1.0 + jnp.exp(-signal))
    return upstream * (sigma * (1.0 + signal * (1.0 - sigma)))


def halves(even, odd):
    return jnp.where(low(even.shape), even, odd)


def inside_kernel(s_ref, offset, cot_ref, p0, p1, p2, g_ref, terms_ref, bias_ref, cot_lines):
    row = iota((SIDE, LANES), 0)
    border = jnp.logical_or(row == 0, row == SIDE - 1)
    added = jnp.concatenate([offset[...], offset[...]], axis=1)

    def step(q, bias):
        upstream = cot_ref[:, tile(q)].astype(F32)
        g = jnp.where(border, 0.0, slope_times(s_ref[block(q), :] + added, upstream)).astype(BF16)
        g_ref[block(q), :] = g
        cot_lines[pl.ds(q, 1), :] = upstream[0:1]
        cot_lines[pl.ds(PAIRS + q, 1), :] = upstream[SIDE - 1 :]
        return bias + jnp.sum(g.astype(F32).reshape(8, 8, LANES), axis=0)

    cot_lines[...] = jnp.zeros(cot_lines.shape, F32)
    bias_ref[...] = lax.fori_loop(1, PAIRS - 1, step, jnp.zeros((8, LANES), F32), unroll=2)
    g_ref[0:SIDE, :] = jnp.zeros((SIDE, LANES), BF16)
    g_ref[ROWS - SIDE :, :] = jnp.zeros((SIDE, LANES), BF16)
    g = g_ref[SIDE : ROWS - SIDE, :]
    for a, p in enumerate((p0, p1, p2)):
        for shift in (0, 1):
            start = (1 + shift) * SIDE
            terms_ref[a, :, shift * LANES : (shift + 1) * LANES] = dot(g, p[start : start + ROWS - 2 * SIDE, :], TN)


def middle_kernel(
    s_ref, offset, cot_ref, p0, p1, p2, lines, terms_ref, bias_ref, cot_lines, rows_a, rows_b, rows_c, rows_d, cols_ref,
    hot_ref, half_ref, w_ref, wb_ref, wc_ref,
    g_lines, g_sides, keep_ref, send_ref, own_ref, cell_scr, gt, gb, gc, own_scr, msg,
):
    added = jnp.concatenate([offset[...], offset[...]], axis=1)
    n = rows_a.shape[0]
    many = 4 * n
    cells = dot(hot_ref[:, many:], cols_ref[...])
    for i, ref in enumerate((rows_a, rows_b, rows_c, rows_d)):
        cells = cells + dot(hot_ref[:, i * n : (i + 1) * n], ref[...])
    other = turn(cells)
    upper = half_ref[...] > 0.5
    edge = 2 * SIDE + 4
    as_low = jnp.where(upper, other, cells)
    as_high = jnp.where(upper, cells, other)
    sides = halves(as_low[edge : edge + SIDE], as_high[edge + SIDE : edge + 2 * SIDE])
    odd = iota(cells.shape, 0) % 2 == 1
    cell_scr[...] = jnp.where(odd, as_high, as_low)

    def windows(both):
        return jnp.concatenate([both[0:PAIRS], both[1 : PAIRS + 1]], axis=1)

    def line_of(start):
        even_cells = cell_scr[pl.ds(start, PAIRS + 1, stride=2), :]
        odd_cells = cell_scr[pl.ds(start + 1, PAIRS + 1, stride=2), :]
        return windows(halves(even_cells, odd_cells))

    is_low = low((SIDE, LANES))
    row = iota((SIDE, LANES), 0)
    top = line_of(0)
    bottom = line_of(SIDE + 2)
    moved = (
        jnp.where(row == 0, 0.0, pltpu.roll(sides, 1, 0)),
        sides,
        jnp.where(row == SIDE - 1, 0.0, pltpu.roll(sides, SIDE - 1, 0)),
    )
    lefts = [jnp.where(is_low, m, 0.0) for m in moved]
    rights = [jnp.where(is_low, 0.0, m) for m in moved]
    top_signal = dot(top.astype(BF16), w_ref[0], NT)
    bottom_signal = dot(bottom.astype(BF16), w_ref[2], NT)

    def side_grad(q, columns, lanes):
        signal = s_ref[q * SIDE : (q + 1) * SIDE, :] + added
        for a in range(3):
            signal = signal + dot(columns[a].astype(BF16), w_ref[a, :, lanes], NT)
        signal = signal + jnp.where(row == 0, top_signal[q : q + 1], 0.0)
        signal = signal + jnp.where(row == SIDE - 1, bottom_signal[q : q + 1], 0.0)
        upstream = cot_ref[:, q * LANES : (q + 1) * LANES].astype(F32)
        return slope_times(signal, upstream).astype(BF16).astype(F32)

    end = PAIRS - 1
    g_left = side_grad(0, lefts, slice(0, LANES))
    g_right = side_grad(end, rights, slice(LANES, 2 * LANES))
    pair = iota((PAIRS, LANES), 0)
    ends = jnp.logical_or(pair == 0, pair == end)

    def line_grad(first_row, halo_signal):
        signal = s_ref[pl.ds(first_row, PAIRS, stride=SIDE), :] + added + halo_signal
        upstream = cot_lines[0:PAIRS, :] if first_row == 0 else cot_lines[PAIRS:, :]
        g = jnp.where(ends, 0.0, slope_times(signal, upstream)).astype(BF16).astype(F32)
        r = slice(first_row, first_row + 1)
        return g, jnp.where(pair == 0, g_left[r], jnp.where(pair == end, g_right[r], g))

    inner_top, all_top = line_grad(0, top_signal)
    inner_bottom, all_bottom = line_grad(SIDE - 1, bottom_signal)
    g_lines[0:PAIRS, :] = all_top
    g_lines[PAIRS:, :] = all_bottom
    g_sides[0:SIDE, :] = g_left.astype(BF16)
    g_sides[SIDE:, :] = g_right.astype(BF16)
    border = jnp.concatenate([inner_top, inner_bottom, g_left, g_right], axis=0)
    bias = jnp.sum(bias_ref[...], axis=0, keepdims=True) + jnp.sum(border, axis=0, keepdims=True)
    border = border.astype(BF16)
    kept = [windows(lines[i]) for i in range(4)]
    none = jnp.zeros((SIDE, LANES), F32)
    wide_row = iota((SIDE, 2 * LANES), 0)

    def side_window(a, p, q, columns):
        parts = [p[(q + i) * SIDE : (q + i + 1) * SIDE, :].astype(F32) for i in range(2)]
        window = jnp.concatenate(parts, axis=1) + columns
        if a == 0:
            window = window + jnp.where(wide_row == 0, top[q : q + 1], 0.0)
        if a == 2:
            window = window + jnp.where(wide_row == SIDE - 1, bottom[q : q + 1], 0.0)
        return window

    terms = []
    over = (top, kept[0], kept[1])
    under = (kept[2], kept[3], bottom)
    for a, p in enumerate((p0, p1, p2)):
        window = jnp.concatenate(
            [
                over[a],
                under[a],
                side_window(a, p, 0, jnp.concatenate([lefts[a], none], axis=1)),
                side_window(a, p, end, jnp.concatenate([none, rights[a]], axis=1)),
            ],
            axis=0,
        ).astype(BF16)
        t = terms_ref[a] + dot(border, window, TN)
        terms += [t[:, :LANES], t[:, LANES:]]
    for scr, line in ((gt, all_top), (gb, all_bottom)):
        turned = turn(line)
        scr[...] = jnp.zeros(scr.shape, F32)
        scr[1 : PAIRS + 1, :] = jnp.where(low(line.shape), turned, 0.0)
        scr[0:PAIRS, :] += jnp.where(low(line.shape), 0.0, turned)

    def tap(m, high):
        a, b = m // 3, m % 3
        result = 0.0
        for e in (0, 1):
            w = e + b
            part = terms[2 * a + w // 2][e * CHANNELS : (e + 1) * CHANNELS]
            result = result + (part if (w % 2 == 1) == high else turn(part))
        return result

    total = bias + turn(bias)
    coarse = total.astype(BF16).astype(F32)
    fine = total - coarse
    for t in range(5):
        if t < 4:
            high = tap(2 * t + 1, True)
        else:
            high = jnp.where(row == 0, coarse, jnp.where(row == 1, fine, 0.0))
        msg[t * SIDE : (t + 1) * SIDE, :] = halves(tap(2 * t, False), high)
    core = lax.axis_index("region") & 1
    keep_ref[...] = msg[pl.ds(pl.multiple_of(core * WROWS, WROWS), WROWS), :].astype(BF16)
    send_ref[0:WROWS, :] = msg[pl.ds(pl.multiple_of((1 - core) * WROWS, WROWS), WROWS), :].astype(BF16)

    lines = []
    for src, tap_row in ((gt, 2), (gb, 0)):
        window = jnp.concatenate([src[0:PAIRS, :], src[1 : PAIRS + 1, :]], axis=1).astype(BF16)
        lines.append(dot(window, wb_ref[tap_row]))
    own_scr[pl.ds(0, PAIRS, stride=2), :] = halves(lines[0], turn(lines[1]))
    own_scr[pl.ds(1, PAIRS, stride=2), :] = halves(turn(lines[0]), lines[1])
    own_ref[...] = own_scr[...].astype(BF16)

    gc[...] = jnp.zeros(gc.shape, F32)
    gc[8 : 8 + SIDE, :] = halves(g_left, g_right)
    grads = dot(gc[8:88, :].astype(BF16), wc_ref[0])
    grads = grads + dot(gc[7:87, :].astype(BF16), wc_ref[1])
    grads = grads + dot(gc[6:86, :].astype(BF16), wc_ref[2])
    other = turn(grads)
    lefts = halves(grads, other)
    rights = halves(other, grads)
    cell_scr[...] = jnp.zeros(cell_scr.shape, F32)
    for at, src, first_row, n in (
        (0, lefts, 0, 1), (SIDE + 1, rights, 0, 1), (SIDE + 2, lefts, SIDE + 1, 1), (edge - 1, rights, SIDE + 1, 1),
        (edge, lefts, 1, SIDE), (edge + SIDE, rights, 1, SIDE),
    ):
        cell_scr[at : at + n, :] = src[first_row : first_row + n]
    placed = jnp.where(upper == low(cells.shape), 0.0, cell_scr[...]).astype(BF16)
    send_ref[WROWS:, :] = dot(hot_ref[:, many:], placed, TN).astype(BF16)


def grad_copies_kernel(g_ref, g_lines, g_sides, p0, p1, p2):
    row = iota((SIDE, LANES), 0)
    left = g_sides[0:SIDE, :].astype(F32)
    right = g_sides[SIDE:, :].astype(F32)

    def load(q):
        g = g_ref[block(q), :].astype(F32)
        g = jnp.where(row == 0, g_lines[pl.ds(q, 1), :], g)
        g = jnp.where(row == SIDE - 1, g_lines[pl.ds(PAIRS + q, 1), :], g)
        return jnp.where(q == 0, left, jnp.where(q == PAIRS - 1, right, g))

    shifted_copies(load, p0, p1, p2)


def inner_kernel(p0, p1, p2, wb_ref, out_ref):
    out_ref[...] = product(p0, p1, p2, wb_ref, ((1,), (0,)))


def added_weights(parts):
    terms = [part[0:WROWS, :].astype(F32) for part in parts]
    while len(terms) > 1:
        terms = [terms[i] + terms[i + 1] for i in range(0, len(terms), 2)]
    tail = terms[0][WROWS - SIDE :]
    return terms[0], tail + pltpu.roll(tail, SIDE - 1, 0)


def bias_lanes(shape):
    return jnp.logical_and(jnp.logical_not(low(shape)), (lax.axis_index("region") & 1) == 1)


def put_weights(parts, out):
    total, whole = added_weights(parts)
    out[0 : WROWS - SIDE, :] = total[: WROWS - SIDE].astype(BF16)
    row = iota(whole.shape, 0)
    coarse = whole.astype(BF16).astype(F32)
    fine = pltpu.roll(whole - coarse, 1, 0)
    out[WROWS - SIDE : WROWS, :] = jnp.where(
        bias_lanes(whole.shape),
        jnp.where(row == 0, coarse, jnp.where(row == 1, fine, 0.0)),
        total[WROWS - SIDE :],
    ).astype(BF16)


def first_join_kernel(mine, other, *rest):
    extra, out = rest[:-1], rest[-1]
    put_weights((mine, other), out)
    if extra:
        out[WROWS:, :] = extra[0][...]


def join_kernel(*refs):
    parts, out = refs[:-1], refs[-1]
    put_weights(parts, out)
    n = parts[0].shape[0] - WROWS
    for i, part in enumerate(parts):
        out[WROWS + i * n : WROWS + (i + 1) * n, :] = part[WROWS:, :]


def close_kernel(scale, *refs):
    parts, out = refs[:-1], refs[-1]
    total, whole = added_weights(parts)
    out[0 : WROWS - SIDE, :] = total[: WROWS - SIDE] * scale
    out[WROWS - SIDE :, :] = jnp.where(bias_lanes(whole.shape), whole, total[WROWS - SIDE :]) * scale


def weight_kernel(mine, other, wt_ref, bias_ref):
    odd = (lax.axis_index("region") & 1) == 1
    a, b = mine[...], other[...]
    full = jnp.concatenate([jnp.where(odd, b, a), jnp.where(odd, a, b)], axis=0)
    for t in range(4):
        wt_ref[:, t * LANES : (t + 1) * LANES] = full[t * SIDE : (t + 1) * SIDE]
    wt_ref[:, 4 * LANES :] = full[4 * SIDE :, :CHANNELS]
    bias_ref[...] = turn(full[4 * SIDE : 4 * SIDE + 8])[0:1, :CHANNELS]


def last_kernel(row_a, row_b, row_c, row_d, inner, pick, *rest):
    side_refs, grad_ref = rest[:-1], rest[-1]
    n = row_a.shape[0] - WROWS
    got = 0.0
    for i, ref in enumerate((row_a, row_b, row_c, row_d)):
        got = got + dot(pick[:, i * n : (i + 1) * n], ref[WROWS:, :])
    a, b, c, d = (got[i * SIDE : (i + 1) * SIDE] for i in range(4))
    rims = halves(a + turn(b), turn(c) + d)
    sides = side_refs[0][side_refs[0].shape[0] - SIDE :, :].astype(F32)
    for ref in side_refs[1:]:
        sides = sides + ref[...].astype(F32)
    row = iota((SIDE, LANES), 0)
    is_low = low((SIDE, LANES))
    for q in range(PAIRS):
        v = inner[q * SIDE : (q + 1) * SIDE, :]
        v = v + jnp.where(row == 0, rims[q : q + 1], jnp.where(row == SIDE - 1, rims[PAIRS + q : PAIRS + q + 1], 0.0))
        if q == 0:
            v = v + jnp.where(is_low, sides, 0.0)
        if q == PAIRS - 1:
            v = v + jnp.where(is_low, 0.0, sides)
        grad_ref[:, q * LANES : (q + 1) * LANES] = v.astype(BF16)


def swap(x, axis, k):
    n = lax.axis_size(axis)
    return lax.ppermute(x, axis, [(i, i ^ k) for i in range(n)])


def shift(x, axis, by):
    n = lax.axis_size(axis)
    return lax.ppermute(x, axis, [(i, (i + by) % n) for i in range(n)])


def steps_of(n):
    ks = []
    k = n // 2
    while k:
        ks.append(k)
        k //= 2
    return ks


def rounds_of(owners):
    count = owners.bit_length() - 1
    pairs = [(bit, bit + 1) for bit in range(count % 2, count, 2)][::-1]
    if count % 2:
        pairs = [tuple(b - 1 for b in p) for p in pairs]
        return [(count - 1,)] + pairs
    return pairs


def slot_bits(owners):
    bits = [bit for bits in rounds_of(owners) for bit in bits]
    return [(bit, to) for to, bit in enumerate(bits)]


def exchange(x, bits):
    ks = [sum(1 << bits[i] for i in range(len(bits)) if (n >> i) & 1) for n in range(1, 1 << len(bits))]
    got = {k: swap(x, "patch", k) for k in ks[::-1]}
    return [got[k] for k in ks]


def body(fine_input, fine_weight, fine_bias, cotangent, halo_index):
    owners = lax.axis_size("patch")
    regions = lax.axis_size("region")
    rounds = rounds_of(owners)
    blocks = 1 if regions == 2 else 2
    x = fine_input.reshape(SIDE, SIDE * CHANNELS)
    cot = cotangent.reshape(SIDE, SIDE * CHANNELS)
    pair = ((ROWS + SIDE, LANES), BF16)

    rows, cols = call(rim_kernel, [((SIDE, LANES), BF16)] * 2, x, scratch=[pltpu.VMEM((SIDE, LANES), F32)])
    if regions == 2:
        cols = swap(cols, "region", 1)
    else:
        cols = jnp.concatenate([shift(cols, "region", 1), shift(cols, "region", -1)], axis=0)
    count = 272
    both = ((ROWS, LANES), F32)
    work = dict(flops=2 * ROWS * 768 * 128, moved=3 * 2**20)

    others = exchange(rows, rounds[0])
    *copies, lines = call(copies_kernel, [pair] * 3 + [((4, 40, LANES), F32)], x, moved=2 * 2**20)
    forward, backward, columns = call(
        weights_kernel,
        [((3, LANES, 2 * LANES), BF16), ((3, 2 * LANES, LANES), BF16), ((3, LANES, LANES), BF16)],
        fine_weight.T,
    )
    signal = call(
        signal_kernel, [both], *copies, forward, **work,
    )[0]
    offset = fine_bias.reshape(1, CHANNELS)
    others, signal, index, offset = lax.optimization_barrier((others, signal, halo_index, offset))
    for bits in rounds[1:]:
        size = ((len(others) + 1) * rows.shape[0], LANES)
        rows = call(rows_kernel, [(size, BF16)], rows, *others)[0]
        others = exchange(rows, bits)
    hot, half_mask = call(
        functools.partial(plan_kernel, owners, regions, blocks),
        [((count, (owners + blocks) * SIDE), BF16), ((count, LANES), F32)],
        index, scratch=[pltpu.VMEM((8, 384), F32)],
    )
    inside = call(
        inside_kernel,
        [((ROWS, LANES), BF16), ((3, LANES, 2 * LANES), F32), ((8, LANES), F32), ((SIDE, LANES), F32)],
        signal, offset, cot, *copies, **work,
    )
    others, hot, half_mask, inside = lax.optimization_barrier((others, hot, half_mask, inside))
    grad, *inside = inside

    line = pltpu.VMEM((40, LANES), F32)
    g_lines, g_sides, message, sent, own_rows = call(
        middle_kernel,
        [
            ((SIDE, LANES), F32), ((2 * SIDE, LANES), BF16),
            ((WROWS, LANES), BF16), ((WROWS + blocks * SIDE, LANES), BF16), ((SIDE, LANES), BF16),
        ],
        signal, offset, cot, *copies, lines, *inside, rows, *others, cols, hot, half_mask, forward, backward, columns,
        scratch=[
            pltpu.VMEM((count, LANES), F32), line, line,
            pltpu.VMEM((96, LANES), F32), pltpu.VMEM((SIDE, LANES), F32), pltpu.VMEM((2 * WROWS, LANES), F32),
        ],
        moved=2**20,
    )

    if regions > 2:
        upper, lower = sent[WROWS + SIDE :], sent[WROWS : WROWS + SIDE]
        sides = [shift(upper, "region", 1), shift(lower, "region", -1)]
        sent = sent[:WROWS]
    other = swap(sent, "region", 1)
    if regions == 2:
        sides = [other]
    far = [k for k in steps_of(regions) if k > 1]
    for k in [1] + far:
        extra = () if k != ([1] + far)[-1] else (own_rows,)
        size = (WROWS + SIDE * len(extra), LANES)
        got = other if k == 1 else swap(message, "region", k)
        message = call(first_join_kernel, [(size, BF16)], message, got, *extra)[0]
    beside = [grad, g_lines, g_sides]
    for bits in rounds[:-1]:
        message, beside, index = lax.optimization_barrier((message, beside, index))
        others = exchange(message, bits)
        if bits == rounds[-2]:
            pick = call(functools.partial(pick_kernel, owners), [((4 * SIDE, owners * SIDE), BF16)], index)[0]
            beside = call(grad_copies_kernel, [pair] * 3, *beside, moved=2 * 2**20)
            others, beside, pick = lax.optimization_barrier((others, beside, pick))
        size = (WROWS + (len(others) + 1) * (message.shape[0] - WROWS), LANES)
        message = call(join_kernel, [(size, BF16)], message, *others)[0]
    message, beside = lax.optimization_barrier((message, beside))
    others = exchange(message, rounds[-1])
    beside = call(inner_kernel, [both], *beside, backward, **work)[0]
    others, beside = lax.optimization_barrier((others, beside))
    scale = 1.0 / math.sqrt(regions * owners * SIDE * SIDE)
    part = call(functools.partial(close_kernel, scale), [((WROWS, LANES), F32)], message, *others)[0]
    other_part = swap(part, "region", 1)
    input_grad = call(
        last_kernel, [((SIDE, SIDE * CHANNELS), BF16)], message, *others, beside, pick, *sides, moved=2 * 2**20
    )[0]
    weight_grad, bias_grad = call(
        weight_kernel, [((CHANNELS, 9 * CHANNELS), F32), ((1, CHANNELS), F32)], part, other_part
    )
    return input_grad.reshape(1, SIDE, SIDE * CHANNELS), weight_grad.T, bias_grad.reshape(CHANNELS)


def solution(mesh):
    placed = (
        P(("region", "patch"), None, None),
        P(),
        P(),
        P(("region", "patch"), None, None),
        P("region", None),
    )
    return jax.shard_map(
        body,
        mesh=mesh,
        in_specs=placed,
        out_specs=(P(("region", "patch"), None, None), P(), P()),
        check_vma=False,
    )
```

```python
import functools
import math

import jax
import jax.numpy as jnp
from jax import lax
from jax.experimental import pallas as pl
from jax.experimental.pallas import tpu as pltpu
from jax.sharding import PartitionSpec as P

CHANNELS = 64
SIDE = 64
PAIRS = SIDE // 2
LANES = 2 * CHANNELS
ROWS = PAIRS * SIDE
WROWS = 5 * CHANNELS // 2
FAR_ORDER = (0, 2, 1)
NEAR_ORDER = (0, 1, 2)
F32 = jnp.float32
BF16 = jnp.bfloat16


def call(kernel, outs, *args, scratch=(), flops=0, moved=0, limit=48):
    whole = pl.BlockSpec(memory_space=pltpu.VMEM)
    shapes = [jax.ShapeDtypeStruct(s, d) for s, d in outs]
    return pl.pallas_call(
        kernel,
        out_shape=shapes,
        in_specs=[whole] * len(args),
        out_specs=[whole] * len(outs),
        scratch_shapes=list(scratch),
        compiler_params=pltpu.CompilerParams(vmem_limit_bytes=limit * 2**20),
        cost_estimate=pl.CostEstimate(flops=flops, bytes_accessed=moved, transcendentals=0),
    )(*args)


def iota(shape, dim):
    return lax.broadcasted_iota(jnp.int32, shape, dim)


def low(shape):
    return iota(shape, len(shape) - 1) < CHANNELS


def turn(x):
    return pltpu.roll(x, CHANNELS, 1)


def tile(q):
    return pl.ds(pl.multiple_of(q * LANES, LANES), LANES)


def block(q):
    return pl.ds(pl.multiple_of(q * SIDE, SIDE), SIDE)


def dot(a, b, dims=((1,), (0,))):
    return lax.dot_general(a, b, (dims, ((), ())), preferred_element_type=F32)


NT = ((1,), (1,))
TN = ((0,), (0,))


def shifted_copies(load, p0, p1, p2, lines=None):
    is_low = low((SIDE, LANES))
    row = iota((SIDE, LANES), 0)

    def put(q, before, now):
        v = jnp.where(is_low, before, now)
        p1[block(q), :] = v.astype(BF16)
        if lines is not None:
            for i, r in enumerate((0, 1, SIDE - 2, SIDE - 1)):
                lines[i, pl.ds(q, 1), :] = v[r : r + 1]
        p0[block(q), :] = jnp.where(row == 0, 0.0, pltpu.roll(v, 1, 0)).astype(BF16)
        p2[block(q), :] = jnp.where(row == SIDE - 1, 0.0, pltpu.roll(v, SIDE - 1, 0)).astype(BF16)

    def step(q, before):
        now = turn(load(q))
        put(q, before, now)
        return now

    zero = jnp.zeros((SIDE, LANES), F32)
    last = lax.fori_loop(0, PAIRS, step, zero, unroll=4)
    put(PAIRS, last, zero)


def product(p0, p1, p2, w_ref, dims):
    total = None
    for a, p in enumerate((p0, p1, p2)):
        window = jnp.concatenate([p[0:ROWS, :], p[SIDE : ROWS + SIDE, :]], axis=1)
        term = dot(window, w_ref[a], dims)
        total = term if total is None else total + term
    return total


def rim_kernel(x_ref, rows_ref, cols_ref, scr):
    for q in range(PAIRS):
        lanes = slice(q * LANES, (q + 1) * LANES)
        scr[q : q + 1, :] = x_ref[0:16, lanes].astype(F32)[0:1]
        scr[PAIRS + q : PAIRS + q + 1, :] = x_ref[SIDE - 16 : SIDE, lanes].astype(F32)[15:16]
    rows_ref[...] = scr[...].astype(BF16)
    first = x_ref[:, 0:LANES].astype(F32)
    last = x_ref[:, (PAIRS - 1) * LANES :].astype(F32)
    cols_ref[...] = halves(first, last).astype(BF16)


def rows_kernel(*refs):
    parts, out = by_distance(refs[:-1], FAR_ORDER), refs[-1]
    n = parts[0].shape[0]
    for i, part in enumerate(parts):
        out[i * n : (i + 1) * n, :] = part[...]


def bits_moved(v, pairs):
    result = jnp.zeros_like(v)
    for from_bit, to_bit in pairs:
        result = result | (((v >> from_bit) & 1) << to_bit)
    return result


def plan_kernel(owners, regions, blocks, index_ref, hot_ref, half_ref, scr):
    owner = lax.axis_index("patch")
    region = lax.axis_index("region")
    bits = owners.bit_length() - 1
    index = index_ref[pl.ds(owner, 1), :]
    source, within = index >> 8, index & 255
    slot = bits_moved((source & (owners - 1)) ^ owner, slot_bits(owners))
    row = within & (SIDE - 1)
    if blocks == 2:
        row = row + jnp.where((((source >> bits) - region + regions) & (regions - 1)) == 1, SIDE, 0)
    is_row = within < 2 * SIDE
    place = jnp.where(is_row, slot * SIDE + (within >> 1), owners * SIDE + row)
    half = jnp.where(is_row, within & 1, (within >> 6) & 1)
    count = index.shape[1]
    scr[...] = jnp.full(scr.shape, -1.0, F32)
    scr[0:1, 0:count] = place.astype(F32)
    scr[1:2, 0:count] = half.astype(F32)
    column = jnp.transpose(scr[...])[0 : hot_ref.shape[0]]
    half_ref[...] = jnp.broadcast_to(column[:, 1:2], half_ref.shape)
    place = column[:, 0:1].astype(jnp.int32)
    for c in range(0, hot_ref.shape[1], LANES):
        n = min(LANES, hot_ref.shape[1] - c)
        hot_ref[:, c : c + n] = (place == iota((hot_ref.shape[0], n), 1) + c).astype(F32).astype(BF16)


def pick_kernel(owners, index_ref, pick_ref):
    owner, region = lax.axis_index("patch"), lax.axis_index("region")
    base = (region * owners + owner) * 4 * SIDE
    want = 2 * iota((SIDE, LANES), 0)
    for t in range(owners // 2):
        pair = []
        for slot in (2 * t, 2 * t + 1):
            relative = sum(1 << bit for bit, to in slot_bits(owners) if (slot >> to) & 1)
            line = index_ref[pl.ds(owner ^ relative, 1), :]
            pair.append((line[:, 1 : SIDE + 1], line[:, SIDE + 3 : 2 * SIDE + 3]))
        for s in range(2):
            both = jnp.concatenate([pair[0][s], pair[1][s]], axis=1) - base
            for e in range(2):
                hit = (both == want + e).astype(F32).astype(BF16)
                n = 2 * e + s
                pick_ref[n * SIDE : (n + 1) * SIDE, t * LANES : (t + 1) * LANES] = hit


def weights_kernel(wt_ref, w_ref, wb_ref, wc_ref):
    wide = [wt_ref[:, t * LANES : (t + 1) * LANES].astype(F32) for t in range(4)]
    tail = wt_ref[:, 4 * LANES :].astype(F32)
    wide.append(jnp.concatenate([tail, tail], axis=1))

    def at(a, b, high):
        m = 3 * a + b
        v = wide[m // 2]
        return v if m == 8 or (m % 2 == 1) == high else turn(v)

    def pair(a, left, right):
        zero = jnp.zeros((CHANNELS, LANES), F32)
        lo = zero if left is None else at(a, left, False)
        hi = zero if right is None else at(a, right, True)
        return halves(lo, hi).astype(BF16)

    c = CHANNELS
    for a in range(3):
        w_ref[a, 0:c, 0:LANES] = pair(a, 0, 1)
        w_ref[a, 0:c, LANES:] = pair(a, 2, None)
        w_ref[a, c:, 0:LANES] = pair(a, None, 0)
        w_ref[a, c:, LANES:] = pair(a, 1, 2)
        for w, (left, right) in enumerate(((2, None), (1, 2), (0, 1), (None, 0))):
            wb_ref[2 - a, w * c : (w + 1) * c, :] = pair(a, left, right)
        wc_ref[a, 0:c, :] = pair(a, 0, None)
        wc_ref[a, c:, :] = pair(a, None, 2)


def copies_kernel(x_ref, p0, p1, p2, lines):
    shifted_copies(lambda q: x_ref[:, tile(q)].astype(F32), p0, p1, p2, lines)


def signal_kernel(p0, p1, p2, w_ref, s_ref):
    s_ref[...] = product(p0, p1, p2, w_ref, NT)


def slope_times(signal, upstream):
    sigma = 1.0 / (1.0 + jnp.exp(-signal))
    return upstream * (sigma * (1.0 + signal * (1.0 - sigma)))


def halves(even, odd):
    return jnp.where(low(even.shape), even, odd)


def inside_kernel(s_ref, offset, cot_ref, p0, p1, p2, g_ref, terms_ref, bias_ref, cot_lines):
    row = iota((SIDE, LANES), 0)
    border = jnp.logical_or(row == 0, row == SIDE - 1)
    added = jnp.concatenate([offset[...], offset[...]], axis=1)

    def step(q, bias):
        upstream = cot_ref[:, tile(q)].astype(F32)
        g = jnp.where(border, 0.0, slope_times(s_ref[block(q), :] + added, upstream)).astype(BF16)
        g_ref[block(q), :] = g
        cot_lines[pl.ds(q, 1), :] = upstream[0:1]
        cot_lines[pl.ds(PAIRS + q, 1), :] = upstream[SIDE - 1 :]
        return bias + jnp.sum(g.astype(F32).reshape(8, 8, LANES), axis=0)

    cot_lines[...] = jnp.zeros(cot_lines.shape, F32)
    bias_ref[...] = lax.fori_loop(1, PAIRS - 1, step, jnp.zeros((8, LANES), F32), unroll=2)
    g_ref[0:SIDE, :] = jnp.zeros((SIDE, LANES), BF16)
    g_ref[ROWS - SIDE :, :] = jnp.zeros((SIDE, LANES), BF16)
    g = g_ref[SIDE : ROWS - SIDE, :]
    for a, p in enumerate((p0, p1, p2)):
        for shift in (0, 1):
            start = (1 + shift) * SIDE
            terms_ref[a, :, shift * LANES : (shift + 1) * LANES] = dot(g, p[start : start + ROWS - 2 * SIDE, :], TN)


def middle_kernel(
    s_ref, offset, cot_ref, p0, p1, p2, lines, terms_ref, bias_ref, cot_lines, rows_a, rows_b, rows_c, rows_d, cols_ref,
    hot_ref, half_ref, w_ref, wc_ref,
    g_lines, g_sides, keep_ref, send_ref, cell_scr, gc, msg,
):
    added = jnp.concatenate([offset[...], offset[...]], axis=1)
    n = rows_a.shape[0]
    many = 4 * n
    cells = dot(hot_ref[:, many:], cols_ref[...])
    for i, ref in enumerate(by_distance((rows_a, rows_b, rows_c, rows_d), NEAR_ORDER)):
        cells = cells + dot(hot_ref[:, i * n : (i + 1) * n], ref[...])
    other = turn(cells)
    upper = half_ref[...] > 0.5
    edge = 2 * SIDE + 4
    as_low = jnp.where(upper, other, cells)
    as_high = jnp.where(upper, cells, other)
    sides = halves(as_low[edge : edge + SIDE], as_high[edge + SIDE : edge + 2 * SIDE])
    odd = iota(cells.shape, 0) % 2 == 1
    cell_scr[...] = jnp.where(odd, as_high, as_low)

    def windows(both):
        return jnp.concatenate([both[0:PAIRS], both[1 : PAIRS + 1]], axis=1)

    def line_of(start):
        even_cells = cell_scr[pl.ds(start, PAIRS + 1, stride=2), :]
        odd_cells = cell_scr[pl.ds(start + 1, PAIRS + 1, stride=2), :]
        return windows(halves(even_cells, odd_cells))

    is_low = low((SIDE, LANES))
    row = iota((SIDE, LANES), 0)
    top = line_of(0)
    bottom = line_of(SIDE + 2)
    moved = (
        jnp.where(row == 0, 0.0, pltpu.roll(sides, 1, 0)),
        sides,
        jnp.where(row == SIDE - 1, 0.0, pltpu.roll(sides, SIDE - 1, 0)),
    )
    lefts = [jnp.where(is_low, m, 0.0) for m in moved]
    rights = [jnp.where(is_low, 0.0, m) for m in moved]
    top_signal = dot(top.astype(BF16), w_ref[0], NT)
    bottom_signal = dot(bottom.astype(BF16), w_ref[2], NT)

    def side_grad(q, columns, lanes):
        signal = s_ref[q * SIDE : (q + 1) * SIDE, :] + added
        for a in range(3):
            signal = signal + dot(columns[a].astype(BF16), w_ref[a, :, lanes], NT)
        signal = signal + jnp.where(row == 0, top_signal[q : q + 1], 0.0)
        signal = signal + jnp.where(row == SIDE - 1, bottom_signal[q : q + 1], 0.0)
        upstream = cot_ref[:, q * LANES : (q + 1) * LANES].astype(F32)
        return slope_times(signal, upstream).astype(BF16).astype(F32)

    end = PAIRS - 1
    g_left = side_grad(0, lefts, slice(0, LANES))
    g_right = side_grad(end, rights, slice(LANES, 2 * LANES))
    pair = iota((PAIRS, LANES), 0)
    ends = jnp.logical_or(pair == 0, pair == end)

    def line_grad(first_row, halo_signal):
        signal = s_ref[pl.ds(first_row, PAIRS, stride=SIDE), :] + added + halo_signal
        upstream = cot_lines[0:PAIRS, :] if first_row == 0 else cot_lines[PAIRS:, :]
        g = jnp.where(ends, 0.0, slope_times(signal, upstream)).astype(BF16).astype(F32)
        r = slice(first_row, first_row + 1)
        return g, jnp.where(pair == 0, g_left[r], jnp.where(pair == end, g_right[r], g))

    inner_top, all_top = line_grad(0, top_signal)
    inner_bottom, all_bottom = line_grad(SIDE - 1, bottom_signal)
    g_lines[0:PAIRS, :] = all_top
    g_lines[PAIRS:, :] = all_bottom
    g_sides[0:SIDE, :] = g_left.astype(BF16)
    g_sides[SIDE:, :] = g_right.astype(BF16)
    border = jnp.concatenate([inner_top, inner_bottom, g_left, g_right], axis=0)
    bias = jnp.sum(bias_ref[...], axis=0, keepdims=True) + jnp.sum(border, axis=0, keepdims=True)
    border = border.astype(BF16)
    kept = [windows(lines[i]) for i in range(4)]
    none = jnp.zeros((SIDE, LANES), F32)
    wide_row = iota((SIDE, 2 * LANES), 0)

    def side_window(a, p, q, columns):
        parts = [p[(q + i) * SIDE : (q + i + 1) * SIDE, :].astype(F32) for i in range(2)]
        window = jnp.concatenate(parts, axis=1) + columns
        if a == 0:
            window = window + jnp.where(wide_row == 0, top[q : q + 1], 0.0)
        if a == 2:
            window = window + jnp.where(wide_row == SIDE - 1, bottom[q : q + 1], 0.0)
        return window

    terms = []
    over = (top, kept[0], kept[1])
    under = (kept[2], kept[3], bottom)
    for a, p in enumerate((p0, p1, p2)):
        window = jnp.concatenate(
            [
                over[a],
                under[a],
                side_window(a, p, 0, jnp.concatenate([lefts[a], none], axis=1)),
                side_window(a, p, end, jnp.concatenate([none, rights[a]], axis=1)),
            ],
            axis=0,
        ).astype(BF16)
        t = terms_ref[a] + dot(border, window, TN)
        terms += [t[:, :LANES], t[:, LANES:]]
    def tap(m, high):
        a, b = m // 3, m % 3
        result = 0.0
        for e in (0, 1):
            w = e + b
            part = terms[2 * a + w // 2][e * CHANNELS : (e + 1) * CHANNELS]
            result = result + (part if (w % 2 == 1) == high else turn(part))
        return result

    total = bias + turn(bias)
    coarse = total.astype(BF16).astype(F32)
    fine = total - coarse
    for t in range(5):
        if t < 4:
            high = tap(2 * t + 1, True)
        else:
            high = jnp.where(row == 0, coarse, jnp.where(row == 1, fine, 0.0))
        msg[t * SIDE : (t + 1) * SIDE, :] = halves(tap(2 * t, False), high)
    core = lax.axis_index("region") & 1
    keep_ref[...] = msg[pl.ds(pl.multiple_of(core * WROWS, WROWS), WROWS), :].astype(BF16)
    send_ref[0:WROWS, :] = msg[pl.ds(pl.multiple_of((1 - core) * WROWS, WROWS), WROWS), :].astype(BF16)

    gc[...] = jnp.zeros(gc.shape, F32)
    gc[8 : 8 + SIDE, :] = halves(g_left, g_right)
    grads = dot(gc[8:88, :].astype(BF16), wc_ref[0])
    grads = grads + dot(gc[7:87, :].astype(BF16), wc_ref[1])
    grads = grads + dot(gc[6:86, :].astype(BF16), wc_ref[2])
    other = turn(grads)
    lefts = halves(grads, other)
    rights = halves(other, grads)
    cell_scr[...] = jnp.zeros(cell_scr.shape, F32)
    for at, src, first_row, n in (
        (0, lefts, 0, 1), (SIDE + 1, rights, 0, 1), (SIDE + 2, lefts, SIDE + 1, 1), (edge - 1, rights, SIDE + 1, 1),
        (edge, lefts, 1, SIDE), (edge + SIDE, rights, 1, SIDE),
    ):
        cell_scr[at : at + n, :] = src[first_row : first_row + n]
    placed = jnp.where(upper == low(cells.shape), 0.0, cell_scr[...]).astype(BF16)
    send_ref[WROWS:, :] = dot(hot_ref[:, many:], placed, TN).astype(BF16)


def halo_rows_kernel(g_lines, wb_ref, own_ref, gt, gb, own_scr):
    all_top, all_bottom = g_lines[0:PAIRS, :], g_lines[PAIRS:, :]
    for scr, line in ((gt, all_top), (gb, all_bottom)):
        turned = turn(line)
        scr[...] = jnp.zeros(scr.shape, F32)
        scr[1 : PAIRS + 1, :] = jnp.where(low(line.shape), turned, 0.0)
        scr[0:PAIRS, :] += jnp.where(low(line.shape), 0.0, turned)
    lines = []
    for src, tap_row in ((gt, 2), (gb, 0)):
        window = jnp.concatenate([src[0:PAIRS, :], src[1 : PAIRS + 1, :]], axis=1).astype(BF16)
        lines.append(dot(window, wb_ref[tap_row]))
    own_scr[pl.ds(0, PAIRS, stride=2), :] = halves(lines[0], turn(lines[1]))
    own_scr[pl.ds(1, PAIRS, stride=2), :] = halves(turn(lines[0]), lines[1])
    own_ref[...] = own_scr[...].astype(BF16)


def grad_copies_kernel(g_ref, g_lines, g_sides, p0, p1, p2):
    row = iota((SIDE, LANES), 0)
    left = g_sides[0:SIDE, :].astype(F32)
    right = g_sides[SIDE:, :].astype(F32)

    def load(q):
        g = g_ref[block(q), :].astype(F32)
        g = jnp.where(row == 0, g_lines[pl.ds(q, 1), :], g)
        g = jnp.where(row == SIDE - 1, g_lines[pl.ds(PAIRS + q, 1), :], g)
        return jnp.where(q == 0, left, jnp.where(q == PAIRS - 1, right, g))

    shifted_copies(load, p0, p1, p2)


def inner_kernel(p0, p1, p2, wb_ref, out_ref):
    out_ref[...] = product(p0, p1, p2, wb_ref, ((1,), (0,)))


def added_weights(parts):
    terms = [part[0:WROWS, :].astype(F32) for part in parts]
    while len(terms) > 1:
        terms = [terms[i] + terms[i + 1] for i in range(0, len(terms), 2)]
    tail = terms[0][WROWS - SIDE :]
    return terms[0], tail + pltpu.roll(tail, SIDE - 1, 0)


def bias_lanes(shape):
    return jnp.logical_and(jnp.logical_not(low(shape)), (lax.axis_index("region") & 1) == 1)


def put_weights(parts, out):
    total, whole = added_weights(parts)
    out[0 : WROWS - SIDE, :] = total[: WROWS - SIDE].astype(BF16)
    row = iota(whole.shape, 0)
    coarse = whole.astype(BF16).astype(F32)
    fine = pltpu.roll(whole - coarse, 1, 0)
    out[WROWS - SIDE : WROWS, :] = jnp.where(
        bias_lanes(whole.shape),
        jnp.where(row == 0, coarse, jnp.where(row == 1, fine, 0.0)),
        total[WROWS - SIDE :],
    ).astype(BF16)


def first_join_kernel(mine, other, *rest):
    extra, out = rest[:-1], rest[-1]
    put_weights((mine, other), out)
    if extra:
        out[WROWS:, :] = extra[0][...]


def join_kernel(*refs):
    parts, out = by_distance(refs[:-1], FAR_ORDER), refs[-1]
    put_weights(parts, out)
    n = parts[0].shape[0] - WROWS
    for i, part in enumerate(parts):
        out[WROWS + i * n : WROWS + (i + 1) * n, :] = part[WROWS:, :]


def close_kernel(scale, *refs):
    parts, out = by_distance(refs[:-1], NEAR_ORDER), refs[-1]
    total, whole = added_weights(parts)
    out[0 : WROWS - SIDE, :] = total[: WROWS - SIDE] * scale
    out[WROWS - SIDE :, :] = jnp.where(bias_lanes(whole.shape), whole, total[WROWS - SIDE :]) * scale


def weight_kernel(mine, other, wt_ref, bias_ref):
    odd = (lax.axis_index("region") & 1) == 1
    a, b = mine[...], other[...]
    full = jnp.concatenate([jnp.where(odd, b, a), jnp.where(odd, a, b)], axis=0)
    for t in range(4):
        wt_ref[:, t * LANES : (t + 1) * LANES] = full[t * SIDE : (t + 1) * SIDE]
    wt_ref[:, 4 * LANES :] = full[4 * SIDE :, :CHANNELS]
    bias_ref[...] = turn(full[4 * SIDE : 4 * SIDE + 8])[0:1, :CHANNELS]


def last_kernel(row_a, row_b, row_c, row_d, inner, pick, *rest):
    side_refs, grad_ref = rest[:-1], rest[-1]
    n = row_a.shape[0] - WROWS
    got = 0.0
    for i, ref in enumerate(by_distance((row_a, row_b, row_c, row_d), NEAR_ORDER)):
        got = got + dot(pick[:, i * n : (i + 1) * n], ref[WROWS:, :])
    a, b, c, d = (got[i * SIDE : (i + 1) * SIDE] for i in range(4))
    rims = halves(a + turn(b), turn(c) + d)
    sides = side_refs[0][side_refs[0].shape[0] - SIDE :, :].astype(F32)
    for ref in side_refs[1:]:
        sides = sides + ref[...].astype(F32)
    row = iota((SIDE, LANES), 0)
    is_low = low((SIDE, LANES))
    for q in range(PAIRS):
        v = inner[q * SIDE : (q + 1) * SIDE, :]
        v = v + jnp.where(row == 0, rims[q : q + 1], jnp.where(row == SIDE - 1, rims[PAIRS + q : PAIRS + q + 1], 0.0))
        if q == 0:
            v = v + jnp.where(is_low, sides, 0.0)
        if q == PAIRS - 1:
            v = v + jnp.where(is_low, 0.0, sides)
        grad_ref[:, q * LANES : (q + 1) * LANES] = v.astype(BF16)


def swap(x, axis, k):
    n = lax.axis_size(axis)
    return lax.ppermute(x, axis, [(i, i ^ k) for i in range(n)])


def shift(x, axis, by):
    n = lax.axis_size(axis)
    return lax.ppermute(x, axis, [(i, (i + by) % n) for i in range(n)])


def steps_of(n):
    ks = []
    k = n // 2
    while k:
        ks.append(k)
        k //= 2
    return ks


def rounds_of(owners):
    count = owners.bit_length() - 1
    pairs = [(bit, bit + 1) for bit in range(count % 2, count, 2)][::-1]
    if count % 2:
        pairs = [tuple(b - 1 for b in p) for p in pairs]
        return [(count - 1,)] + pairs
    return pairs


def slot_bits(owners):
    bits = [bit for bits in rounds_of(owners) for bit in bits]
    return [(bit, to) for to, bit in enumerate(bits)]


def exchange(x, bits, order):
    ks = [sum(1 << bits[i] for i in range(len(bits)) if (n >> i) & 1) for n in range(1, 1 << len(bits))]
    return [swap(x, "patch", ks[i]) for i in order if i < len(ks)]


def by_distance(parts, order):
    places = [i for i in order if i < len(parts) - 1]
    return [parts[0]] + [parts[1 + places.index(i)] for i in range(len(places))]


def body(fine_input, fine_weight, fine_bias, cotangent, halo_index):
    owners = lax.axis_size("patch")
    regions = lax.axis_size("region")
    rounds = rounds_of(owners)
    blocks = 1 if regions == 2 else 2
    x = fine_input.reshape(SIDE, SIDE * CHANNELS)
    cot = cotangent.reshape(SIDE, SIDE * CHANNELS)
    pair = ((ROWS + SIDE, LANES), BF16)

    rows, cols = call(rim_kernel, [((SIDE, LANES), BF16)] * 2, x, scratch=[pltpu.VMEM((SIDE, LANES), F32)])
    if regions == 2:
        cols = swap(cols, "region", 1)
    else:
        cols = jnp.concatenate([shift(cols, "region", 1), shift(cols, "region", -1)], axis=0)
    count = 272
    both = ((ROWS, LANES), F32)
    work = dict(flops=2 * ROWS * 768 * 128, moved=3 * 2**20)

    others = exchange(rows, rounds[0], FAR_ORDER)
    *copies, lines = call(copies_kernel, [pair] * 3 + [((4, 40, LANES), F32)], x, moved=2 * 2**20)
    forward, backward, columns = call(
        weights_kernel,
        [((3, LANES, 2 * LANES), BF16), ((3, 2 * LANES, LANES), BF16), ((3, LANES, LANES), BF16)],
        fine_weight.T,
    )
    signal = call(
        signal_kernel, [both], *copies, forward, **work,
    )[0]
    offset = fine_bias.reshape(1, CHANNELS)
    others, signal, index, offset = lax.optimization_barrier((others, signal, halo_index, offset))
    for bits in rounds[1:]:
        size = ((len(others) + 1) * rows.shape[0], LANES)
        rows = call(rows_kernel, [(size, BF16)], rows, *others)[0]
        others = exchange(rows, bits, NEAR_ORDER if bits == rounds[-1] else FAR_ORDER)
    hot, half_mask = call(
        functools.partial(plan_kernel, owners, regions, blocks),
        [((count, (owners + blocks) * SIDE), BF16), ((count, LANES), F32)],
        index, scratch=[pltpu.VMEM((8, 384), F32)],
    )
    inside = call(
        inside_kernel,
        [((ROWS, LANES), BF16), ((3, LANES, 2 * LANES), F32), ((8, LANES), F32), ((SIDE, LANES), F32)],
        signal, offset, cot, *copies, **work,
    )
    others, hot, half_mask, inside = lax.optimization_barrier((others, hot, half_mask, inside))
    grad, *inside = inside

    line = pltpu.VMEM((40, LANES), F32)
    g_lines, g_sides, message, sent = call(
        middle_kernel,
        [
            ((SIDE, LANES), F32), ((2 * SIDE, LANES), BF16),
            ((WROWS, LANES), BF16), ((WROWS + blocks * SIDE, LANES), BF16),
        ],
        signal, offset, cot, *copies, lines, *inside, rows, *others, cols, hot, half_mask, forward, columns,
        scratch=[
            pltpu.VMEM((count, LANES), F32), pltpu.VMEM((96, LANES), F32), pltpu.VMEM((2 * WROWS, LANES), F32),
        ],
        moved=2**20,
    )

    if regions > 2:
        upper, lower = sent[WROWS + SIDE :], sent[WROWS : WROWS + SIDE]
        sides = [shift(upper, "region", 1), shift(lower, "region", -1)]
        sent = sent[:WROWS]
    other = swap(sent, "region", 1)
    own_rows = call(
        halo_rows_kernel, [((SIDE, LANES), BF16)], g_lines, backward,
        scratch=[line, line, pltpu.VMEM((SIDE, LANES), F32)],
    )[0]
    other, own_rows = lax.optimization_barrier((other, own_rows))
    if regions == 2:
        sides = [other]
    far = [k for k in steps_of(regions) if k > 1]
    for k in [1] + far:
        extra = () if k != ([1] + far)[-1] else (own_rows,)
        size = (WROWS + SIDE * len(extra), LANES)
        got = other if k == 1 else swap(message, "region", k)
        message = call(first_join_kernel, [(size, BF16)], message, got, *extra)[0]
    beside = [grad, g_lines, g_sides]
    for bits in rounds[:-1]:
        message, beside, index = lax.optimization_barrier((message, beside, index))
        others = exchange(message, bits, FAR_ORDER)
        if bits == rounds[-2]:
            pick = call(functools.partial(pick_kernel, owners), [((4 * SIDE, owners * SIDE), BF16)], index)[0]
            beside = call(grad_copies_kernel, [pair] * 3, *beside, moved=2 * 2**20)
            others, beside, pick = lax.optimization_barrier((others, beside, pick))
        size = (WROWS + (len(others) + 1) * (message.shape[0] - WROWS), LANES)
        message = call(join_kernel, [(size, BF16)], message, *others)[0]
    message, beside = lax.optimization_barrier((message, beside))
    others = exchange(message, rounds[-1], NEAR_ORDER)
    beside = call(inner_kernel, [both], *beside, backward, **work)[0]
    others, beside = lax.optimization_barrier((others, beside))
    scale = 1.0 / math.sqrt(regions * owners * SIDE * SIDE)
    part = call(functools.partial(close_kernel, scale), [((WROWS, LANES), F32)], message, *others)[0]
    other_part = swap(part, "region", 1)
    input_grad = call(
        last_kernel, [((SIDE, SIDE * CHANNELS), BF16)], message, *others, beside, pick, *sides, moved=2 * 2**20
    )[0]
    weight_grad, bias_grad = call(
        weight_kernel, [((CHANNELS, 9 * CHANNELS), F32), ((1, CHANNELS), F32)], part, other_part
    )
    return input_grad.reshape(1, SIDE, SIDE * CHANNELS), weight_grad.T, bias_grad.reshape(CHANNELS)


def solution(mesh):
    placed = (
        P(("region", "patch"), None, None),
        P(),
        P(),
        P(("region", "patch"), None, None),
        P("region", None),
    )
    return jax.shard_map(
        body,
        mesh=mesh,
        in_specs=placed,
        out_specs=(P(("region", "patch"), None, None), P(), P()),
        check_vma=False,
    )
```

```python
import functools
import math

import jax
import jax.numpy as jnp
from jax import lax
from jax.experimental import pallas as pl
from jax.experimental.pallas import tpu as pltpu
from jax.sharding import PartitionSpec as P

CHANNELS = 64
SIDE = 64
PAIRS = SIDE // 2
LANES = 2 * CHANNELS
ROWS = PAIRS * SIDE
WROWS = 5 * CHANNELS // 2
FAR_ORDER = (0, 2, 1)
NEAR_ORDER = (0, 1, 2)
F32 = jnp.float32
BF16 = jnp.bfloat16


def call(kernel, outs, *args, scratch=(), flops=0, moved=0, limit=48):
    whole = pl.BlockSpec(memory_space=pltpu.VMEM)
    shapes = [jax.ShapeDtypeStruct(s, d) for s, d in outs]
    return pl.pallas_call(
        kernel,
        out_shape=shapes,
        in_specs=[whole] * len(args),
        out_specs=[whole] * len(outs),
        scratch_shapes=list(scratch),
        compiler_params=pltpu.CompilerParams(vmem_limit_bytes=limit * 2**20),
        cost_estimate=pl.CostEstimate(flops=flops, bytes_accessed=moved, transcendentals=0),
    )(*args)


def iota(shape, dim):
    return lax.broadcasted_iota(jnp.int32, shape, dim)


def low(shape):
    return iota(shape, len(shape) - 1) < CHANNELS


def turn(x):
    return pltpu.roll(x, CHANNELS, 1)


def tile(q):
    return pl.ds(pl.multiple_of(q * LANES, LANES), LANES)


def block(q):
    return pl.ds(pl.multiple_of(q * SIDE, SIDE), SIDE)


def dot(a, b, dims=((1,), (0,))):
    return lax.dot_general(a, b, (dims, ((), ())), preferred_element_type=F32)


NT = ((1,), (1,))
TN = ((0,), (0,))


def shifted_copies(load, p0, p1, p2, lines=None):
    is_low = low((SIDE, LANES))
    row = iota((SIDE, LANES), 0)

    def put(q, before, now):
        v = jnp.where(is_low, before, now)
        p1[block(q), :] = v.astype(BF16)
        if lines is not None:
            for i, r in enumerate((0, 1, SIDE - 2, SIDE - 1)):
                lines[i, pl.ds(q, 1), :] = v[r : r + 1]
        p0[block(q), :] = jnp.where(row == 0, 0.0, pltpu.roll(v, 1, 0)).astype(BF16)
        p2[block(q), :] = jnp.where(row == SIDE - 1, 0.0, pltpu.roll(v, SIDE - 1, 0)).astype(BF16)

    def step(q, before):
        now = turn(load(q))
        put(q, before, now)
        return now

    zero = jnp.zeros((SIDE, LANES), F32)
    last = lax.fori_loop(0, PAIRS, step, zero, unroll=4)
    put(PAIRS, last, zero)


def product(p0, p1, p2, w_ref, dims):
    total = None
    for a, p in enumerate((p0, p1, p2)):
        window = jnp.concatenate([p[0:ROWS, :], p[SIDE : ROWS + SIDE, :]], axis=1)
        term = dot(window, w_ref[a], dims)
        total = term if total is None else total + term
    return total


def rim_kernel(top, bottom, rows_ref, scr):
    for q in range(PAIRS):
        lanes = slice(q * LANES, (q + 1) * LANES)
        scr[q : q + 1, :] = top[:, lanes].astype(F32)[0:1]
        scr[PAIRS + q : PAIRS + q + 1, :] = bottom[:, lanes].astype(F32)[15:16]
    rows_ref[...] = scr[...].astype(BF16)


def rows_kernel(*refs):
    parts, out = by_distance(refs[:-1], FAR_ORDER), refs[-1]
    n = parts[0].shape[0]
    for i, part in enumerate(parts):
        out[i * n : (i + 1) * n, :] = part[...]


def bits_moved(v, pairs):
    result = jnp.zeros_like(v)
    for from_bit, to_bit in pairs:
        result = result | (((v >> from_bit) & 1) << to_bit)
    return result


def plan_kernel(owners, regions, blocks, index_ref, hot_ref, half_ref, scr):
    owner = lax.axis_index("patch")
    region = lax.axis_index("region")
    bits = owners.bit_length() - 1
    index = index_ref[pl.ds(owner, 1), :]
    source, within = index >> 8, index & 255
    slot = bits_moved((source & (owners - 1)) ^ owner, slot_bits(owners))
    row = within & (SIDE - 1)
    if blocks == 2:
        row = row + jnp.where((((source >> bits) - region + regions) & (regions - 1)) == 1, SIDE, 0)
    is_row = within < 2 * SIDE
    place = jnp.where(is_row, slot * SIDE + (within >> 1), owners * SIDE + row)
    half = jnp.where(is_row, within & 1, (within >> 6) & 1)
    count = index.shape[1]
    scr[...] = jnp.full(scr.shape, -1.0, F32)
    scr[0:1, 0:count] = place.astype(F32)
    scr[1:2, 0:count] = half.astype(F32)
    column = jnp.transpose(scr[...])[0 : hot_ref.shape[0]]
    half_ref[...] = jnp.broadcast_to(column[:, 1:2], half_ref.shape)
    place = column[:, 0:1].astype(jnp.int32)
    for c in range(0, hot_ref.shape[1], LANES):
        n = min(LANES, hot_ref.shape[1] - c)
        hot_ref[:, c : c + n] = (place == iota((hot_ref.shape[0], n), 1) + c).astype(F32).astype(BF16)


def pick_kernel(owners, index_ref, pick_ref):
    owner, region = lax.axis_index("patch"), lax.axis_index("region")
    base = (region * owners + owner) * 4 * SIDE
    want = 2 * iota((SIDE, LANES), 0)
    for t in range(owners // 2):
        pair = []
        for slot in (2 * t, 2 * t + 1):
            relative = sum(1 << bit for bit, to in slot_bits(owners) if (slot >> to) & 1)
            line = index_ref[pl.ds(owner ^ relative, 1), :]
            pair.append((line[:, 1 : SIDE + 1], line[:, SIDE + 3 : 2 * SIDE + 3]))
        for s in range(2):
            both = jnp.concatenate([pair[0][s], pair[1][s]], axis=1) - base
            for e in range(2):
                hit = (both == want + e).astype(F32).astype(BF16)
                n = 2 * e + s
                pick_ref[n * SIDE : (n + 1) * SIDE, t * LANES : (t + 1) * LANES] = hit


def weights_kernel(wt_ref, w_ref, wb_ref, wc_ref):
    wide = [wt_ref[:, t * LANES : (t + 1) * LANES].astype(F32) for t in range(4)]
    tail = wt_ref[:, 4 * LANES :].astype(F32)
    wide.append(jnp.concatenate([tail, tail], axis=1))

    def at(a, b, high):
        m = 3 * a + b
        v = wide[m // 2]
        return v if m == 8 or (m % 2 == 1) == high else turn(v)

    def pair(a, left, right):
        zero = jnp.zeros((CHANNELS, LANES), F32)
        lo = zero if left is None else at(a, left, False)
        hi = zero if right is None else at(a, right, True)
        return halves(lo, hi).astype(BF16)

    c = CHANNELS
    for a in range(3):
        w_ref[a, 0:c, 0:LANES] = pair(a, 0, 1)
        w_ref[a, 0:c, LANES:] = pair(a, 2, None)
        w_ref[a, c:, 0:LANES] = pair(a, None, 0)
        w_ref[a, c:, LANES:] = pair(a, 1, 2)
        for w, (left, right) in enumerate(((2, None), (1, 2), (0, 1), (None, 0))):
            wb_ref[2 - a, w * c : (w + 1) * c, :] = pair(a, left, right)
        wc_ref[a, 0:c, :] = pair(a, 0, None)
        wc_ref[a, c:, :] = pair(a, None, 2)


def copies_kernel(x_ref, p0, p1, p2, lines, cols_ref):
    first = x_ref[:, 0:LANES].astype(F32)
    last = x_ref[:, (PAIRS - 1) * LANES :].astype(F32)
    cols_ref[...] = halves(first, last).astype(BF16)
    shifted_copies(lambda q: x_ref[:, tile(q)].astype(F32), p0, p1, p2, lines)


def signal_kernel(p0, p1, p2, w_ref, s_ref):
    s_ref[...] = product(p0, p1, p2, w_ref, NT)


def slope_times(signal, upstream):
    sigma = 1.0 / (1.0 + jnp.exp(-signal))
    return upstream * (sigma * (1.0 + signal * (1.0 - sigma)))


def halves(even, odd):
    return jnp.where(low(even.shape), even, odd)


def inside_kernel(s_ref, offset, cot_ref, p0, p1, p2, g_ref, terms_ref, bias_ref, cot_lines):
    row = iota((SIDE, LANES), 0)
    border = jnp.logical_or(row == 0, row == SIDE - 1)
    added = jnp.concatenate([offset[...], offset[...]], axis=1)

    def step(q, bias):
        upstream = cot_ref[:, tile(q)].astype(F32)
        g = jnp.where(border, 0.0, slope_times(s_ref[block(q), :] + added, upstream)).astype(BF16)
        g_ref[block(q), :] = g
        cot_lines[pl.ds(q, 1), :] = upstream[0:1]
        cot_lines[pl.ds(PAIRS + q, 1), :] = upstream[SIDE - 1 :]
        return bias + jnp.sum(g.astype(F32).reshape(8, 8, LANES), axis=0)

    cot_lines[...] = jnp.zeros(cot_lines.shape, F32)
    bias_ref[...] = lax.fori_loop(1, PAIRS - 1, step, jnp.zeros((8, LANES), F32), unroll=2)
    g_ref[0:SIDE, :] = jnp.zeros((SIDE, LANES), BF16)
    g_ref[ROWS - SIDE :, :] = jnp.zeros((SIDE, LANES), BF16)
    g = g_ref[SIDE : ROWS - SIDE, :]
    for a, p in enumerate((p0, p1, p2)):
        for shift in (0, 1):
            start = (1 + shift) * SIDE
            terms_ref[a, :, shift * LANES : (shift + 1) * LANES] = dot(g, p[start : start + ROWS - 2 * SIDE, :], TN)


def middle_kernel(
    s_ref, offset, cot_ref, p0, p1, p2, lines, terms_ref, bias_ref, cot_lines, rows_a, rows_b, rows_c, rows_d, cols_ref,
    hot_ref, half_ref, w_ref, wc_ref,
    g_lines, g_sides, keep_ref, send_ref, cell_scr, gc, msg,
):
    added = jnp.concatenate([offset[...], offset[...]], axis=1)
    n = rows_a.shape[0]
    many = 4 * n
    cells = dot(hot_ref[:, many:], cols_ref[...])
    for i, ref in enumerate(by_distance((rows_a, rows_b, rows_c, rows_d), NEAR_ORDER)):
        cells = cells + dot(hot_ref[:, i * n : (i + 1) * n], ref[...])
    other = turn(cells)
    upper = half_ref[...] > 0.5
    edge = 2 * SIDE + 4
    as_low = jnp.where(upper, other, cells)
    as_high = jnp.where(upper, cells, other)
    sides = halves(as_low[edge : edge + SIDE], as_high[edge + SIDE : edge + 2 * SIDE])
    odd = iota(cells.shape, 0) % 2 == 1
    cell_scr[...] = jnp.where(odd, as_high, as_low)

    def windows(both):
        return jnp.concatenate([both[0:PAIRS], both[1 : PAIRS + 1]], axis=1)

    def line_of(start):
        even_cells = cell_scr[pl.ds(start, PAIRS + 1, stride=2), :]
        odd_cells = cell_scr[pl.ds(start + 1, PAIRS + 1, stride=2), :]
        return windows(halves(even_cells, odd_cells))

    is_low = low((SIDE, LANES))
    row = iota((SIDE, LANES), 0)
    top = line_of(0)
    bottom = line_of(SIDE + 2)
    moved = (
        jnp.where(row == 0, 0.0, pltpu.roll(sides, 1, 0)),
        sides,
        jnp.where(row == SIDE - 1, 0.0, pltpu.roll(sides, SIDE - 1, 0)),
    )
    lefts = [jnp.where(is_low, m, 0.0) for m in moved]
    rights = [jnp.where(is_low, 0.0, m) for m in moved]
    top_signal = dot(top.astype(BF16), w_ref[0], NT)
    bottom_signal = dot(bottom.astype(BF16), w_ref[2], NT)

    def side_grad(q, columns, lanes):
        signal = s_ref[q * SIDE : (q + 1) * SIDE, :] + added
        for a in range(3):
            signal = signal + dot(columns[a].astype(BF16), w_ref[a, :, lanes], NT)
        signal = signal + jnp.where(row == 0, top_signal[q : q + 1], 0.0)
        signal = signal + jnp.where(row == SIDE - 1, bottom_signal[q : q + 1], 0.0)
        upstream = cot_ref[:, q * LANES : (q + 1) * LANES].astype(F32)
        return slope_times(signal, upstream).astype(BF16).astype(F32)

    end = PAIRS - 1
    g_left = side_grad(0, lefts, slice(0, LANES))
    g_right = side_grad(end, rights, slice(LANES, 2 * LANES))
    pair = iota((PAIRS, LANES), 0)
    ends = jnp.logical_or(pair == 0, pair == end)

    def line_grad(first_row, halo_signal):
        signal = s_ref[pl.ds(first_row, PAIRS, stride=SIDE), :] + added + halo_signal
        upstream = cot_lines[0:PAIRS, :] if first_row == 0 else cot_lines[PAIRS:, :]
        g = jnp.where(ends, 0.0, slope_times(signal, upstream)).astype(BF16).astype(F32)
        r = slice(first_row, first_row + 1)
        return g, jnp.where(pair == 0, g_left[r], jnp.where(pair == end, g_right[r], g))

    inner_top, all_top = line_grad(0, top_signal)
    inner_bottom, all_bottom = line_grad(SIDE - 1, bottom_signal)
    g_lines[0:PAIRS, :] = all_top
    g_lines[PAIRS:, :] = all_bottom
    g_sides[0:SIDE, :] = g_left.astype(BF16)
    g_sides[SIDE:, :] = g_right.astype(BF16)
    border = jnp.concatenate([inner_top, inner_bottom, g_left, g_right], axis=0)
    bias = jnp.sum(bias_ref[...], axis=0, keepdims=True) + jnp.sum(border, axis=0, keepdims=True)
    border = border.astype(BF16)
    kept = [windows(lines[i]) for i in range(4)]
    none = jnp.zeros((SIDE, LANES), F32)
    wide_row = iota((SIDE, 2 * LANES), 0)

    def side_window(a, p, q, columns):
        parts = [p[(q + i) * SIDE : (q + i + 1) * SIDE, :].astype(F32) for i in range(2)]
        window = jnp.concatenate(parts, axis=1) + columns
        if a == 0:
            window = window + jnp.where(wide_row == 0, top[q : q + 1], 0.0)
        if a == 2:
            window = window + jnp.where(wide_row == SIDE - 1, bottom[q : q + 1], 0.0)
        return window

    terms = []
    over = (top, kept[0], kept[1])
    under = (kept[2], kept[3], bottom)
    for a, p in enumerate((p0, p1, p2)):
        window = jnp.concatenate(
            [
                over[a],
                under[a],
                side_window(a, p, 0, jnp.concatenate([lefts[a], none], axis=1)),
                side_window(a, p, end, jnp.concatenate([none, rights[a]], axis=1)),
            ],
            axis=0,
        ).astype(BF16)
        t = terms_ref[a] + dot(border, window, TN)
        terms += [t[:, :LANES], t[:, LANES:]]
    def tap(m, high):
        a, b = m // 3, m % 3
        result = 0.0
        for e in (0, 1):
            w = e + b
            part = terms[2 * a + w // 2][e * CHANNELS : (e + 1) * CHANNELS]
            result = result + (part if (w % 2 == 1) == high else turn(part))
        return result

    total = bias + turn(bias)
    coarse = total.astype(BF16).astype(F32)
    fine = total - coarse
    for t in range(5):
        if t < 4:
            high = tap(2 * t + 1, True)
        else:
            high = jnp.where(row == 0, coarse, jnp.where(row == 1, fine, 0.0))
        msg[t * SIDE : (t + 1) * SIDE, :] = halves(tap(2 * t, False), high)
    core = lax.axis_index("region") & 1
    keep_ref[...] = msg[pl.ds(pl.multiple_of(core * WROWS, WROWS), WROWS), :].astype(BF16)
    send_ref[0:WROWS, :] = msg[pl.ds(pl.multiple_of((1 - core) * WROWS, WROWS), WROWS), :].astype(BF16)

    gc[...] = jnp.zeros(gc.shape, F32)
    gc[8 : 8 + SIDE, :] = halves(g_left, g_right)
    grads = dot(gc[8:88, :].astype(BF16), wc_ref[0])
    grads = grads + dot(gc[7:87, :].astype(BF16), wc_ref[1])
    grads = grads + dot(gc[6:86, :].astype(BF16), wc_ref[2])
    other = turn(grads)
    lefts = halves(grads, other)
    rights = halves(other, grads)
    cell_scr[...] = jnp.zeros(cell_scr.shape, F32)
    for at, src, first_row, n in (
        (0, lefts, 0, 1), (SIDE + 1, rights, 0, 1), (SIDE + 2, lefts, SIDE + 1, 1), (edge - 1, rights, SIDE + 1, 1),
        (edge, lefts, 1, SIDE), (edge + SIDE, rights, 1, SIDE),
    ):
        cell_scr[at : at + n, :] = src[first_row : first_row + n]
    placed = jnp.where(upper == low(cells.shape), 0.0, cell_scr[...]).astype(BF16)
    send_ref[WROWS:, :] = dot(hot_ref[:, many:], placed, TN).astype(BF16)


def halo_rows_kernel(g_lines, wb_ref, own_ref, gt, gb, own_scr):
    all_top, all_bottom = g_lines[0:PAIRS, :], g_lines[PAIRS:, :]
    for scr, line in ((gt, all_top), (gb, all_bottom)):
        turned = turn(line)
        scr[...] = jnp.zeros(scr.shape, F32)
        scr[1 : PAIRS + 1, :] = jnp.where(low(line.shape), turned, 0.0)
        scr[0:PAIRS, :] += jnp.where(low(line.shape), 0.0, turned)
    lines = []
    for src, tap_row in ((gt, 2), (gb, 0)):
        window = jnp.concatenate([src[0:PAIRS, :], src[1 : PAIRS + 1, :]], axis=1).astype(BF16)
        lines.append(dot(window, wb_ref[tap_row]))
    own_scr[pl.ds(0, PAIRS, stride=2), :] = halves(lines[0], turn(lines[1]))
    own_scr[pl.ds(1, PAIRS, stride=2), :] = halves(turn(lines[0]), lines[1])
    own_ref[...] = own_scr[...].astype(BF16)


def grad_copies_kernel(g_ref, g_lines, g_sides, p0, p1, p2):
    row = iota((SIDE, LANES), 0)
    left = g_sides[0:SIDE, :].astype(F32)
    right = g_sides[SIDE:, :].astype(F32)

    def load(q):
        g = g_ref[block(q), :].astype(F32)
        g = jnp.where(row == 0, g_lines[pl.ds(q, 1), :], g)
        g = jnp.where(row == SIDE - 1, g_lines[pl.ds(PAIRS + q, 1), :], g)
        return jnp.where(q == 0, left, jnp.where(q == PAIRS - 1, right, g))

    shifted_copies(load, p0, p1, p2)


def inner_kernel(p0, p1, p2, wb_ref, out_ref):
    out_ref[...] = product(p0, p1, p2, wb_ref, ((1,), (0,)))


def added_weights(parts):
    terms = [part[0:WROWS, :].astype(F32) for part in parts]
    while len(terms) > 1:
        terms = [terms[i] + terms[i + 1] for i in range(0, len(terms), 2)]
    tail = terms[0][WROWS - SIDE :]
    return terms[0], tail + pltpu.roll(tail, SIDE - 1, 0)


def bias_lanes(shape):
    return jnp.logical_and(jnp.logical_not(low(shape)), (lax.axis_index("region") & 1) == 1)


def put_weights(parts, out):
    total, whole = added_weights(parts)
    out[0 : WROWS - SIDE, :] = total[: WROWS - SIDE].astype(BF16)
    row = iota(whole.shape, 0)
    coarse = whole.astype(BF16).astype(F32)
    fine = pltpu.roll(whole - coarse, 1, 0)
    out[WROWS - SIDE : WROWS, :] = jnp.where(
        bias_lanes(whole.shape),
        jnp.where(row == 0, coarse, jnp.where(row == 1, fine, 0.0)),
        total[WROWS - SIDE :],
    ).astype(BF16)


def first_join_kernel(mine, other, *rest):
    extra, out = rest[:-1], rest[-1]
    put_weights((mine, other), out)
    if extra:
        out[WROWS:, :] = extra[0][...]


def join_kernel(*refs):
    parts, out = by_distance(refs[:-1], FAR_ORDER), refs[-1]
    put_weights(parts, out)
    n = parts[0].shape[0] - WROWS
    for i, part in enumerate(parts):
        out[WROWS + i * n : WROWS + (i + 1) * n, :] = part[WROWS:, :]


def close_kernel(scale, *refs):
    parts, out = by_distance(refs[:-1], NEAR_ORDER), refs[-1]
    total, whole = added_weights(parts)
    out[0 : WROWS - SIDE, :] = total[: WROWS - SIDE] * scale
    out[WROWS - SIDE :, :] = jnp.where(bias_lanes(whole.shape), whole, total[WROWS - SIDE :]) * scale


def weight_kernel(mine, other, wt_ref, bias_ref):
    odd = (lax.axis_index("region") & 1) == 1
    a, b = mine[...], other[...]
    full = jnp.concatenate([jnp.where(odd, b, a), jnp.where(odd, a, b)], axis=0)
    for t in range(4):
        wt_ref[:, t * LANES : (t + 1) * LANES] = full[t * SIDE : (t + 1) * SIDE]
    wt_ref[:, 4 * LANES :] = full[4 * SIDE :, :CHANNELS]
    bias_ref[...] = turn(full[4 * SIDE : 4 * SIDE + 8])[0:1, :CHANNELS]


def last_kernel(row_a, row_b, row_c, row_d, inner, pick, *rest):
    side_refs, grad_ref = rest[:-1], rest[-1]
    n = row_a.shape[0] - WROWS
    got = 0.0
    for i, ref in enumerate(by_distance((row_a, row_b, row_c, row_d), NEAR_ORDER)):
        got = got + dot(pick[:, i * n : (i + 1) * n], ref[WROWS:, :])
    a, b, c, d = (got[i * SIDE : (i + 1) * SIDE] for i in range(4))
    rims = halves(a + turn(b), turn(c) + d)
    sides = side_refs[0][side_refs[0].shape[0] - SIDE :, :].astype(F32)
    for ref in side_refs[1:]:
        sides = sides + ref[...].astype(F32)
    row = iota((SIDE, LANES), 0)
    is_low = low((SIDE, LANES))
    for q in range(PAIRS):
        v = inner[q * SIDE : (q + 1) * SIDE, :]
        v = v + jnp.where(row == 0, rims[q : q + 1], jnp.where(row == SIDE - 1, rims[PAIRS + q : PAIRS + q + 1], 0.0))
        if q == 0:
            v = v + jnp.where(is_low, sides, 0.0)
        if q == PAIRS - 1:
            v = v + jnp.where(is_low, 0.0, sides)
        grad_ref[:, q * LANES : (q + 1) * LANES] = v.astype(BF16)


def swap(x, axis, k):
    n = lax.axis_size(axis)
    return lax.ppermute(x, axis, [(i, i ^ k) for i in range(n)])


def shift(x, axis, by):
    n = lax.axis_size(axis)
    return lax.ppermute(x, axis, [(i, (i + by) % n) for i in range(n)])


def steps_of(n):
    ks = []
    k = n // 2
    while k:
        ks.append(k)
        k //= 2
    return ks


def rounds_of(owners):
    count = owners.bit_length() - 1
    pairs = [(bit, bit + 1) for bit in range(count % 2, count, 2)][::-1]
    if count % 2:
        pairs = [tuple(b - 1 for b in p) for p in pairs]
        return [(count - 1,)] + pairs
    return pairs


def slot_bits(owners):
    bits = [bit for bits in rounds_of(owners) for bit in bits]
    return [(bit, to) for to, bit in enumerate(bits)]


def exchange(x, bits, order):
    ks = [sum(1 << bits[i] for i in range(len(bits)) if (n >> i) & 1) for n in range(1, 1 << len(bits))]
    return [swap(x, "patch", ks[i]) for i in order if i < len(ks)]


def by_distance(parts, order):
    places = [i for i in order if i < len(parts) - 1]
    return [parts[0]] + [parts[1 + places.index(i)] for i in range(len(places))]


def body(fine_input, fine_weight, fine_bias, cotangent, halo_index):
    owners = lax.axis_size("patch")
    regions = lax.axis_size("region")
    rounds = rounds_of(owners)
    blocks = 1 if regions == 2 else 2
    x = fine_input.reshape(SIDE, SIDE * CHANNELS)
    cot = cotangent.reshape(SIDE, SIDE * CHANNELS)
    pair = ((ROWS + SIDE, LANES), BF16)

    rows = call(
        rim_kernel, [((SIDE, LANES), BF16)], x[:16], x[SIDE - 16 :], scratch=[pltpu.VMEM((SIDE, LANES), F32)]
    )[0]
    count = 272
    both = ((ROWS, LANES), F32)
    work = dict(flops=2 * ROWS * 768 * 128, moved=3 * 2**20)

    others = exchange(rows, rounds[0], FAR_ORDER)
    *copies, lines, cols = call(
        copies_kernel, [pair] * 3 + [((4, 40, LANES), F32), ((SIDE, LANES), BF16)], x, moved=2 * 2**20
    )
    if regions == 2:
        cols = swap(cols, "region", 1)
    else:
        cols = jnp.concatenate([shift(cols, "region", 1), shift(cols, "region", -1)], axis=0)
    forward, backward, columns = call(
        weights_kernel,
        [((3, LANES, 2 * LANES), BF16), ((3, 2 * LANES, LANES), BF16), ((3, LANES, LANES), BF16)],
        fine_weight.T,
    )
    signal = call(
        signal_kernel, [both], *copies, forward, **work,
    )[0]
    offset = fine_bias.reshape(1, CHANNELS)
    others, signal, index, offset = lax.optimization_barrier((others, signal, halo_index, offset))
    for bits in rounds[1:]:
        size = ((len(others) + 1) * rows.shape[0], LANES)
        rows = call(rows_kernel, [(size, BF16)], rows, *others)[0]
        others = exchange(rows, bits, NEAR_ORDER if bits == rounds[-1] else FAR_ORDER)
    hot, half_mask = call(
        functools.partial(plan_kernel, owners, regions, blocks),
        [((count, (owners + blocks) * SIDE), BF16), ((count, LANES), F32)],
        index, scratch=[pltpu.VMEM((8, 384), F32)],
    )
    inside = call(
        inside_kernel,
        [((ROWS, LANES), BF16), ((3, LANES, 2 * LANES), F32), ((8, LANES), F32), ((SIDE, LANES), F32)],
        signal, offset, cot, *copies, **work,
    )
    others, hot, half_mask, inside = lax.optimization_barrier((others, hot, half_mask, inside))
    grad, *inside = inside

    line = pltpu.VMEM((40, LANES), F32)
    g_lines, g_sides, message, sent = call(
        middle_kernel,
        [
            ((SIDE, LANES), F32), ((2 * SIDE, LANES), BF16),
            ((WROWS, LANES), BF16), ((WROWS + blocks * SIDE, LANES), BF16),
        ],
        signal, offset, cot, *copies, lines, *inside, rows, *others, cols, hot, half_mask, forward, columns,
        scratch=[
            pltpu.VMEM((count, LANES), F32), pltpu.VMEM((96, LANES), F32), pltpu.VMEM((2 * WROWS, LANES), F32),
        ],
        moved=2**20,
    )

    if regions > 2:
        upper, lower = sent[WROWS + SIDE :], sent[WROWS : WROWS + SIDE]
        sides = [shift(upper, "region", 1), shift(lower, "region", -1)]
        sent = sent[:WROWS]
    other = swap(sent, "region", 1)
    own_rows = call(
        halo_rows_kernel, [((SIDE, LANES), BF16)], g_lines, backward,
        scratch=[line, line, pltpu.VMEM((SIDE, LANES), F32)],
    )[0]
    other, own_rows = lax.optimization_barrier((other, own_rows))
    if regions == 2:
        sides = [other]
    far = [k for k in steps_of(regions) if k > 1]
    for k in [1] + far:
        extra = () if k != ([1] + far)[-1] else (own_rows,)
        size = (WROWS + SIDE * len(extra), LANES)
        got = other if k == 1 else swap(message, "region", k)
        message = call(first_join_kernel, [(size, BF16)], message, got, *extra)[0]
    beside = [grad, g_lines, g_sides]
    for bits in rounds[:-1]:
        message, beside, index = lax.optimization_barrier((message, beside, index))
        others = exchange(message, bits, FAR_ORDER)
        if bits == rounds[-2]:
            pick = call(functools.partial(pick_kernel, owners), [((4 * SIDE, owners * SIDE), BF16)], index)[0]
            beside = call(grad_copies_kernel, [pair] * 3, *beside, moved=2 * 2**20)
            others, beside, pick = lax.optimization_barrier((others, beside, pick))
        size = (WROWS + (len(others) + 1) * (message.shape[0] - WROWS), LANES)
        message = call(join_kernel, [(size, BF16)], message, *others)[0]
    message, beside = lax.optimization_barrier((message, beside))
    others = exchange(message, rounds[-1], NEAR_ORDER)
    beside = call(inner_kernel, [both], *beside, backward, **work)[0]
    others, beside = lax.optimization_barrier((others, beside))
    scale = 1.0 / math.sqrt(regions * owners * SIDE * SIDE)
    part = call(functools.partial(close_kernel, scale), [((WROWS, LANES), F32)], message, *others)[0]
    other_part = swap(part, "region", 1)
    input_grad = call(
        last_kernel, [((SIDE, SIDE * CHANNELS), BF16)], message, *others, beside, pick, *sides, moved=2 * 2**20
    )[0]
    weight_grad, bias_grad = call(
        weight_kernel, [((CHANNELS, 9 * CHANNELS), F32), ((1, CHANNELS), F32)], part, other_part
    )
    return input_grad.reshape(1, SIDE, SIDE * CHANNELS), weight_grad.T, bias_grad.reshape(CHANNELS)


def solution(mesh):
    placed = (
        P(("region", "patch"), None, None),
        P(),
        P(),
        P(("region", "patch"), None, None),
        P("region", None),
    )
    return jax.shard_map(
        body,
        mesh=mesh,
        in_specs=placed,
        out_specs=(P(("region", "patch"), None, None), P(), P()),
        check_vma=False,
    )
```

```python
import functools
import math

import jax
import jax.numpy as jnp
from jax import lax
from jax.experimental import pallas as pl
from jax.experimental.pallas import tpu as pltpu
from jax.sharding import PartitionSpec as P

CHANNELS = 64
SIDE = 64
PAIRS = SIDE // 2
LANES = 2 * CHANNELS
ROWS = PAIRS * SIDE
WROWS = 5 * CHANNELS // 2
FAR_ORDER = (0, 2, 1)
NEAR_ORDER = (0, 1, 2)
F32 = jnp.float32
BF16 = jnp.bfloat16


def call(kernel, outs, *args, scratch=(), flops=0, moved=0, limit=48):
    whole = pl.BlockSpec(memory_space=pltpu.VMEM)
    shapes = [jax.ShapeDtypeStruct(s, d) for s, d in outs]
    return pl.pallas_call(
        kernel,
        out_shape=shapes,
        in_specs=[whole] * len(args),
        out_specs=[whole] * len(outs),
        scratch_shapes=list(scratch),
        compiler_params=pltpu.CompilerParams(vmem_limit_bytes=limit * 2**20),
        cost_estimate=pl.CostEstimate(flops=flops, bytes_accessed=moved, transcendentals=0),
    )(*args)


def iota(shape, dim):
    return lax.broadcasted_iota(jnp.int32, shape, dim)


def low(shape):
    return iota(shape, len(shape) - 1) < CHANNELS


def turn(x):
    return pltpu.roll(x, CHANNELS, 1)


def tile(q):
    return pl.ds(pl.multiple_of(q * LANES, LANES), LANES)


def block(q):
    return pl.ds(pl.multiple_of(q * SIDE, SIDE), SIDE)


def dot(a, b, dims=((1,), (0,))):
    return lax.dot_general(a, b, (dims, ((), ())), preferred_element_type=F32)


NT = ((1,), (1,))
TN = ((0,), (0,))


def shifted_copies(load, p0, p1, p2, lines=None):
    is_low = low((SIDE, LANES))
    row = iota((SIDE, LANES), 0)

    def put(q, before, now):
        v = jnp.where(is_low, before, now)
        p1[block(q), :] = v.astype(BF16)
        if lines is not None:
            for i, r in enumerate((0, 1, SIDE - 2, SIDE - 1)):
                lines[i, pl.ds(q, 1), :] = v[r : r + 1]
        p0[block(q), :] = jnp.where(row == 0, 0.0, pltpu.roll(v, 1, 0)).astype(BF16)
        p2[block(q), :] = jnp.where(row == SIDE - 1, 0.0, pltpu.roll(v, SIDE - 1, 0)).astype(BF16)

    def step(q, before):
        now = turn(load(q))
        put(q, before, now)
        return now

    zero = jnp.zeros((SIDE, LANES), F32)
    last = lax.fori_loop(0, PAIRS, step, zero, unroll=4)
    put(PAIRS, last, zero)


def product(p0, p1, p2, w_ref, dims):
    total = None
    for a, p in enumerate((p0, p1, p2)):
        window = jnp.concatenate([p[0:ROWS, :], p[SIDE : ROWS + SIDE, :]], axis=1)
        term = dot(window, w_ref[a], dims)
        total = term if total is None else total + term
    return total


def rim_kernel(top, bottom, rows_ref, scr):
    for q in range(PAIRS):
        lanes = slice(q * LANES, (q + 1) * LANES)
        scr[q : q + 1, :] = top[:, lanes].astype(F32)[0:1]
        scr[PAIRS + q : PAIRS + q + 1, :] = bottom[:, lanes].astype(F32)[15:16]
    rows_ref[...] = scr[...].astype(BF16)


def rows_kernel(*refs):
    parts, out = by_distance(refs[:-1], FAR_ORDER), refs[-1]
    n = parts[0].shape[0]
    for i, part in enumerate(parts):
        out[i * n : (i + 1) * n, :] = part[...]


def bits_moved(v, pairs):
    result = jnp.zeros_like(v)
    for from_bit, to_bit in pairs:
        result = result | (((v >> from_bit) & 1) << to_bit)
    return result


def plan_kernel(owners, regions, blocks, index_ref, hot_ref, half_ref, scr):
    owner = lax.axis_index("patch")
    region = lax.axis_index("region")
    bits = owners.bit_length() - 1
    index = index_ref[pl.ds(owner, 1), :]
    source, within = index >> 8, index & 255
    slot = bits_moved((source & (owners - 1)) ^ owner, slot_bits(owners))
    row = within & (SIDE - 1)
    if blocks == 2:
        row = row + jnp.where((((source >> bits) - region + regions) & (regions - 1)) == 1, SIDE, 0)
    is_row = within < 2 * SIDE
    place = jnp.where(is_row, slot * SIDE + (within >> 1), owners * SIDE + row)
    half = jnp.where(is_row, within & 1, (within >> 6) & 1)
    count = index.shape[1]
    scr[...] = jnp.full(scr.shape, -1.0, F32)
    scr[0:1, 0:count] = place.astype(F32)
    scr[1:2, 0:count] = half.astype(F32)
    column = jnp.transpose(scr[...])[0 : hot_ref.shape[0]]
    half_ref[...] = jnp.broadcast_to(column[:, 1:2], half_ref.shape)
    place = column[:, 0:1].astype(jnp.int32)
    for c in range(0, hot_ref.shape[1], LANES):
        n = min(LANES, hot_ref.shape[1] - c)
        hot_ref[:, c : c + n] = (place == iota((hot_ref.shape[0], n), 1) + c).astype(F32).astype(BF16)


def pick_kernel(owners, index_ref, pick_ref):
    owner, region = lax.axis_index("patch"), lax.axis_index("region")
    base = (region * owners + owner) * 4 * SIDE
    want = 2 * iota((SIDE, LANES), 0)
    for t in range(owners // 2):
        pair = []
        for slot in (2 * t, 2 * t + 1):
            relative = sum(1 << bit for bit, to in slot_bits(owners) if (slot >> to) & 1)
            line = index_ref[pl.ds(owner ^ relative, 1), :]
            pair.append((line[:, 1 : SIDE + 1], line[:, SIDE + 3 : 2 * SIDE + 3]))
        for s in range(2):
            both = jnp.concatenate([pair[0][s], pair[1][s]], axis=1) - base
            for e in range(2):
                hit = (both == want + e).astype(F32).astype(BF16)
                n = 2 * e + s
                pick_ref[n * SIDE : (n + 1) * SIDE, t * LANES : (t + 1) * LANES] = hit


def weights_kernel(wt_ref, w_ref, wb_ref, wc_ref):
    wide = [wt_ref[:, t * LANES : (t + 1) * LANES].astype(F32) for t in range(4)]
    tail = wt_ref[:, 4 * LANES :].astype(F32)
    wide.append(jnp.concatenate([tail, tail], axis=1))

    def at(a, b, high):
        m = 3 * a + b
        v = wide[m // 2]
        return v if m == 8 or (m % 2 == 1) == high else turn(v)

    def pair(a, left, right):
        zero = jnp.zeros((CHANNELS, LANES), F32)
        lo = zero if left is None else at(a, left, False)
        hi = zero if right is None else at(a, right, True)
        return halves(lo, hi).astype(BF16)

    c = CHANNELS
    for a in range(3):
        w_ref[a, 0:c, 0:LANES] = pair(a, 0, 1)
        w_ref[a, 0:c, LANES:] = pair(a, 2, None)
        w_ref[a, c:, 0:LANES] = pair(a, None, 0)
        w_ref[a, c:, LANES:] = pair(a, 1, 2)
        for w, (left, right) in enumerate(((2, None), (1, 2), (0, 1), (None, 0))):
            wb_ref[2 - a, w * c : (w + 1) * c, :] = pair(a, left, right)
        wc_ref[a, 0:c, :] = pair(a, 0, None)
        wc_ref[a, c:, :] = pair(a, None, 2)


def copies_kernel(x_ref, p0, p1, p2, lines, cols_ref):
    first = x_ref[:, 0:LANES].astype(F32)
    last = x_ref[:, (PAIRS - 1) * LANES :].astype(F32)
    cols_ref[...] = halves(first, last).astype(BF16)
    shifted_copies(lambda q: x_ref[:, tile(q)].astype(F32), p0, p1, p2, lines)


def signal_kernel(p0, p1, p2, w_ref, s_ref):
    s_ref[...] = product(p0, p1, p2, w_ref, NT)


def slope_times(signal, upstream):
    sigma = 1.0 / (1.0 + jnp.exp(-signal))
    return upstream * (sigma * (1.0 + signal * (1.0 - sigma)))


def halves(even, odd):
    return jnp.where(low(even.shape), even, odd)


def inside_kernel(s_ref, offset, cot_ref, p0, p1, p2, g_ref, terms_ref, bias_ref, cot_lines):
    row = iota((SIDE, LANES), 0)
    border = jnp.logical_or(row == 0, row == SIDE - 1)
    added = jnp.concatenate([offset[...], offset[...]], axis=1)

    def step(q, bias):
        upstream = cot_ref[:, tile(q)].astype(F32)
        g = jnp.where(border, 0.0, slope_times(s_ref[block(q), :] + added, upstream)).astype(BF16)
        g_ref[block(q), :] = g
        cot_lines[pl.ds(q, 1), :] = upstream[0:1]
        cot_lines[pl.ds(PAIRS + q, 1), :] = upstream[SIDE - 1 :]
        return bias + jnp.sum(g.astype(F32).reshape(8, 8, LANES), axis=0)

    cot_lines[...] = jnp.zeros(cot_lines.shape, F32)
    bias_ref[...] = lax.fori_loop(1, PAIRS - 1, step, jnp.zeros((8, LANES), F32), unroll=6)
    g_ref[0:SIDE, :] = jnp.zeros((SIDE, LANES), BF16)
    g_ref[ROWS - SIDE :, :] = jnp.zeros((SIDE, LANES), BF16)
    g = g_ref[SIDE : ROWS - SIDE, :]
    for a, p in enumerate((p0, p1, p2)):
        for shift in (0, 1):
            start = (1 + shift) * SIDE
            terms_ref[a, :, shift * LANES : (shift + 1) * LANES] = dot(g, p[start : start + ROWS - 2 * SIDE, :], TN)


def middle_kernel(
    s_ref, offset, cot_ref, p0, p1, p2, lines, terms_ref, bias_ref, cot_lines, rows_a, rows_b, rows_c, rows_d, cols_ref,
    hot_ref, half_ref, w_ref, wc_ref,
    g_lines, g_sides, keep_ref, send_ref, cell_scr, gc, msg,
):
    added = jnp.concatenate([offset[...], offset[...]], axis=1)
    n = rows_a.shape[0]
    many = 4 * n
    cells = dot(hot_ref[:, many:], cols_ref[...])
    for i, ref in enumerate(by_distance((rows_a, rows_b, rows_c, rows_d), NEAR_ORDER)):
        cells = cells + dot(hot_ref[:, i * n : (i + 1) * n], ref[...])
    other = turn(cells)
    upper = half_ref[...] > 0.5
    edge = 2 * SIDE + 4
    as_low = jnp.where(upper, other, cells)
    as_high = jnp.where(upper, cells, other)
    sides = halves(as_low[edge : edge + SIDE], as_high[edge + SIDE : edge + 2 * SIDE])
    odd = iota(cells.shape, 0) % 2 == 1
    cell_scr[...] = jnp.where(odd, as_high, as_low)

    def windows(both):
        return jnp.concatenate([both[0:PAIRS], both[1 : PAIRS + 1]], axis=1)

    def line_of(start):
        even_cells = cell_scr[pl.ds(start, PAIRS + 1, stride=2), :]
        odd_cells = cell_scr[pl.ds(start + 1, PAIRS + 1, stride=2), :]
        return windows(halves(even_cells, odd_cells))

    is_low = low((SIDE, LANES))
    row = iota((SIDE, LANES), 0)
    top = line_of(0)
    bottom = line_of(SIDE + 2)
    moved = (
        jnp.where(row == 0, 0.0, pltpu.roll(sides, 1, 0)),
        sides,
        jnp.where(row == SIDE - 1, 0.0, pltpu.roll(sides, SIDE - 1, 0)),
    )
    lefts = [jnp.where(is_low, m, 0.0) for m in moved]
    rights = [jnp.where(is_low, 0.0, m) for m in moved]
    top_signal = dot(top.astype(BF16), w_ref[0], NT)
    bottom_signal = dot(bottom.astype(BF16), w_ref[2], NT)

    def side_grad(q, columns, lanes):
        signal = s_ref[q * SIDE : (q + 1) * SIDE, :] + added
        for a in range(3):
            signal = signal + dot(columns[a].astype(BF16), w_ref[a, :, lanes], NT)
        signal = signal + jnp.where(row == 0, top_signal[q : q + 1], 0.0)
        signal = signal + jnp.where(row == SIDE - 1, bottom_signal[q : q + 1], 0.0)
        upstream = cot_ref[:, q * LANES : (q + 1) * LANES].astype(F32)
        return slope_times(signal, upstream).astype(BF16).astype(F32)

    end = PAIRS - 1
    g_left = side_grad(0, lefts, slice(0, LANES))
    g_right = side_grad(end, rights, slice(LANES, 2 * LANES))
    pair = iota((PAIRS, LANES), 0)
    ends = jnp.logical_or(pair == 0, pair == end)

    def line_grad(first_row, halo_signal):
        signal = s_ref[pl.ds(first_row, PAIRS, stride=SIDE), :] + added + halo_signal
        upstream = cot_lines[0:PAIRS, :] if first_row == 0 else cot_lines[PAIRS:, :]
        g = jnp.where(ends, 0.0, slope_times(signal, upstream)).astype(BF16).astype(F32)
        r = slice(first_row, first_row + 1)
        return g, jnp.where(pair == 0, g_left[r], jnp.where(pair == end, g_right[r], g))

    inner_top, all_top = line_grad(0, top_signal)
    inner_bottom, all_bottom = line_grad(SIDE - 1, bottom_signal)
    g_lines[0:PAIRS, :] = all_top
    g_lines[PAIRS:, :] = all_bottom
    g_sides[0:SIDE, :] = g_left.astype(BF16)
    g_sides[SIDE:, :] = g_right.astype(BF16)
    border = jnp.concatenate([inner_top, inner_bottom, g_left, g_right], axis=0)
    bias = jnp.sum(bias_ref[...], axis=0, keepdims=True) + jnp.sum(border, axis=0, keepdims=True)
    border = border.astype(BF16)
    kept = [windows(lines[i]) for i in range(4)]
    none = jnp.zeros((SIDE, LANES), F32)
    wide_row = iota((SIDE, 2 * LANES), 0)

    def side_window(a, p, q, columns):
        parts = [p[(q + i) * SIDE : (q + i + 1) * SIDE, :].astype(F32) for i in range(2)]
        window = jnp.concatenate(parts, axis=1) + columns
        if a == 0:
            window = window + jnp.where(wide_row == 0, top[q : q + 1], 0.0)
        if a == 2:
            window = window + jnp.where(wide_row == SIDE - 1, bottom[q : q + 1], 0.0)
        return window

    terms = []
    over = (top, kept[0], kept[1])
    under = (kept[2], kept[3], bottom)
    for a, p in enumerate((p0, p1, p2)):
        window = jnp.concatenate(
            [
                over[a],
                under[a],
                side_window(a, p, 0, jnp.concatenate([lefts[a], none], axis=1)),
                side_window(a, p, end, jnp.concatenate([none, rights[a]], axis=1)),
            ],
            axis=0,
        ).astype(BF16)
        t = terms_ref[a] + dot(border, window, TN)
        terms += [t[:, :LANES], t[:, LANES:]]
    def tap(m, high):
        a, b = m // 3, m % 3
        result = 0.0
        for e in (0, 1):
            w = e + b
            part = terms[2 * a + w // 2][e * CHANNELS : (e + 1) * CHANNELS]
            result = result + (part if (w % 2 == 1) == high else turn(part))
        return result

    total = bias + turn(bias)
    coarse = total.astype(BF16).astype(F32)
    fine = total - coarse
    for t in range(5):
        if t < 4:
            high = tap(2 * t + 1, True)
        else:
            high = jnp.where(row == 0, coarse, jnp.where(row == 1, fine, 0.0))
        msg[t * SIDE : (t + 1) * SIDE, :] = halves(tap(2 * t, False), high)
    core = lax.axis_index("region") & 1
    keep_ref[...] = msg[pl.ds(pl.multiple_of(core * WROWS, WROWS), WROWS), :].astype(BF16)
    send_ref[0:WROWS, :] = msg[pl.ds(pl.multiple_of((1 - core) * WROWS, WROWS), WROWS), :].astype(BF16)

    gc[...] = jnp.zeros(gc.shape, F32)
    gc[8 : 8 + SIDE, :] = halves(g_left, g_right)
    grads = dot(gc[8:88, :].astype(BF16), wc_ref[0])
    grads = grads + dot(gc[7:87, :].astype(BF16), wc_ref[1])
    grads = grads + dot(gc[6:86, :].astype(BF16), wc_ref[2])
    other = turn(grads)
    lefts = halves(grads, other)
    rights = halves(other, grads)
    cell_scr[...] = jnp.zeros(cell_scr.shape, F32)
    for at, src, first_row, n in (
        (0, lefts, 0, 1), (SIDE + 1, rights, 0, 1), (SIDE + 2, lefts, SIDE + 1, 1), (edge - 1, rights, SIDE + 1, 1),
        (edge, lefts, 1, SIDE), (edge + SIDE, rights, 1, SIDE),
    ):
        cell_scr[at : at + n, :] = src[first_row : first_row + n]
    placed = jnp.where(upper == low(cells.shape), 0.0, cell_scr[...]).astype(BF16)
    send_ref[WROWS:, :] = dot(hot_ref[:, many:], placed, TN).astype(BF16)


def halo_rows_kernel(g_lines, wb_ref, own_ref, gt, gb, own_scr):
    all_top, all_bottom = g_lines[0:PAIRS, :], g_lines[PAIRS:, :]
    for scr, line in ((gt, all_top), (gb, all_bottom)):
        turned = turn(line)
        scr[...] = jnp.zeros(scr.shape, F32)
        scr[1 : PAIRS + 1, :] = jnp.where(low(line.shape), turned, 0.0)
        scr[0:PAIRS, :] += jnp.where(low(line.shape), 0.0, turned)
    lines = []
    for src, tap_row in ((gt, 2), (gb, 0)):
        window = jnp.concatenate([src[0:PAIRS, :], src[1 : PAIRS + 1, :]], axis=1).astype(BF16)
        lines.append(dot(window, wb_ref[tap_row]))
    own_scr[pl.ds(0, PAIRS, stride=2), :] = halves(lines[0], turn(lines[1]))
    own_scr[pl.ds(1, PAIRS, stride=2), :] = halves(turn(lines[0]), lines[1])
    own_ref[...] = own_scr[...].astype(BF16)


def grad_copies_kernel(g_ref, g_lines, g_sides, p0, p1, p2):
    row = iota((SIDE, LANES), 0)
    left = g_sides[0:SIDE, :].astype(F32)
    right = g_sides[SIDE:, :].astype(F32)

    def load(q):
        g = g_ref[block(q), :].astype(F32)
        g = jnp.where(row == 0, g_lines[pl.ds(q, 1), :], g)
        g = jnp.where(row == SIDE - 1, g_lines[pl.ds(PAIRS + q, 1), :], g)
        return jnp.where(q == 0, left, jnp.where(q == PAIRS - 1, right, g))

    shifted_copies(load, p0, p1, p2)


def inner_kernel(p0, p1, p2, wb_ref, out_ref):
    out_ref[...] = product(p0, p1, p2, wb_ref, ((1,), (0,)))


def added_weights(parts):
    terms = [part[0:WROWS, :].astype(F32) for part in parts]
    while len(terms) > 1:
        terms = [terms[i] + terms[i + 1] for i in range(0, len(terms), 2)]
    tail = terms[0][WROWS - SIDE :]
    return terms[0], tail + pltpu.roll(tail, SIDE - 1, 0)


def bias_lanes(shape):
    return jnp.logical_and(jnp.logical_not(low(shape)), (lax.axis_index("region") & 1) == 1)


def put_weights(parts, out):
    total, whole = added_weights(parts)
    out[0 : WROWS - SIDE, :] = total[: WROWS - SIDE].astype(BF16)
    row = iota(whole.shape, 0)
    coarse = whole.astype(BF16).astype(F32)
    fine = pltpu.roll(whole - coarse, 1, 0)
    out[WROWS - SIDE : WROWS, :] = jnp.where(
        bias_lanes(whole.shape),
        jnp.where(row == 0, coarse, jnp.where(row == 1, fine, 0.0)),
        total[WROWS - SIDE :],
    ).astype(BF16)


def first_join_kernel(mine, other, *rest):
    extra, out = rest[:-1], rest[-1]
    put_weights((mine, other), out)
    if extra:
        out[WROWS:, :] = extra[0][...]


def join_kernel(*refs):
    parts, out = by_distance(refs[:-1], FAR_ORDER), refs[-1]
    put_weights(parts, out)
    n = parts[0].shape[0] - WROWS
    for i, part in enumerate(parts):
        out[WROWS + i * n : WROWS + (i + 1) * n, :] = part[WROWS:, :]


def close_kernel(scale, *refs):
    parts, out = by_distance(refs[:-1], NEAR_ORDER), refs[-1]
    total, whole = added_weights(parts)
    out[0 : WROWS - SIDE, :] = total[: WROWS - SIDE] * scale
    out[WROWS - SIDE :, :] = jnp.where(bias_lanes(whole.shape), whole, total[WROWS - SIDE :]) * scale


def weight_kernel(mine, other, wt_ref, bias_ref):
    odd = (lax.axis_index("region") & 1) == 1
    a, b = mine[...], other[...]
    full = jnp.concatenate([jnp.where(odd, b, a), jnp.where(odd, a, b)], axis=0)
    for t in range(4):
        wt_ref[:, t * LANES : (t + 1) * LANES] = full[t * SIDE : (t + 1) * SIDE]
    wt_ref[:, 4 * LANES :] = full[4 * SIDE :, :CHANNELS]
    bias_ref[...] = turn(full[4 * SIDE : 4 * SIDE + 8])[0:1, :CHANNELS]


def last_kernel(row_a, row_b, row_c, row_d, inner, pick, *rest):
    side_refs, grad_ref = rest[:-1], rest[-1]
    n = row_a.shape[0] - WROWS
    got = 0.0
    for i, ref in enumerate(by_distance((row_a, row_b, row_c, row_d), NEAR_ORDER)):
        got = got + dot(pick[:, i * n : (i + 1) * n], ref[WROWS:, :])
    a, b, c, d = (got[i * SIDE : (i + 1) * SIDE] for i in range(4))
    rims = halves(a + turn(b), turn(c) + d)
    sides = side_refs[0][side_refs[0].shape[0] - SIDE :, :].astype(F32)
    for ref in side_refs[1:]:
        sides = sides + ref[...].astype(F32)
    row = iota((SIDE, LANES), 0)
    is_low = low((SIDE, LANES))
    for q in range(PAIRS):
        v = inner[q * SIDE : (q + 1) * SIDE, :]
        v = v + jnp.where(row == 0, rims[q : q + 1], jnp.where(row == SIDE - 1, rims[PAIRS + q : PAIRS + q + 1], 0.0))
        if q == 0:
            v = v + jnp.where(is_low, sides, 0.0)
        if q == PAIRS - 1:
            v = v + jnp.where(is_low, 0.0, sides)
        grad_ref[:, q * LANES : (q + 1) * LANES] = v.astype(BF16)


def swap(x, axis, k):
    n = lax.axis_size(axis)
    return lax.ppermute(x, axis, [(i, i ^ k) for i in range(n)])


def shift(x, axis, by):
    n = lax.axis_size(axis)
    return lax.ppermute(x, axis, [(i, (i + by) % n) for i in range(n)])


def steps_of(n):
    ks = []
    k = n // 2
    while k:
        ks.append(k)
        k //= 2
    return ks


def rounds_of(owners):
    count = owners.bit_length() - 1
    pairs = [(bit, bit + 1) for bit in range(count % 2, count, 2)][::-1]
    if count % 2:
        pairs = [tuple(b - 1 for b in p) for p in pairs]
        return [(count - 1,)] + pairs
    return pairs


def slot_bits(owners):
    bits = [bit for bits in rounds_of(owners) for bit in bits]
    return [(bit, to) for to, bit in enumerate(bits)]


def exchange(x, bits, order):
    ks = [sum(1 << bits[i] for i in range(len(bits)) if (n >> i) & 1) for n in range(1, 1 << len(bits))]
    return [swap(x, "patch", ks[i]) for i in order if i < len(ks)]


def by_distance(parts, order):
    places = [i for i in order if i < len(parts) - 1]
    return [parts[0]] + [parts[1 + places.index(i)] for i in range(len(places))]


def body(fine_input, fine_weight, fine_bias, cotangent, halo_index):
    owners = lax.axis_size("patch")
    regions = lax.axis_size("region")
    rounds = rounds_of(owners)
    blocks = 1 if regions == 2 else 2
    x = fine_input.reshape(SIDE, SIDE * CHANNELS)
    cot = cotangent.reshape(SIDE, SIDE * CHANNELS)
    pair = ((ROWS + SIDE, LANES), BF16)

    rows = call(
        rim_kernel, [((SIDE, LANES), BF16)], x[:16], x[SIDE - 16 :], scratch=[pltpu.VMEM((SIDE, LANES), F32)]
    )[0]
    count = 272
    both = ((ROWS, LANES), F32)
    work = dict(flops=2 * ROWS * 768 * 128, moved=3 * 2**20)

    others = exchange(rows, rounds[0], FAR_ORDER)
    *copies, lines, cols = call(
        copies_kernel, [pair] * 3 + [((4, 40, LANES), F32), ((SIDE, LANES), BF16)], x, moved=2 * 2**20
    )
    if regions == 2:
        cols = swap(cols, "region", 1)
    else:
        cols = jnp.concatenate([shift(cols, "region", 1), shift(cols, "region", -1)], axis=0)
    forward, backward, columns = call(
        weights_kernel,
        [((3, LANES, 2 * LANES), BF16), ((3, 2 * LANES, LANES), BF16), ((3, LANES, LANES), BF16)],
        fine_weight.T,
    )
    signal = call(
        signal_kernel, [both], *copies, forward, **work,
    )[0]
    offset = fine_bias.reshape(1, CHANNELS)
    others, signal, index, offset = lax.optimization_barrier((others, signal, halo_index, offset))
    for bits in rounds[1:]:
        size = ((len(others) + 1) * rows.shape[0], LANES)
        rows = call(rows_kernel, [(size, BF16)], rows, *others)[0]
        others = exchange(rows, bits, NEAR_ORDER if bits == rounds[-1] else FAR_ORDER)
    hot, half_mask = call(
        functools.partial(plan_kernel, owners, regions, blocks),
        [((count, (owners + blocks) * SIDE), BF16), ((count, LANES), F32)],
        index, scratch=[pltpu.VMEM((8, 384), F32)],
    )
    inside = call(
        inside_kernel,
        [((ROWS, LANES), BF16), ((3, LANES, 2 * LANES), F32), ((8, LANES), F32), ((SIDE, LANES), F32)],
        signal, offset, cot, *copies, **work,
    )
    others, hot, half_mask, inside = lax.optimization_barrier((others, hot, half_mask, inside))
    grad, *inside = inside

    line = pltpu.VMEM((40, LANES), F32)
    g_lines, g_sides, message, sent = call(
        middle_kernel,
        [
            ((SIDE, LANES), F32), ((2 * SIDE, LANES), BF16),
            ((WROWS, LANES), BF16), ((WROWS + blocks * SIDE, LANES), BF16),
        ],
        signal, offset, cot, *copies, lines, *inside, rows, *others, cols, hot, half_mask, forward, columns,
        scratch=[
            pltpu.VMEM((count, LANES), F32), pltpu.VMEM((96, LANES), F32), pltpu.VMEM((2 * WROWS, LANES), F32),
        ],
        moved=2**20,
    )

    if regions > 2:
        upper, lower = sent[WROWS + SIDE :], sent[WROWS : WROWS + SIDE]
        sides = [shift(upper, "region", 1), shift(lower, "region", -1)]
        sent = sent[:WROWS]
    other = swap(sent, "region", 1)
    own_rows = call(
        halo_rows_kernel, [((SIDE, LANES), BF16)], g_lines, backward,
        scratch=[line, line, pltpu.VMEM((SIDE, LANES), F32)],
    )[0]
    other, own_rows = lax.optimization_barrier((other, own_rows))
    if regions == 2:
        sides = [other]
    far = [k for k in steps_of(regions) if k > 1]
    for k in [1] + far:
        extra = () if k != ([1] + far)[-1] else (own_rows,)
        size = (WROWS + SIDE * len(extra), LANES)
        got = other if k == 1 else swap(message, "region", k)
        message = call(first_join_kernel, [(size, BF16)], message, got, *extra)[0]
    beside = [grad, g_lines, g_sides]
    for bits in rounds[:-1]:
        message, beside, index = lax.optimization_barrier((message, beside, index))
        others = exchange(message, bits, FAR_ORDER)
        if bits == rounds[-2]:
            pick = call(functools.partial(pick_kernel, owners), [((4 * SIDE, owners * SIDE), BF16)], index)[0]
            beside = call(grad_copies_kernel, [pair] * 3, *beside, moved=2 * 2**20)
            others, beside, pick = lax.optimization_barrier((others, beside, pick))
        size = (WROWS + (len(others) + 1) * (message.shape[0] - WROWS), LANES)
        message = call(join_kernel, [(size, BF16)], message, *others)[0]
    message, beside = lax.optimization_barrier((message, beside))
    others = exchange(message, rounds[-1], NEAR_ORDER)
    beside = call(inner_kernel, [both], *beside, backward, **work)[0]
    others, beside = lax.optimization_barrier((others, beside))
    scale = 1.0 / math.sqrt(regions * owners * SIDE * SIDE)
    part = call(functools.partial(close_kernel, scale), [((WROWS, LANES), F32)], message, *others)[0]
    other_part = swap(part, "region", 1)
    input_grad = call(
        last_kernel, [((SIDE, SIDE * CHANNELS), BF16)], message, *others, beside, pick, *sides, moved=2 * 2**20
    )[0]
    weight_grad, bias_grad = call(
        weight_kernel, [((CHANNELS, 9 * CHANNELS), F32), ((1, CHANNELS), F32)], part, other_part
    )
    return input_grad.reshape(1, SIDE, SIDE * CHANNELS), weight_grad.T, bias_grad.reshape(CHANNELS)


def solution(mesh):
    placed = (
        P(("region", "patch"), None, None),
        P(),
        P(),
        P(("region", "patch"), None, None),
        P("region", None),
    )
    return jax.shard_map(
        body,
        mesh=mesh,
        in_specs=placed,
        out_specs=(P(("region", "patch"), None, None), P(), P()),
        check_vma=False,
    )
```

```python
import functools
import math

import jax
import jax.numpy as jnp
from jax import lax
from jax.experimental import pallas as pl
from jax.experimental.pallas import tpu as pltpu
from jax.sharding import PartitionSpec as P

CHANNELS = 64
SIDE = 64
PAIRS = SIDE // 2
LANES = 2 * CHANNELS
ROWS = PAIRS * SIDE
WROWS = 5 * CHANNELS // 2
FAR_ORDER = (0, 2, 1)
NEAR_ORDER = (0, 1, 2)
F32 = jnp.float32
BF16 = jnp.bfloat16


def call(kernel, outs, *args, scratch=(), flops=0, moved=0, limit=48):
    whole = pl.BlockSpec(memory_space=pltpu.VMEM)
    shapes = [jax.ShapeDtypeStruct(s, d) for s, d in outs]
    return pl.pallas_call(
        kernel,
        out_shape=shapes,
        in_specs=[whole] * len(args),
        out_specs=[whole] * len(outs),
        scratch_shapes=list(scratch),
        compiler_params=pltpu.CompilerParams(vmem_limit_bytes=limit * 2**20),
        cost_estimate=pl.CostEstimate(flops=flops, bytes_accessed=moved, transcendentals=0),
    )(*args)


def iota(shape, dim):
    return lax.broadcasted_iota(jnp.int32, shape, dim)


def low(shape):
    return iota(shape, len(shape) - 1) < CHANNELS


def turn(x):
    return pltpu.roll(x, CHANNELS, 1)


def tile(q):
    return pl.ds(pl.multiple_of(q * LANES, LANES), LANES)


def block(q):
    return pl.ds(pl.multiple_of(q * SIDE, SIDE), SIDE)


def dot(a, b, dims=((1,), (0,))):
    return lax.dot_general(a, b, (dims, ((), ())), preferred_element_type=F32)


NT = ((1,), (1,))
TN = ((0,), (0,))


def shifted_copies(load, p0, p1, p2, lines=None):
    is_low = low((SIDE, LANES))
    row = iota((SIDE, LANES), 0)

    def put(q, before, now):
        v = jnp.where(is_low, before, now)
        p1[block(q), :] = v.astype(BF16)
        if lines is not None:
            for i, r in enumerate((0, 1, SIDE - 2, SIDE - 1)):
                lines[i, pl.ds(q, 1), :] = v[r : r + 1]
        p0[block(q), :] = jnp.where(row == 0, 0.0, pltpu.roll(v, 1, 0)).astype(BF16)
        p2[block(q), :] = jnp.where(row == SIDE - 1, 0.0, pltpu.roll(v, SIDE - 1, 0)).astype(BF16)

    def step(q, before):
        now = turn(load(q))
        put(q, before, now)
        return now

    zero = jnp.zeros((SIDE, LANES), F32)
    last = lax.fori_loop(0, PAIRS, step, zero, unroll=8)
    put(PAIRS, last, zero)


def product(p0, p1, p2, w_ref, dims):
    total = None
    for a, p in enumerate((p0, p1, p2)):
        window = jnp.concatenate([p[0:ROWS, :], p[SIDE : ROWS + SIDE, :]], axis=1)
        term = dot(window, w_ref[a], dims)
        total = term if total is None else total + term
    return total


def rim_kernel(top, bottom, rows_ref, scr):
    for q in range(PAIRS):
        lanes = slice(q * LANES, (q + 1) * LANES)
        scr[q : q + 1, :] = top[:, lanes].astype(F32)[0:1]
        scr[PAIRS + q : PAIRS + q + 1, :] = bottom[:, lanes].astype(F32)[15:16]
    rows_ref[...] = scr[...].astype(BF16)


def rows_kernel(*refs):
    parts, out = by_distance(refs[:-1], FAR_ORDER), refs[-1]
    n = parts[0].shape[0]
    for i, part in enumerate(parts):
        out[i * n : (i + 1) * n, :] = part[...]


def bits_moved(v, pairs):
    result = jnp.zeros_like(v)
    for from_bit, to_bit in pairs:
        result = result | (((v >> from_bit) & 1) << to_bit)
    return result


def plan_kernel(owners, regions, blocks, index_ref, hot_ref, half_ref, scr):
    owner = lax.axis_index("patch")
    region = lax.axis_index("region")
    bits = owners.bit_length() - 1
    index = index_ref[pl.ds(owner, 1), :]
    source, within = index >> 8, index & 255
    slot = bits_moved((source & (owners - 1)) ^ owner, slot_bits(owners))
    row = within & (SIDE - 1)
    if blocks == 2:
        row = row + jnp.where((((source >> bits) - region + regions) & (regions - 1)) == 1, SIDE, 0)
    is_row = within < 2 * SIDE
    place = jnp.where(is_row, slot * SIDE + (within >> 1), owners * SIDE + row)
    half = jnp.where(is_row, within & 1, (within >> 6) & 1)
    count = index.shape[1]
    scr[...] = jnp.full(scr.shape, -1.0, F32)
    scr[0:1, 0:count] = place.astype(F32)
    scr[1:2, 0:count] = half.astype(F32)
    column = jnp.transpose(scr[...])[0 : hot_ref.shape[0]]
    half_ref[...] = jnp.broadcast_to(column[:, 1:2], half_ref.shape)
    place = column[:, 0:1].astype(jnp.int32)
    for c in range(0, hot_ref.shape[1], LANES):
        n = min(LANES, hot_ref.shape[1] - c)
        hot_ref[:, c : c + n] = (place == iota((hot_ref.shape[0], n), 1) + c).astype(F32).astype(BF16)


def pick_kernel(owners, index_ref, pick_ref):
    owner, region = lax.axis_index("patch"), lax.axis_index("region")
    base = (region * owners + owner) * 4 * SIDE
    want = 2 * iota((SIDE, LANES), 0)
    for t in range(owners // 2):
        pair = []
        for slot in (2 * t, 2 * t + 1):
            relative = sum(1 << bit for bit, to in slot_bits(owners) if (slot >> to) & 1)
            line = index_ref[pl.ds(owner ^ relative, 1), :]
            pair.append((line[:, 1 : SIDE + 1], line[:, SIDE + 3 : 2 * SIDE + 3]))
        for s in range(2):
            both = jnp.concatenate([pair[0][s], pair[1][s]], axis=1) - base
            for e in range(2):
                hit = (both == want + e).astype(F32).astype(BF16)
                n = 2 * e + s
                pick_ref[n * SIDE : (n + 1) * SIDE, t * LANES : (t + 1) * LANES] = hit


def weights_kernel(wt_ref, w_ref, wb_ref, wc_ref):
    wide = [wt_ref[:, t * LANES : (t + 1) * LANES].astype(F32) for t in range(4)]
    tail = wt_ref[:, 4 * LANES :].astype(F32)
    wide.append(jnp.concatenate([tail, tail], axis=1))

    def at(a, b, high):
        m = 3 * a + b
        v = wide[m // 2]
        return v if m == 8 or (m % 2 == 1) == high else turn(v)

    def pair(a, left, right):
        zero = jnp.zeros((CHANNELS, LANES), F32)
        lo = zero if left is None else at(a, left, False)
        hi = zero if right is None else at(a, right, True)
        return halves(lo, hi).astype(BF16)

    c = CHANNELS
    for a in range(3):
        w_ref[a, 0:c, 0:LANES] = pair(a, 0, 1)
        w_ref[a, 0:c, LANES:] = pair(a, 2, None)
        w_ref[a, c:, 0:LANES] = pair(a, None, 0)
        w_ref[a, c:, LANES:] = pair(a, 1, 2)
        for w, (left, right) in enumerate(((2, None), (1, 2), (0, 1), (None, 0))):
            wb_ref[2 - a, w * c : (w + 1) * c, :] = pair(a, left, right)
        wc_ref[a, 0:c, :] = pair(a, 0, None)
        wc_ref[a, c:, :] = pair(a, None, 2)


def copies_kernel(x_ref, p0, p1, p2, lines, cols_ref):
    first = x_ref[:, 0:LANES].astype(F32)
    last = x_ref[:, (PAIRS - 1) * LANES :].astype(F32)
    cols_ref[...] = halves(first, last).astype(BF16)
    shifted_copies(lambda q: x_ref[:, tile(q)].astype(F32), p0, p1, p2, lines)


def signal_kernel(p0, p1, p2, w_ref, s_ref):
    s_ref[...] = product(p0, p1, p2, w_ref, NT)


def slope_times(signal, upstream):
    sigma = 1.0 / (1.0 + jnp.exp(-signal))
    return upstream * (sigma * (1.0 + signal * (1.0 - sigma)))


def halves(even, odd):
    return jnp.where(low(even.shape), even, odd)


def inside_kernel(s_ref, offset, cot_ref, p0, p1, p2, g_ref, terms_ref, bias_ref, cot_lines):
    row = iota((SIDE, LANES), 0)
    border = jnp.logical_or(row == 0, row == SIDE - 1)
    added = jnp.concatenate([offset[...], offset[...]], axis=1)

    def step(q, bias):
        upstream = cot_ref[:, tile(q)].astype(F32)
        g = jnp.where(border, 0.0, slope_times(s_ref[block(q), :] + added, upstream)).astype(BF16)
        g_ref[block(q), :] = g
        cot_lines[pl.ds(q, 1), :] = upstream[0:1]
        cot_lines[pl.ds(PAIRS + q, 1), :] = upstream[SIDE - 1 :]
        return bias + jnp.sum(g.astype(F32).reshape(8, 8, LANES), axis=0)

    cot_lines[...] = jnp.zeros(cot_lines.shape, F32)
    bias_ref[...] = lax.fori_loop(1, PAIRS - 1, step, jnp.zeros((8, LANES), F32), unroll=6)
    g_ref[0:SIDE, :] = jnp.zeros((SIDE, LANES), BF16)
    g_ref[ROWS - SIDE :, :] = jnp.zeros((SIDE, LANES), BF16)
    g = g_ref[SIDE : ROWS - SIDE, :]
    for a, p in enumerate((p0, p1, p2)):
        for shift in (0, 1):
            start = (1 + shift) * SIDE
            terms_ref[a, :, shift * LANES : (shift + 1) * LANES] = dot(g, p[start : start + ROWS - 2 * SIDE, :], TN)


def middle_kernel(
    s_ref, offset, cot_ref, p0, p1, p2, lines, terms_ref, bias_ref, cot_lines, rows_a, rows_b, rows_c, rows_d, cols_ref,
    hot_ref, half_ref, w_ref, wc_ref,
    g_lines, g_sides, keep_ref, send_ref, cell_scr, gc, msg,
):
    added = jnp.concatenate([offset[...], offset[...]], axis=1)
    n = rows_a.shape[0]
    many = 4 * n
    cells = dot(hot_ref[:, many:], cols_ref[...])
    for i, ref in enumerate(by_distance((rows_a, rows_b, rows_c, rows_d), NEAR_ORDER)):
        cells = cells + dot(hot_ref[:, i * n : (i + 1) * n], ref[...])
    other = turn(cells)
    upper = half_ref[...] > 0.5
    edge = 2 * SIDE + 4
    as_low = jnp.where(upper, other, cells)
    as_high = jnp.where(upper, cells, other)
    sides = halves(as_low[edge : edge + SIDE], as_high[edge + SIDE : edge + 2 * SIDE])
    odd = iota(cells.shape, 0) % 2 == 1
    cell_scr[...] = jnp.where(odd, as_high, as_low)

    def windows(both):
        return jnp.concatenate([both[0:PAIRS], both[1 : PAIRS + 1]], axis=1)

    def line_of(start):
        even_cells = cell_scr[pl.ds(start, PAIRS + 1, stride=2), :]
        odd_cells = cell_scr[pl.ds(start + 1, PAIRS + 1, stride=2), :]
        return windows(halves(even_cells, odd_cells))

    is_low = low((SIDE, LANES))
    row = iota((SIDE, LANES), 0)
    top = line_of(0)
    bottom = line_of(SIDE + 2)
    moved = (
        jnp.where(row == 0, 0.0, pltpu.roll(sides, 1, 0)),
        sides,
        jnp.where(row == SIDE - 1, 0.0, pltpu.roll(sides, SIDE - 1, 0)),
    )
    lefts = [jnp.where(is_low, m, 0.0) for m in moved]
    rights = [jnp.where(is_low, 0.0, m) for m in moved]
    top_signal = dot(top.astype(BF16), w_ref[0], NT)
    bottom_signal = dot(bottom.astype(BF16), w_ref[2], NT)

    def side_grad(q, columns, lanes):
        signal = s_ref[q * SIDE : (q + 1) * SIDE, :] + added
        for a in range(3):
            signal = signal + dot(columns[a].astype(BF16), w_ref[a, :, lanes], NT)
        signal = signal + jnp.where(row == 0, top_signal[q : q + 1], 0.0)
        signal = signal + jnp.where(row == SIDE - 1, bottom_signal[q : q + 1], 0.0)
        upstream = cot_ref[:, q * LANES : (q + 1) * LANES].astype(F32)
        return slope_times(signal, upstream).astype(BF16).astype(F32)

    end = PAIRS - 1
    g_left = side_grad(0, lefts, slice(0, LANES))
    g_right = side_grad(end, rights, slice(LANES, 2 * LANES))
    pair = iota((PAIRS, LANES), 0)
    ends = jnp.logical_or(pair == 0, pair == end)

    def line_grad(first_row, halo_signal):
        signal = s_ref[pl.ds(first_row, PAIRS, stride=SIDE), :] + added + halo_signal
        upstream = cot_lines[0:PAIRS, :] if first_row == 0 else cot_lines[PAIRS:, :]
        g = jnp.where(ends, 0.0, slope_times(signal, upstream)).astype(BF16).astype(F32)
        r = slice(first_row, first_row + 1)
        return g, jnp.where(pair == 0, g_left[r], jnp.where(pair == end, g_right[r], g))

    inner_top, all_top = line_grad(0, top_signal)
    inner_bottom, all_bottom = line_grad(SIDE - 1, bottom_signal)
    g_lines[0:PAIRS, :] = all_top
    g_lines[PAIRS:, :] = all_bottom
    g_sides[0:SIDE, :] = g_left.astype(BF16)
    g_sides[SIDE:, :] = g_right.astype(BF16)
    border = jnp.concatenate([inner_top, inner_bottom, g_left, g_right], axis=0)
    bias = jnp.sum(bias_ref[...], axis=0, keepdims=True) + jnp.sum(border, axis=0, keepdims=True)
    border = border.astype(BF16)
    kept = [windows(lines[i]) for i in range(4)]
    none = jnp.zeros((SIDE, LANES), F32)
    wide_row = iota((SIDE, 2 * LANES), 0)

    def side_window(a, p, q, columns):
        parts = [p[(q + i) * SIDE : (q + i + 1) * SIDE, :].astype(F32) for i in range(2)]
        window = jnp.concatenate(parts, axis=1) + columns
        if a == 0:
            window = window + jnp.where(wide_row == 0, top[q : q + 1], 0.0)
        if a == 2:
            window = window + jnp.where(wide_row == SIDE - 1, bottom[q : q + 1], 0.0)
        return window

    terms = []
    over = (top, kept[0], kept[1])
    under = (kept[2], kept[3], bottom)
    for a, p in enumerate((p0, p1, p2)):
        window = jnp.concatenate(
            [
                over[a],
                under[a],
                side_window(a, p, 0, jnp.concatenate([lefts[a], none], axis=1)),
                side_window(a, p, end, jnp.concatenate([none, rights[a]], axis=1)),
            ],
            axis=0,
        ).astype(BF16)
        t = terms_ref[a] + dot(border, window, TN)
        terms += [t[:, :LANES], t[:, LANES:]]
    def tap(m, high):
        a, b = m // 3, m % 3
        result = 0.0
        for e in (0, 1):
            w = e + b
            part = terms[2 * a + w // 2][e * CHANNELS : (e + 1) * CHANNELS]
            result = result + (part if (w % 2 == 1) == high else turn(part))
        return result

    total = bias + turn(bias)
    coarse = total.astype(BF16).astype(F32)
    fine = total - coarse
    for t in range(5):
        if t < 4:
            high = tap(2 * t + 1, True)
        else:
            high = jnp.where(row == 0, coarse, jnp.where(row == 1, fine, 0.0))
        msg[t * SIDE : (t + 1) * SIDE, :] = halves(tap(2 * t, False), high)
    core = lax.axis_index("region") & 1
    keep_ref[...] = msg[pl.ds(pl.multiple_of(core * WROWS, WROWS), WROWS), :].astype(BF16)
    send_ref[0:WROWS, :] = msg[pl.ds(pl.multiple_of((1 - core) * WROWS, WROWS), WROWS), :].astype(BF16)

    gc[...] = jnp.zeros(gc.shape, F32)
    gc[8 : 8 + SIDE, :] = halves(g_left, g_right)
    grads = dot(gc[8:88, :].astype(BF16), wc_ref[0])
    grads = grads + dot(gc[7:87, :].astype(BF16), wc_ref[1])
    grads = grads + dot(gc[6:86, :].astype(BF16), wc_ref[2])
    other = turn(grads)
    lefts = halves(grads, other)
    rights = halves(other, grads)
    cell_scr[...] = jnp.zeros(cell_scr.shape, F32)
    for at, src, first_row, n in (
        (0, lefts, 0, 1), (SIDE + 1, rights, 0, 1), (SIDE + 2, lefts, SIDE + 1, 1), (edge - 1, rights, SIDE + 1, 1),
        (edge, lefts, 1, SIDE), (edge + SIDE, rights, 1, SIDE),
    ):
        cell_scr[at : at + n, :] = src[first_row : first_row + n]
    placed = jnp.where(upper == low(cells.shape), 0.0, cell_scr[...]).astype(BF16)
    send_ref[WROWS:, :] = dot(hot_ref[:, many:], placed, TN).astype(BF16)


def halo_rows_kernel(g_lines, wb_ref, own_ref, gt, gb, own_scr):
    all_top, all_bottom = g_lines[0:PAIRS, :], g_lines[PAIRS:, :]
    for scr, line in ((gt, all_top), (gb, all_bottom)):
        turned = turn(line)
        scr[...] = jnp.zeros(scr.shape, F32)
        scr[1 : PAIRS + 1, :] = jnp.where(low(line.shape), turned, 0.0)
        scr[0:PAIRS, :] += jnp.where(low(line.shape), 0.0, turned)
    lines = []
    for src, tap_row in ((gt, 2), (gb, 0)):
        window = jnp.concatenate([src[0:PAIRS, :], src[1 : PAIRS + 1, :]], axis=1).astype(BF16)
        lines.append(dot(window, wb_ref[tap_row]))
    own_scr[pl.ds(0, PAIRS, stride=2), :] = halves(lines[0], turn(lines[1]))
    own_scr[pl.ds(1, PAIRS, stride=2), :] = halves(turn(lines[0]), lines[1])
    own_ref[...] = own_scr[...].astype(BF16)


def grad_copies_kernel(g_ref, g_lines, g_sides, p0, p1, p2):
    row = iota((SIDE, LANES), 0)
    left = g_sides[0:SIDE, :].astype(F32)
    right = g_sides[SIDE:, :].astype(F32)

    def load(q):
        g = g_ref[block(q), :].astype(F32)
        g = jnp.where(row == 0, g_lines[pl.ds(q, 1), :], g)
        g = jnp.where(row == SIDE - 1, g_lines[pl.ds(PAIRS + q, 1), :], g)
        return jnp.where(q == 0, left, jnp.where(q == PAIRS - 1, right, g))

    shifted_copies(load, p0, p1, p2)


def inner_kernel(p0, p1, p2, wb_ref, out_ref):
    out_ref[...] = product(p0, p1, p2, wb_ref, ((1,), (0,)))


def added_weights(parts):
    terms = [part[0:WROWS, :].astype(F32) for part in parts]
    while len(terms) > 1:
        terms = [terms[i] + terms[i + 1] for i in range(0, len(terms), 2)]
    tail = terms[0][WROWS - SIDE :]
    return terms[0], tail + pltpu.roll(tail, SIDE - 1, 0)


def bias_lanes(shape):
    return jnp.logical_and(jnp.logical_not(low(shape)), (lax.axis_index("region") & 1) == 1)


def put_weights(parts, out):
    total, whole = added_weights(parts)
    out[0 : WROWS - SIDE, :] = total[: WROWS - SIDE].astype(BF16)
    row = iota(whole.shape, 0)
    coarse = whole.astype(BF16).astype(F32)
    fine = pltpu.roll(whole - coarse, 1, 0)
    out[WROWS - SIDE : WROWS, :] = jnp.where(
        bias_lanes(whole.shape),
        jnp.where(row == 0, coarse, jnp.where(row == 1, fine, 0.0)),
        total[WROWS - SIDE :],
    ).astype(BF16)


def first_join_kernel(mine, other, *rest):
    extra, out = rest[:-1], rest[-1]
    put_weights((mine, other), out)
    if extra:
        out[WROWS:, :] = extra[0][...]


def join_kernel(*refs):
    parts, out = by_distance(refs[:-1], FAR_ORDER), refs[-1]
    put_weights(parts, out)
    n = parts[0].shape[0] - WROWS
    for i, part in enumerate(parts):
        out[WROWS + i * n : WROWS + (i + 1) * n, :] = part[WROWS:, :]


def close_kernel(scale, *refs):
    parts, out = by_distance(refs[:-1], NEAR_ORDER), refs[-1]
    total, whole = added_weights(parts)
    out[0 : WROWS - SIDE, :] = total[: WROWS - SIDE] * scale
    out[WROWS - SIDE :, :] = jnp.where(bias_lanes(whole.shape), whole, total[WROWS - SIDE :]) * scale


def weight_kernel(mine, other, wt_ref, bias_ref):
    odd = (lax.axis_index("region") & 1) == 1
    a, b = mine[...], other[...]
    full = jnp.concatenate([jnp.where(odd, b, a), jnp.where(odd, a, b)], axis=0)
    for t in range(4):
        wt_ref[:, t * LANES : (t + 1) * LANES] = full[t * SIDE : (t + 1) * SIDE]
    wt_ref[:, 4 * LANES :] = full[4 * SIDE :, :CHANNELS]
    bias_ref[...] = turn(full[4 * SIDE : 4 * SIDE + 8])[0:1, :CHANNELS]


def last_kernel(row_a, row_b, row_c, row_d, inner, pick, *rest):
    side_refs, grad_ref = rest[:-1], rest[-1]
    n = row_a.shape[0] - WROWS
    got = 0.0
    for i, ref in enumerate(by_distance((row_a, row_b, row_c, row_d), NEAR_ORDER)):
        got = got + dot(pick[:, i * n : (i + 1) * n], ref[WROWS:, :])
    a, b, c, d = (got[i * SIDE : (i + 1) * SIDE] for i in range(4))
    rims = halves(a + turn(b), turn(c) + d)
    sides = side_refs[0][side_refs[0].shape[0] - SIDE :, :].astype(F32)
    for ref in side_refs[1:]:
        sides = sides + ref[...].astype(F32)
    row = iota((SIDE, LANES), 0)
    is_low = low((SIDE, LANES))
    for q in range(PAIRS):
        v = inner[q * SIDE : (q + 1) * SIDE, :]
        v = v + jnp.where(row == 0, rims[q : q + 1], jnp.where(row == SIDE - 1, rims[PAIRS + q : PAIRS + q + 1], 0.0))
        if q == 0:
            v = v + jnp.where(is_low, sides, 0.0)
        if q == PAIRS - 1:
            v = v + jnp.where(is_low, 0.0, sides)
        grad_ref[:, q * LANES : (q + 1) * LANES] = v.astype(BF16)


def swap(x, axis, k):
    n = lax.axis_size(axis)
    return lax.ppermute(x, axis, [(i, i ^ k) for i in range(n)])


def shift(x, axis, by):
    n = lax.axis_size(axis)
    return lax.ppermute(x, axis, [(i, (i + by) % n) for i in range(n)])


def steps_of(n):
    ks = []
    k = n // 2
    while k:
        ks.append(k)
        k //= 2
    return ks


def rounds_of(owners):
    count = owners.bit_length() - 1
    pairs = [(bit, bit + 1) for bit in range(count % 2, count, 2)][::-1]
    if count % 2:
        pairs = [tuple(b - 1 for b in p) for p in pairs]
        return [(count - 1,)] + pairs
    return pairs


def slot_bits(owners):
    bits = [bit for bits in rounds_of(owners) for bit in bits]
    return [(bit, to) for to, bit in enumerate(bits)]


def exchange(x, bits, order):
    ks = [sum(1 << bits[i] for i in range(len(bits)) if (n >> i) & 1) for n in range(1, 1 << len(bits))]
    return [swap(x, "patch", ks[i]) for i in order if i < len(ks)]


def by_distance(parts, order):
    places = [i for i in order if i < len(parts) - 1]
    return [parts[0]] + [parts[1 + places.index(i)] for i in range(len(places))]


def body(fine_input, fine_weight, fine_bias, cotangent, halo_index):
    owners = lax.axis_size("patch")
    regions = lax.axis_size("region")
    rounds = rounds_of(owners)
    blocks = 1 if regions == 2 else 2
    x = fine_input.reshape(SIDE, SIDE * CHANNELS)
    cot = cotangent.reshape(SIDE, SIDE * CHANNELS)
    pair = ((ROWS + SIDE, LANES), BF16)

    rows = call(
        rim_kernel, [((SIDE, LANES), BF16)], x[:16], x[SIDE - 16 :], scratch=[pltpu.VMEM((SIDE, LANES), F32)]
    )[0]
    count = 272
    both = ((ROWS, LANES), F32)
    work = dict(flops=2 * ROWS * 768 * 128, moved=3 * 2**20)

    others = exchange(rows, rounds[0], FAR_ORDER)
    *copies, lines, cols = call(
        copies_kernel, [pair] * 3 + [((4, 40, LANES), F32), ((SIDE, LANES), BF16)], x, moved=2 * 2**20
    )
    if regions == 2:
        cols = swap(cols, "region", 1)
    else:
        cols = jnp.concatenate([shift(cols, "region", 1), shift(cols, "region", -1)], axis=0)
    forward, backward, columns = call(
        weights_kernel,
        [((3, LANES, 2 * LANES), BF16), ((3, 2 * LANES, LANES), BF16), ((3, LANES, LANES), BF16)],
        fine_weight.T,
    )
    signal = call(
        signal_kernel, [both], *copies, forward, **work,
    )[0]
    offset = fine_bias.reshape(1, CHANNELS)
    others, signal, index, offset = lax.optimization_barrier((others, signal, halo_index, offset))
    for bits in rounds[1:]:
        size = ((len(others) + 1) * rows.shape[0], LANES)
        rows = call(rows_kernel, [(size, BF16)], rows, *others)[0]
        others = exchange(rows, bits, NEAR_ORDER if bits == rounds[-1] else FAR_ORDER)
    hot, half_mask = call(
        functools.partial(plan_kernel, owners, regions, blocks),
        [((count, (owners + blocks) * SIDE), BF16), ((count, LANES), F32)],
        index, scratch=[pltpu.VMEM((8, 384), F32)],
    )
    inside = call(
        inside_kernel,
        [((ROWS, LANES), BF16), ((3, LANES, 2 * LANES), F32), ((8, LANES), F32), ((SIDE, LANES), F32)],
        signal, offset, cot, *copies, **work,
    )
    others, hot, half_mask, inside = lax.optimization_barrier((others, hot, half_mask, inside))
    grad, *inside = inside

    line = pltpu.VMEM((40, LANES), F32)
    g_lines, g_sides, message, sent = call(
        middle_kernel,
        [
            ((SIDE, LANES), F32), ((2 * SIDE, LANES), BF16),
            ((WROWS, LANES), BF16), ((WROWS + blocks * SIDE, LANES), BF16),
        ],
        signal, offset, cot, *copies, lines, *inside, rows, *others, cols, hot, half_mask, forward, columns,
        scratch=[
            pltpu.VMEM((count, LANES), F32), pltpu.VMEM((96, LANES), F32), pltpu.VMEM((2 * WROWS, LANES), F32),
        ],
        moved=2**20,
    )

    if regions > 2:
        upper, lower = sent[WROWS + SIDE :], sent[WROWS : WROWS + SIDE]
        sides = [shift(upper, "region", 1), shift(lower, "region", -1)]
        sent = sent[:WROWS]
    other = swap(sent, "region", 1)
    own_rows = call(
        halo_rows_kernel, [((SIDE, LANES), BF16)], g_lines, backward,
        scratch=[line, line, pltpu.VMEM((SIDE, LANES), F32)],
    )[0]
    other, own_rows = lax.optimization_barrier((other, own_rows))
    if regions == 2:
        sides = [other]
    far = [k for k in steps_of(regions) if k > 1]
    for k in [1] + far:
        extra = () if k != ([1] + far)[-1] else (own_rows,)
        size = (WROWS + SIDE * len(extra), LANES)
        got = other if k == 1 else swap(message, "region", k)
        message = call(first_join_kernel, [(size, BF16)], message, got, *extra)[0]
    beside = [grad, g_lines, g_sides]
    for bits in rounds[:-1]:
        message, beside, index = lax.optimization_barrier((message, beside, index))
        others = exchange(message, bits, FAR_ORDER)
        if bits == rounds[-2]:
            pick = call(functools.partial(pick_kernel, owners), [((4 * SIDE, owners * SIDE), BF16)], index)[0]
            beside = call(grad_copies_kernel, [pair] * 3, *beside, moved=2 * 2**20)
            others, beside, pick = lax.optimization_barrier((others, beside, pick))
        size = (WROWS + (len(others) + 1) * (message.shape[0] - WROWS), LANES)
        message = call(join_kernel, [(size, BF16)], message, *others)[0]
    message, beside = lax.optimization_barrier((message, beside))
    others = exchange(message, rounds[-1], NEAR_ORDER)
    beside = call(inner_kernel, [both], *beside, backward, **work)[0]
    others, beside = lax.optimization_barrier((others, beside))
    scale = 1.0 / math.sqrt(regions * owners * SIDE * SIDE)
    part = call(functools.partial(close_kernel, scale), [((WROWS, LANES), F32)], message, *others)[0]
    other_part = swap(part, "region", 1)
    input_grad = call(
        last_kernel, [((SIDE, SIDE * CHANNELS), BF16)], message, *others, beside, pick, *sides, moved=2 * 2**20
    )[0]
    weight_grad, bias_grad = call(
        weight_kernel, [((CHANNELS, 9 * CHANNELS), F32), ((1, CHANNELS), F32)], part, other_part
    )
    return input_grad.reshape(1, SIDE, SIDE * CHANNELS), weight_grad.T, bias_grad.reshape(CHANNELS)


def solution(mesh):
    placed = (
        P(("region", "patch"), None, None),
        P(),
        P(),
        P(("region", "patch"), None, None),
        P("region", None),
    )
    return jax.shard_map(
        body,
        mesh=mesh,
        in_specs=placed,
        out_specs=(P(("region", "patch"), None, None), P(), P()),
        check_vma=False,
    )
```
